256 devices in a mesh: dp: 8 (over y, z_lo), frame: 32 (over z_hi, x, core).
Axes of the slice: x: 4, y: 4, z: 8 (z_hi: 4, z_lo: 2; z = z_hi * 2 + z_lo), core: 2. Of those that a mesh axis runs over, the one named last changes fastest.
Arguments:
- recorded_exposures: float32 [16, 128, 128, 128], P('dp', 'frame'), may hold values from -6 to 6
- aberration_phase_screens: float32 [44, 16384], replicated, may hold values from -0.875 to 0.875
- entry_convolution_kernel: float32 [256, 256], replicated, may hold values from -0.375 to 0.375
- residual_inner_map: float32 [256, 256], replicated, may hold values from -0.375 to 0.375
- residual_outer_map: float32 [256, 256], replicated, may hold values from -0.375 to 0.375
- output_projection_kernel: float32 [256, 44], replicated, may hold values from -0.375 to 0.375
Outputs:
- phase_weights_derivative: float32 [16, 128, 44], P('dp', 'frame')
- grad_embed: float32 [256, 256], replicated
- grad_first: float32 [256, 256], replicated
- grad_second: float32 [256, 256], replicated
- grad_head: float32 [256, 44], replicated
- patch_loss: float32 [16], P('dp')
The draws below stay inside these ranges and needn't reach their ends.
All inputs are finite; a program needn't handle non-finite values.
Results may differ from the reference program's by a relative error of at most 0.0003.
Values sent between devices are 32-bit elements; how exact they have to be, the bound alone decides.
A program may use at most 64 MiB of HBM per device.

```python
import jax
import jax.numpy as jnp
from jax import lax

REGION_PIXELS = 128
MODES = 44
CH = 256
REGION_TOTAL = 16
SHOTS_PER_SET = 128


def block_scale(rng, extent, split, least, largest):
    def one(axis_at, parts):
        heights = jax.random.uniform(jax.random.fold_in(jax.random.fold_in(rng, 6), axis_at), (parts,), jnp.float32, least / len(split), largest / len(split))
        return jnp.repeat(jnp.exp(heights), extent[axis_at] // parts).reshape((-1,) + (1,) * (len(extent) - axis_at - 1))

    gain = one(*split[0])
    for cut in split[1:]:
        gain = gain * one(*cut)
    return gain


def noise(key, dims, scale, bound, cuts=(), dtype=jnp.bfloat16):
    gain = block_scale(key, dims, cuts, -0.22, 0.18) if cuts else 1.0
    entries = jax.random.normal(key, dims, jnp.float32) * scale * gain
    return jnp.minimum(jnp.maximum(entries, -bound), bound).astype(dtype)


def setup_inputs(seed: int = 0) -> dict:
    keys = jax.random.split(jax.random.key(seed), 7)
    return {
        "recorded_exposures": noise(keys[0], (REGION_TOTAL, SHOTS_PER_SET, REGION_PIXELS, REGION_PIXELS), 1.0, 6.0, ((0, 8), (1, 32)), jnp.float32),
        "aberration_phase_screens": noise(keys[1], (MODES, REGION_PIXELS * REGION_PIXELS), MODES ** -0.5, 0.875, (), jnp.float32),
        "entry_convolution_kernel": noise(keys[2], (256, CH), 256 ** -0.5, 0.375, (), jnp.float32),
        "residual_inner_map": noise(keys[3], (CH, CH), CH ** -0.5, 0.375, (), jnp.float32),
        "residual_outer_map": noise(keys[4], (CH, CH), CH ** -0.5, 0.375, (), jnp.float32),
        "output_projection_kernel": noise(keys[5], (CH, MODES), CH ** -0.5, 0.375, (), jnp.float32),
    }


entry_block_length = 16
regularizer_relative = 0.001

def silu_act(value):
    return value / (1.0 + jnp.exp(-value))

def summarizer_apply(learned_model_state, recorded_exposures):
    entry_convolution_kernel, residual_inner_map, residual_outer_map, output_projection_kernel = learned_model_state
    highest_precision = lax.Precision.HIGHEST
    region_number, exposure_number, region_length = (recorded_exposures.shape[0], recorded_exposures.shape[1], recorded_exposures.shape[2])
    lattice_length = region_length // entry_block_length
    entry_block_pieces = recorded_exposures.reshape(region_number, exposure_number, lattice_length, entry_block_length, lattice_length, entry_block_length)
    entry_block_pieces = entry_block_pieces.transpose(0, 1, 2, 4, 3, 5).reshape(region_number, exposure_number, lattice_length * lattice_length, entry_block_length * entry_block_length)
    hidden = silu_act(jnp.einsum('pftk,kc->pftc', entry_block_pieces, entry_convolution_kernel, precision=highest_precision))
    inner = silu_act(jnp.einsum('pftc,cd->pftd', hidden, residual_inner_map, precision=highest_precision))
    hidden = hidden + jnp.einsum('pftd,dc->pftc', inner, residual_outer_map, precision=highest_precision)
    pooled_features = lax.optimization_barrier(jnp.mean(hidden, axis=2))
    return jnp.einsum('odg,ge->ode', pooled_features, output_projection_kernel, precision=highest_precision)

def pupil_mask(region_length):
    coords = jnp.arange(region_length) - region_length // 2
    radius = coords[:, None] * coords[:, None] + coords[None, :] * coords[None, :]
    return jnp.where(radius <= region_length // 4 * (region_length // 4), 1.0, 0.0).astype(jnp.float32)

def reference(recorded_exposures, aberration_phase_screens, entry_convolution_kernel, residual_inner_map, residual_outer_map, output_projection_kernel):
    kernel_collection = (entry_convolution_kernel, residual_inner_map, residual_outer_map, output_projection_kernel)
    aberration_amplitudes, summarizer_adjoint = jax.vjp(lambda learned_model_state: summarizer_apply(learned_model_state, recorded_exposures), kernel_collection)
    aperture = pupil_mask(REGION_PIXELS)
    spot_scale = 1.0 / (REGION_PIXELS * REGION_PIXELS * jnp.sum(aperture))
    regularizer_strength = regularizer_relative * SHOTS_PER_SET

    def region_cost_scalar(pair):
        aberration_number, frames = pair
        wavefront_angle = jnp.dot(aberration_number, aberration_phase_screens, precision=lax.Precision.HIGHEST).reshape(SHOTS_PER_SET, REGION_PIXELS, REGION_PIXELS)
        field = aperture * jnp.exp(1j * wavefront_angle)
        focal = jnp.fft.fft2(field)
        spot = (focal.real * focal.real + focal.imag * focal.imag) * spot_scale
        otf = jnp.fft.fft2(spot)
        spec = jnp.fft.fft2(frames) / REGION_PIXELS
        num = lax.optimization_barrier(jnp.sum(spec * jnp.conj(otf), axis=0))
        den = lax.optimization_barrier(jnp.sum(otf.real * otf.real + otf.imag * otf.imag, axis=0)) + regularizer_strength
        energy = lax.optimization_barrier(jnp.sum(spec.real * spec.real + spec.imag * spec.imag, axis=0))
        return jnp.sum(energy - (num.real * num.real + num.imag * num.imag) / den) / (REGION_PIXELS * REGION_PIXELS)

    def total(aberration_number):
        region_misfits = lax.map(region_cost_scalar, (aberration_number, recorded_exposures))
        return (jnp.sum(region_misfits), region_misfits)
    total_value, total_back, region_misfits = jax.vjp(total, aberration_amplitudes, has_aux=True)
    phase_weights_derivative, = total_back(jnp.ones_like(total_value))
    derivative_bundle = summarizer_adjoint(phase_weights_derivative)[0]
    return (phase_weights_derivative, derivative_bundle[0], derivative_bundle[1], derivative_bundle[2], derivative_bundle[3], region_misfits / SHOTS_PER_SET)
```

```python
import functools
import math

import jax
import jax.numpy as jnp
from jax import lax
from jax.experimental import pallas as pl
from jax.experimental.pallas import tpu as pltpu
from jax.sharding import PartitionSpec as P

entry_block_length = 16
regularizer_relative = 0.001
MESH = pl.DeviceIdType.MESH


def silu_act(value):
    return value / (1.0 + jnp.exp(-value))


def summarizer_apply(learned_model_state, recorded_exposures):
    entry_convolution_kernel, residual_inner_map, residual_outer_map, output_projection_kernel = (
        learned_model_state
    )
    highest_precision = lax.Precision.HIGHEST
    region_number, exposure_number, region_length = (
        recorded_exposures.shape[0],
        recorded_exposures.shape[1],
        recorded_exposures.shape[2],
    )
    lattice_length = region_length // entry_block_length
    entry_block_pieces = recorded_exposures.reshape(
        region_number,
        exposure_number,
        lattice_length,
        entry_block_length,
        lattice_length,
        entry_block_length,
    )
    entry_block_pieces = entry_block_pieces.transpose(0, 1, 2, 4, 3, 5).reshape(
        region_number,
        exposure_number,
        lattice_length * lattice_length,
        entry_block_length * entry_block_length,
    )
    hidden = silu_act(
        jnp.einsum(
            "pftk,kc->pftc",
            entry_block_pieces,
            entry_convolution_kernel,
            precision=highest_precision,
        )
    )
    inner = silu_act(
        jnp.einsum("pftc,cd->pftd", hidden, residual_inner_map, precision=highest_precision)
    )
    hidden = hidden + jnp.einsum(
        "pftd,dc->pftc", inner, residual_outer_map, precision=highest_precision
    )
    pooled_features = jnp.mean(hidden, axis=2)
    return jnp.einsum(
        "odg,ge->ode", pooled_features, output_projection_kernel, precision=highest_precision
    )


def pupil_mask(region_length):
    coords = jnp.arange(region_length) - region_length // 2
    radius = coords[:, None] * coords[:, None] + coords[None, :] * coords[None, :]
    return jnp.where(radius <= region_length // 4 * (region_length // 4), 1.0, 0.0).astype(
        jnp.float32
    )


def tables(region_length):
    index = jnp.arange(region_length, dtype=jnp.int32)
    product = index[:, None] * index[None, :] % region_length
    angle = 2.0 * math.pi / region_length * product.astype(jnp.float32)
    return (jnp.cos(angle), jnp.sin(angle))


def left_mul(matrix, value):
    return jnp.einsum("ij,...jk->...ik", matrix, value, precision=lax.Precision.HIGHEST)


def right_mul(value, matrix):
    return jnp.einsum("...ij,jk->...ik", value, matrix, precision=lax.Precision.HIGHEST)


def fourier_transform(
    real_part, imag_part, harmonic_even_matrix, harmonic_odd_matrix, col_cos, col_sin
):
    if imag_part is None:
        half_r = left_mul(harmonic_even_matrix, real_part)
        half_i = -left_mul(harmonic_odd_matrix, real_part)
    else:
        half_r = left_mul(harmonic_even_matrix, real_part) + left_mul(
            harmonic_odd_matrix, imag_part
        )
        half_i = left_mul(harmonic_even_matrix, imag_part) - left_mul(
            harmonic_odd_matrix, real_part
        )
    out_r = right_mul(half_r, col_cos) + right_mul(half_i, col_sin)
    out_i = right_mul(half_i, col_cos) - right_mul(half_r, col_sin)
    return (out_r, out_i)


def spectral_kernel(group, regularizer_strength, part_ref, ratio_ref, inbox, gathered, sems):
    me = lax.axis_index("frame")
    rows = gathered.shape[1]

    def peer(step):
        return lax.rem(me + step, group)

    def greet(step, carry):
        pl.semaphore_signal(
            pltpu.get_barrier_semaphore(),
            inc=1,
            device_id={"frame": peer(step)},
            device_id_type=MESH,
        )
        return carry

    lax.fori_loop(1, group, greet, 0)
    pl.semaphore_wait(pltpu.get_barrier_semaphore(), group - 1)

    def scatter_copy(step):
        return pltpu.make_async_remote_copy(
            src_ref=part_ref.at[peer(step)],
            dst_ref=inbox.at[step],
            send_sem=sems.at[0, step],
            recv_sem=sems.at[1, step],
            device_id={"frame": peer(step)},
            device_id_type=MESH,
        )

    def gather_copy(step):
        return pltpu.make_async_remote_copy(
            src_ref=gathered.at[me],
            dst_ref=gathered.at[me],
            send_sem=sems.at[2, step],
            recv_sem=sems.at[3, step],
            device_id={"frame": peer(step)},
            device_id_type=MESH,
        )

    def start(copy):
        def step_fn(step, carry):
            copy(step).start()
            return carry

        lax.fori_loop(1, group, step_fn, 0)

    start(scatter_copy)

    def add(step, total):
        scatter_copy(step).wait_recv()
        return total + inbox[step]

    total = lax.fori_loop(1, group, add, part_ref[me])
    num = total[:rows]
    den = total[rows:] + regularizer_strength
    gathered[me] = num / jnp.concatenate([den, den], axis=0)
    start(gather_copy)

    def finish(step, carry):
        scatter_copy(step).wait_send()
        gather_copy(step).wait()
        return carry

    lax.fori_loop(1, group, finish, 0)
    ratio_ref[...] = gathered[...]


def spectral_exchange(part, regularizer_strength):
    group, rows, lanes = part.shape
    ratio_rows = rows * 2 // 3
    return pl.pallas_call(
        functools.partial(spectral_kernel, group, regularizer_strength),
        out_shape=jax.ShapeDtypeStruct((group, ratio_rows, lanes), jnp.float32),
        in_specs=[pl.BlockSpec(memory_space=pltpu.VMEM)],
        out_specs=pl.BlockSpec(memory_space=pltpu.VMEM),
        scratch_shapes=[
            pltpu.VMEM((group, rows, lanes), jnp.float32),
            pltpu.VMEM((group, ratio_rows, lanes), jnp.float32),
            pltpu.SemaphoreType.DMA((4, group)),
        ],
        compiler_params=pltpu.CompilerParams(
            collective_id=0, has_side_effects=True, vmem_limit_bytes=32 << 20
        ),
    )(part)


part_rows = (256, 256, 256, 128)
zone_rows = 64


def gradient_kernel(
    embed_ref, first_ref, second_ref, head_ref, out_ref,
    core_in0, core_in1, core_in2, core_in3,
    sum0, sum1, sum2, sum3,
    x_in0, x_in1, x_in2, x_in3,
    xsum0, xsum1, xsum2, xsum3,
    y_in0, y_in1, y_in2, y_in3,
    zone, z_in, z_all, y_all, x_all, core_all, sems,
):
    parts = (embed_ref, first_ref, second_ref, head_ref)
    core_in = (core_in0, core_in1, core_in2, core_in3)
    sums = (sum0, sum1, sum2, sum3)
    x_in = (x_in0, x_in1, x_in2, x_in3)
    x_sums = (xsum0, xsum1, xsum2, xsum3)
    y_in = (y_in0, y_in1, y_in2, y_in3)
    dp, frame = lax.axis_index("dp"), lax.axis_index("frame")
    core, x, z_hi = lax.rem(frame, 2), lax.rem(frame // 2, 4), frame // 8
    y, z_lo = dp // 2, lax.rem(dp, 2)
    z = z_hi * 2 + z_lo

    def device(c, px, py, pz):
        return {"dp": py * 2 + lax.rem(pz, 2), "frame": (pz // 2) * 8 + px * 2 + c}

    core_peer = device(1 - core, x, y, z)

    def x_peer(step):
        return lax.rem(x + step, 4)

    def y_peer(step):
        return lax.rem(y + step, 4)

    def z_peer(step):
        return lax.rem(z + step, 8)

    peers = [core_peer]
    peers += [device(core, x_peer(s), y, z) for s in range(1, 4)]
    peers += [device(core, x, y_peer(s), z) for s in range(1, 4)]
    peers += [device(core, x, y, z_peer(s)) for s in range(1, 8)]
    barrier = pltpu.get_barrier_semaphore()
    for target in peers:
        pl.semaphore_signal(barrier, inc=1, device_id=target, device_id_type=MESH)
    pl.semaphore_wait(barrier, len(peers))

    used = [0]

    def copy(src, dst, target):
        slot = used[0]
        used[0] += 1
        one = pltpu.make_async_remote_copy(
            src_ref=src,
            dst_ref=dst,
            send_sem=sems.at[0, slot],
            recv_sem=sems.at[1, slot],
            device_id=target,
            device_id_type=MESH,
        )
        one.start()
        return one

    sent = []
    lanes = parts[0].shape[1] // 2
    mine = pl.ds(pl.multiple_of(core * lanes, lanes), lanes)
    other = pl.ds(pl.multiple_of((1 - core) * lanes, lanes), lanes)
    core_copies = [copy(parts[p].at[:, other], core_in[p], core_peer) for p in range(4)]
    sent += core_copies

    x_copies = []
    for p in range(4):
        core_copies[p].wait_recv()
        sums[p][...] = parts[p][:, mine] + core_in[p][...]
        size = part_rows[p] // 4
        x_copies.append([
            copy(
                sums[p].at[pl.ds(pl.multiple_of(x_peer(s) * size, size), size)],
                x_in[p].at[s - 1],
                device(core, x_peer(s), y, z),
            )
            for s in range(1, 4)
        ])
        sent += x_copies[p]

    y_copies = []
    for p in range(4):
        for one in x_copies[p]:
            one.wait_recv()
        size = part_rows[p] // 4
        own = sums[p][pl.ds(pl.multiple_of(x * size, size), size)]
        x_sums[p][...] = own + x_in[p][0] + x_in[p][1] + x_in[p][2]
        size = part_rows[p] // 16
        y_copies.append([
            copy(
                x_sums[p].at[pl.ds(pl.multiple_of(y_peer(s) * size, size), size)],
                y_in[p].at[s - 1],
                device(core, x, y_peer(s), z),
            )
            for s in range(1, 4)
        ])
        sent += y_copies[p]

    at = 0
    for p in range(4):
        for one in y_copies[p]:
            one.wait_recv()
        size = part_rows[p] // 16
        own = x_sums[p][pl.ds(pl.multiple_of(y * size, size), size)]
        total = own + y_in[p][0] + y_in[p][1] + y_in[p][2]
        for row in range(0, size, 8):
            zone[at // 8] = total[row : row + 8]
            at += 8
    zone[7] = jnp.zeros_like(zone[7])

    z_copies = [
        copy(zone.at[z_peer(s)], z_in.at[s - 1], device(core, x, y, z_peer(s))) for s in range(1, 8)
    ]
    sent += z_copies
    total = zone[z]
    for s in range(1, 8):
        z_copies[s - 1].wait_recv()
        total = total + z_in[s - 1]
    z_all[z] = total
    z_gather = [
        copy(z_all.at[z], z_all.at[z], device(core, x, y, z_peer(s))) for s in range(1, 8)
    ]
    sent += z_gather
    for one in z_gather:
        one.wait_recv()

    y_all[y] = z_all[...]
    y_gather = [
        copy(y_all.at[y], y_all.at[y], device(core, x, y_peer(s), z)) for s in range(1, 4)
    ]
    sent += y_gather
    for one in y_gather:
        one.wait_recv()

    x_all[x] = y_all[...]
    x_gather = [
        copy(x_all.at[x], x_all.at[x], device(core, x_peer(s), y, z)) for s in range(1, 4)
    ]
    sent += x_gather
    core_gather = [copy(x_all.at[x], core_all.at[x], core_peer)]
    for s in range(1, 4):
        x_gather[s - 1].wait_recv()
        came_from = lax.rem(x + 4 - s, 4)
        core_gather.append(copy(x_all.at[came_from], core_all.at[came_from], core_peer))
    sent += core_gather
    for one in core_gather:
        one.wait_recv()

    starts = (0, 2, 4, 6)
    for p in range(4):
        quarter, size = part_rows[p] // 4, part_rows[p] // 16
        base = p * 256
        for px in range(4):
            for py in range(4):
                for row in range(0, size, 8):
                    at = base + px * quarter + py * size + row
                    tile = starts[p] + row // 8
                    out_ref[at : at + 8, mine] = x_all[px, py, tile]
                    out_ref[at : at + 8, other] = core_all[px, py, tile]
    for one in sent:
        one.wait_send()


def gradient_exchange(embed, first, second, head):
    width = embed.shape[1]
    half = width // 2
    f32 = jnp.float32
    scratch = [pltpu.VMEM((r, half), f32) for r in part_rows]
    scratch += [pltpu.VMEM((r, half), f32) for r in part_rows]
    scratch += [pltpu.VMEM((3, r // 4, half), f32) for r in part_rows]
    scratch += [pltpu.VMEM((r // 4, half), f32) for r in part_rows]
    scratch += [pltpu.VMEM((3, r // 16, half), f32) for r in part_rows]
    scratch += [
        pltpu.VMEM((8, 8, half), f32),
        pltpu.VMEM((7, 8, half), f32),
        pltpu.VMEM((8, 8, half), f32),
        pltpu.VMEM((4, 8, 8, half), f32),
        pltpu.VMEM((4, 4, 8, 8, half), f32),
        pltpu.VMEM((4, 4, 8, 8, half), f32),
        pltpu.SemaphoreType.DMA((2, 64)),
    ]
    return pl.pallas_call(
        gradient_kernel,
        out_shape=jax.ShapeDtypeStruct((sum(part_rows), width), f32),
        in_specs=[pl.BlockSpec(memory_space=pltpu.VMEM)] * 4,
        out_specs=pl.BlockSpec(memory_space=pltpu.VMEM),
        scratch_shapes=scratch,
        compiler_params=pltpu.CompilerParams(
            collective_id=1, has_side_effects=True, vmem_limit_bytes=32 << 20
        ),
    )(embed, first, second, head)


def local(
    recorded_exposures,
    aberration_phase_screens,
    entry_convolution_kernel,
    residual_inner_map,
    residual_outer_map,
    output_projection_kernel,
):
    region_number, exposure_number, region_length = (
        recorded_exposures.shape[0],
        recorded_exposures.shape[1],
        recorded_exposures.shape[2],
    )
    frames_total = exposure_number * lax.axis_size("frame")
    regularizer_strength = regularizer_relative * frames_total
    kernel_collection = (
        entry_convolution_kernel,
        residual_inner_map,
        residual_outer_map,
        output_projection_kernel,
    )
    aberration_amplitudes, summarizer_adjoint = jax.vjp(
        lambda learned_model_state: summarizer_apply(learned_model_state, recorded_exposures),
        kernel_collection,
    )
    harmonic_even_matrix, harmonic_odd_matrix = tables(region_length)
    aperture = pupil_mask(region_length)
    spot_scale = 1.0 / (region_length * region_length * jnp.sum(aperture))
    observed_real, observed_imaginary = fourier_transform(
        recorded_exposures,
        None,
        harmonic_even_matrix,
        harmonic_odd_matrix,
        harmonic_even_matrix,
        harmonic_odd_matrix,
    )
    observed_real = observed_real / region_length
    observed_imaginary = observed_imaginary / region_length

    def spectra(aberration_number):
        wavefront_angle = jnp.einsum(
            "pfm,mk->pfk",
            aberration_number,
            aberration_phase_screens,
            precision=lax.Precision.HIGHEST,
        )
        wavefront_angle = wavefront_angle.reshape(
            region_number, exposure_number, region_length, region_length
        )
        focal_r, focal_i = fourier_transform(
            aperture * jnp.cos(wavefront_angle),
            aperture * jnp.sin(wavefront_angle),
            harmonic_even_matrix,
            harmonic_odd_matrix,
            harmonic_even_matrix,
            harmonic_odd_matrix,
        )
        spot = (focal_r * focal_r + focal_i * focal_i) * spot_scale
        otf_r, otf_i = fourier_transform(
            spot,
            None,
            harmonic_even_matrix,
            harmonic_odd_matrix,
            harmonic_even_matrix,
            harmonic_odd_matrix,
        )
        num_r = jnp.sum(observed_real * otf_r + observed_imaginary * otf_i, axis=1)
        num_i = jnp.sum(observed_imaginary * otf_r - observed_real * otf_i, axis=1)
        den = jnp.sum(otf_r * otf_r + otf_i * otf_i, axis=1)
        return (num_r, num_i, den)

    local_terms, optics_back = jax.vjp(spectra, aberration_amplitudes)

    part = jnp.stack(local_terms).reshape(3, region_number, 32, region_length // 32, region_length)
    part = part.transpose(2, 0, 1, 3, 4).reshape(32, -1, region_length)
    ratio = spectral_exchange(part, regularizer_strength)
    ratio = ratio.reshape(32, 2, region_number, region_length // 32, region_length)
    ratio = ratio.transpose(1, 2, 0, 3, 4).reshape(2, region_number, region_length, region_length)
    ratio_r, ratio_i = ratio[0], ratio[1]
    scale = 1.0 / (region_length * region_length)
    cotangents = (
        -2.0 * scale * ratio_r,
        -2.0 * scale * ratio_i,
        scale * (ratio_r * ratio_r + ratio_i * ratio_i),
    )
    explained = jnp.sum(local_terms[0] * ratio_r + local_terms[1] * ratio_i, axis=(1, 2)) * scale
    energy = jnp.sum(recorded_exposures * recorded_exposures, axis=(1, 2, 3))
    patch_part = energy * scale - explained
    (phase_weights_derivative,) = optics_back(cotangents)
    local_grads = summarizer_adjoint(phase_weights_derivative)[0]
    dp = lax.axis_index("dp")
    patches = region_number * lax.axis_size("dp")
    losses = lax.dynamic_update_slice(
        jnp.zeros((patches,), jnp.float32), patch_part, (dp * region_number,)
    )
    modes = local_grads[3].shape[1]
    head = jnp.pad(local_grads[3], ((0, 0), (0, 128 - modes)))
    head = head.at[0, 64 : 64 + patches].set(losses)
    head = jnp.concatenate([head[:128], head[128:]], axis=1)
    total = gradient_exchange(local_grads[0], local_grads[1], local_grads[2], head)
    losses = lax.dynamic_slice(total[768, 64 : 64 + patches], (dp * region_number,), (region_number,))
    head = jnp.concatenate([total[768:, :modes], total[768:, 128 : 128 + modes]], axis=0)
    return (
        phase_weights_derivative,
        total[:256],
        total[256:512],
        total[512:768],
        head,
        losses / frames_total,
    )


def solution(mesh):
    placed = (P("dp", "frame", None, None), P(), P(), P(), P(), P())
    return jax.shard_map(
        local,
        mesh=mesh,
        in_specs=placed,
        out_specs=(P("dp", "frame", None), P(), P(), P(), P(), P("dp")),
        check_vma=False,
    )
```

```python
import functools
import types

import jax
import jax.numpy as jnp
import numpy as np
from jax import lax
from jax.experimental import pallas as pl
from jax.experimental.pallas import tpu as pltpu
from jax.sharding import PartitionSpec as P

entry_block_length = 16
regularizer_relative = 0.001
MESH = pl.DeviceIdType.MESH
HIGH = lax.Precision.HIGH
HIGHEST = lax.Precision.HIGHEST
side = 128
half = side // 2
span = half + 1
pad_span = 72
images = 8
frames_here = 4
modes = 44
tiles_each = 64
loss_lane = 64


def dot(a, b, precision=HIGH):
    return jnp.dot(a, b, precision=precision, preferred_element_type=jnp.float32)


def dot_tn(a, b, precision=HIGH):
    return lax.dot_general(
        a, b, (((0,), (0,)), ((), ())), precision=precision, preferred_element_type=jnp.float32
    )


def dot_nt(a, b, precision=HIGH):
    return lax.dot_general(
        a, b, (((1,), (1,)), ((), ())), precision=precision, preferred_element_type=jnp.float32
    )


def transform_tables():
    index = np.arange(side)
    angle = 2.0 * np.pi / side * (index[:, None] * index[None, :] % side)
    c, s = np.cos(angle), np.sin(angle)
    both = np.block([[c, -s], [s, c]])
    lo = slice(0, half)
    half_plane = np.concatenate([both[:, lo], both[:, side : side + half]], axis=1)
    swapped = np.concatenate([half_plane, half_plane[:, half:], half_plane[:, :half]], axis=1)
    rows = slice(half // 2, half // 2 + span)
    pupil = np.zeros((2 * side, 2 * pad_span))
    pupil[:side, :span], pupil[:side, pad_span : pad_span + span] = c[:, rows], s[:, rows]
    pupil[side:, :span], pupil[side:, pad_span : pad_span + span] = -s[:, rows], c[:, rows]
    real = np.concatenate([c, -s], axis=0)
    tables = (both, both.T, pupil, pupil.T, real, real.T, half_plane, half_plane.T, swapped / side)
    return tuple(np.ascontiguousarray(t.astype(np.float32)) for t in tables)


def aperture_area():
    at = np.arange(side) - half
    return float(np.sum(at[:, None] ** 2 + at[None, :] ** 2 <= (side // 4) ** 2))


def sigmoid(value):
    return 1.0 / (1.0 + jnp.exp(-value))


def silu_act(value):
    return value / (1.0 + jnp.exp(-value))


def silu_slope(value):
    gate = sigmoid(value)
    return gate * (1.0 + value * (1.0 - gate))


def alternating(rows):
    lane = lax.broadcasted_iota(jnp.int32, (rows, side), 1)
    return jnp.where(lax.rem(lane, 2) == 0, 1.0, -1.0).astype(jnp.float32)


def corner(rows):
    row = lax.broadcasted_iota(jnp.int32, (rows, side), 0)
    lane = lax.broadcasted_iota(jnp.int32, (rows, side), 1)
    return jnp.logical_and(row == 0, lax.rem(lane, half) == 0)


def cut_tiles(img, tiles):
    group = lax.broadcasted_iota(jnp.int32, (8, side), 1) // 16

    def one(n, carry):
        for g in range(2):
            x = [img[n, pl.ds(8 * g + j, 8, stride=16), :] for j in range(8)]
            for bit in (1, 2, 4):
                low = lax.rem(group // bit, 2) == 0
                y = list(x)
                for p in range(8):
                    if p & bit == 0:
                        q = p + bit
                        y[p] = jnp.where(low, x[p], pltpu.roll(x[q], 16 * bit, 1))
                        y[q] = jnp.where(low, pltpu.roll(x[p], side - 16 * bit, 1), x[q])
                x = y
            for c in range(8):
                tiles[pl.ds(pl.multiple_of(n * 64 + c * 8, 8), 8), g * side : (g + 1) * side] = x[c]
        return carry

    lax.fori_loop(0, images, one, 0)


def tile_sum(value):
    return jnp.sum(value.reshape(images, tiles_each, value.shape[1]), axis=1)


def encode(tiles, embed, first, second, head, hid_pre, inn_pre, inner_sum, pooled):
    pre = dot(tiles[...], embed[...], HIGHEST)
    hid_pre[...] = pre
    hidden = silu_act(pre)
    pre2 = dot(hidden, first[...], HIGHEST)
    inn_pre[...] = pre2
    total = tile_sum(silu_act(pre2))
    inner_sum[...] = total
    mean = (tile_sum(hidden) + dot(total, second[...], HIGHEST)) * (1.0 / tiles_each)
    pooled[...] = mean
    return dot(mean, head[...], HIGHEST)


def pupil_field(alpha, screens, spread, field):
    for m in range(modes):
        spread[m] = jnp.broadcast_to(alpha[:, m : m + 1], (images, side))
    lane = lax.broadcasted_iota(jnp.int32, (images, side), 1) - half
    width = 5

    def rows(block, carry):
        at = [pl.multiple_of((block * width + i) * side, side) for i in range(width)]
        total = [jnp.zeros((images, side), jnp.float32) for _ in range(width)]
        for m in range(modes):
            weight = spread[m]
            for i in range(width):
                total[i] = total[i] + weight * screens[m : m + 1, pl.ds(at[i], side)]
        for i in range(width):
            up = block * width + i - half // 2
            inside = lane * lane + up * up <= (side // 4) ** 2
            field[block * width + i, :, 0:side] = jnp.where(inside, jnp.cos(total[i]), 0.0)
            field[block * width + i, :, side : 2 * side] = jnp.where(inside, jnp.sin(total[i]), 0.0)
        return carry

    lax.fori_loop(0, span // width, rows, 0)
    for i in range(span, pad_span):
        field[i] = jnp.zeros((images, 2 * side), jnp.float32)


def real_transform(planes, real, table, staged, out, alt):
    staged[...] = dot(real[...], planes)
    edge = []
    for n in range(images):
        lanes = slice(n * side, (n + 1) * side)
        edge.append(jnp.sum(staged[0:1, lanes] * alt, axis=1, keepdims=True))
        pair = jnp.concatenate([staged[0:side, lanes], staged[side : 2 * side, lanes]], axis=1)
        out[n] = dot(pair, table[...])
    return edge


def forward(img, screens, embed, first, second, head, tables, s):
    both, _, pupil, _, real, _, half_plane, _, swapped = tables
    alt = alternating(1)
    slot = jnp.logical_and(
        lax.broadcasted_iota(jnp.int32, (8, 2 * side), 0) == 0,
        lax.broadcasted_iota(jnp.int32, (8, 2 * side), 1) == half,
    )
    cut_tiles(img, s.tiles)
    alpha = encode(s.tiles, embed, first, second, head, s.hid_pre, s.inn_pre, s.inner_sum, s.pooled)
    planes = jnp.concatenate([img[n] for n in range(images)], axis=1)
    edge = real_transform(planes, real, swapped, s.staged, s.spec, alt)
    for n in range(images):
        s.spec[n, 0:8, :] = jnp.where(slot, edge[n] * (1.0 / side), s.spec[n, 0:8, :])
        s.energy[n : n + 1, :] = jnp.sum(img[n] * img[n], axis=0, keepdims=True)
    s.wait_screens()
    pupil_field(alpha, screens, s.spread, s.field)
    rowed = dot(s.field[...].reshape(pad_span * images, 2 * side), both[...])
    s.rowed_r[...] = rowed[:, 0:side]
    s.rowed_i[...] = rowed[:, side : 2 * side]
    for n in range(images):
        lanes = slice(n * side, (n + 1) * side)
        rows = pl.ds(n, pad_span, stride=images)
        s.stack[0:pad_span, lanes] = s.rowed_r[rows, :]
        s.stack[pad_span : 2 * pad_span, lanes] = s.rowed_i[rows, :]
    s.focal[...] = dot(pupil[...], s.stack[...])
    scale = 1.0 / (side * side * aperture_area())
    fr, fi = s.focal[0:side, :], s.focal[side : 2 * side, :]
    spot = (fr * fr + fi * fi) * scale
    edge = real_transform(spot, real, half_plane, s.staged, s.otf, alt)
    lane = lax.broadcasted_iota(jnp.int32, (side, side), 1)
    real_slot, at_corner = lane < half, corner(side)
    for n in range(images):
        s.otf[n, 0:8, :] = jnp.where(slot[:, :side], edge[n], s.otf[n, 0:8, :])
    for p in range(images // frames_here):
        t1 = t2 = t3 = None
        for f in range(frames_here):
            n = p * frames_here + f
            o, a, b = s.otf[n], s.spec[n, :, 0:side], s.spec[n, :, side : 2 * side]
            t1 = a * o if t1 is None else t1 + a * o
            t2 = b * o if t2 is None else t2 + b * o
            t3 = o * o if t3 is None else t3 + o * o
        turned = pltpu.roll(t2, half, 1)
        num = jnp.where(real_slot, t1 + pltpu.roll(t1, half, 1), turned - t2)
        num = jnp.where(at_corner, t1, num)
        den = jnp.where(at_corner, t3, t3 + pltpu.roll(t3, half, 1))
        s.part[p * 16 : (p + 1) * 16, 0:8, :] = num.reshape(16, 8, side)
        s.part[p * 16 : (p + 1) * 16, 8:16, :] = den.reshape(16, 8, side)


def backward(screens, tables, s):
    _, both_t, _, pupil_t, _, real_t, _, half_plane_t, _ = tables
    lane = lax.broadcasted_iota(jnp.int32, (side, side), 1)
    real_slot, at_corner = lane < half, corner(side)
    alt = alternating(1)
    per_pixel = 1.0 / (side * side)
    weight = jnp.where(lax.rem(lane, half) == 0, per_pixel, 2.0 * per_pixel)
    losses = []
    for p in range(images // frames_here):
        rho = s.ratio[p * 16 : (p + 1) * 16].reshape(side, side)
        num = s.part[p * 16 : (p + 1) * 16, 0:8, :].reshape(side, side)
        turned = pltpu.roll(rho, half, 1)
        square = rho * rho
        a = jnp.where(jnp.logical_or(real_slot, at_corner), rho, turned) * (-2.0 * weight)
        b = jnp.where(real_slot, turned, -rho)
        b = jnp.where(at_corner, 0.0, b) * (-2.0 * weight)
        m = jnp.where(at_corner, square, square + turned * turned) * (2.0 * weight)
        explained = jnp.sum(jnp.sum(weight * rho * num, axis=0, keepdims=True), axis=1, keepdims=True)
        energy = s.energy[p * frames_here : (p + 1) * frames_here, :]
        energy = jnp.sum(jnp.sum(energy, axis=0, keepdims=True), axis=1, keepdims=True)
        losses.append(energy * per_pixel - explained)
        for f in range(frames_here):
            n = p * frames_here + f
            lanes = slice(n * side, (n + 1) * side)
            g = a * s.spec[n, :, 0:side] + b * s.spec[n, :, side : 2 * side] + m * s.otf[n]
            y = dot(g, half_plane_t[...])
            s.staged[0:side, lanes] = y[:, 0:side]
            s.staged[side : 2 * side, lanes] = y[:, side : 2 * side]
            s.staged[0:1, lanes] = y[0:1, 0:side] + g[0:1, half : half + 1] * alt
    d_spot = dot(real_t[...], s.staged[...]) * (2.0 / (side * side * aperture_area()))
    d_focal = jnp.concatenate([s.focal[0:side, :] * d_spot, s.focal[side : 2 * side, :] * d_spot], axis=0)
    s.stack[...] = dot(pupil_t[...], d_focal)
    for n in range(images):
        lanes = slice(n * side, (n + 1) * side)
        rows = pl.ds(n, pad_span, stride=images)
        s.rowed_r[rows, :] = s.stack[0:pad_span, lanes]
        s.rowed_i[rows, :] = s.stack[pad_span : 2 * pad_span, lanes]
    rowed = jnp.concatenate([s.rowed_r[...], s.rowed_i[...]], axis=1)
    d_field = dot(rowed, both_t[...]).reshape(pad_span, images, 2 * side)
    f_r, f_i = s.field[:, :, 0:side], s.field[:, :, side : 2 * side]
    s.phase[...] = d_field[:, :, side : 2 * side] * f_r - d_field[:, :, 0:side] * f_i

    alpha_lane = lax.broadcasted_iota(jnp.int32, (images, side), 1)
    d_alpha = jnp.zeros((images, side), jnp.float32)
    chunk = 11
    for start in range(0, modes, chunk):

        def rows(i, total, start=start):
            value = s.phase[i]
            at = pl.multiple_of(i * side, side)
            return tuple(
                total[m] + value * screens[start + m : start + m + 1, pl.ds(at, side)]
                for m in range(chunk)
            )

        zero = tuple(jnp.zeros((images, side), jnp.float32) for _ in range(chunk))
        total = lax.fori_loop(0, span, rows, zero)
        for m in range(chunk):
            d_alpha = jnp.where(
                alpha_lane == start + m, jnp.sum(total[m], axis=1, keepdims=True), d_alpha
            )
    return d_alpha, losses


def encoder_gradients(d_alpha, tiles, embed, first, second, head, s):
    d_alpha44 = d_alpha[:, 0:modes]
    d_pooled = dot_nt(d_alpha44, head[...]) * (1.0 / tiles_each)
    s.grad_head[:, 0:side] = dot_tn(s.pooled[...], d_alpha)
    s.grad_second[...] = dot_tn(s.inner_sum[...], d_pooled)
    d_inner = dot_nt(d_pooled, second[...])
    width = embed.shape[1]

    def spread(value):
        return jnp.broadcast_to(value[:, None, :], (images, tiles_each, width)).reshape(-1, width)

    d_inner_pre = spread(d_inner) * silu_slope(s.inn_pre[...])
    s.grad_first[...] = dot_tn(silu_act(s.hid_pre[...]), d_inner_pre)
    d_hidden = spread(d_pooled) + dot_nt(d_inner_pre, first[...])
    s.grad_embed[...] = dot_tn(tiles[...], d_hidden * silu_slope(s.hid_pre[...]))


state_shapes = dict(
    tiles=(images * tiles_each, 256),
    hid_pre=(images * tiles_each, 256),
    inn_pre=(images * tiles_each, 256),
    inner_sum=(images, 256),
    pooled=(images, 256),
    energy=(images, side),
    spread=(modes, images, side),
    field=(pad_span, images, 2 * side),
    rowed_r=(pad_span * images, side),
    rowed_i=(pad_span * images, side),
    stack=(2 * pad_span, images * side),
    focal=(2 * side, images * side),
    staged=(2 * side, images * side),
    spec=(images, side, 2 * side),
    otf=(images, side, side),
    part=(32, 16, side),
    inbox=(32, 16, side),
    ratio=(32, 8, side),
    phase=(pad_span, images, side),
    screens=(modes, span * side),
)
gradient_shapes = dict(
    grad_embed=(256, 256), grad_first=(256, 256), grad_second=(256, 256), grad_head=(256, side), grad_tail=(128, 256)
)


class Place:
    def __init__(self):
        self.dp, self.frame = lax.axis_index("dp"), lax.axis_index("frame")
        self.core, self.x = lax.rem(self.frame, 2), lax.rem(self.frame // 2, 4)
        self.y, self.z_lo = self.dp // 2, lax.rem(self.dp, 2)
        self.z = (self.frame // 8) * 2 + self.z_lo

    def device(self, core, x, y, z):
        return {"dp": y * 2 + lax.rem(z, 2), "frame": (z // 2) * 8 + x * 2 + core}

    def x_peer(self, step):
        return lax.rem(self.x + step, 4)

    def y_peer(self, step):
        return lax.rem(self.y + step, 4)

    def z_peer(self, step):
        return lax.rem(self.z + step, 8)


def greet(group):
    place = Place()
    barrier = pltpu.get_barrier_semaphore()

    def one(step, carry):
        target = {"frame": lax.rem(place.frame + step, group)}
        pl.semaphore_signal(barrier, inc=1, device_id=target, device_id_type=MESH)
        return carry

    lax.fori_loop(1, group, one, 0)
    others = [place.device(place.core, place.x, place.y_peer(s), place.z) for s in range(1, 4)]
    others += [place.device(place.core, place.x, place.y, place.z_peer(s)) for s in (1, 3, 5, 7)]
    for target in others:
        pl.semaphore_signal(barrier, inc=1, device_id=target, device_id_type=MESH)
    return group - 1 + len(others)


def spectral_exchange(s, group, sems):
    me = lax.axis_index("frame")

    def peer(step):
        return lax.rem(me + step, group)

    def scatter_copy(step):
        return pltpu.make_async_remote_copy(
            src_ref=s.part.at[peer(step)],
            dst_ref=s.inbox.at[step],
            send_sem=sems.at[0, step],
            recv_sem=sems.at[1, step],
            device_id={"frame": peer(step)},
            device_id_type=MESH,
        )

    def gather_copy(step):
        return pltpu.make_async_remote_copy(
            src_ref=s.ratio.at[me],
            dst_ref=s.ratio.at[me],
            send_sem=sems.at[2, step],
            recv_sem=sems.at[3, step],
            device_id={"frame": peer(step)},
            device_id_type=MESH,
        )

    def start(copy):
        def one(step, carry):
            copy(step).start()
            return carry

        lax.fori_loop(1, group, one, 0)

    start(scatter_copy)

    def add(step, total):
        scatter_copy(step).wait_recv()
        return total + s.inbox[step]

    total = lax.fori_loop(1, group, add, s.part[me])
    s.ratio[me] = total[0:8] / (total[8:16] + regularizer_relative * (group * frames_here))
    start(gather_copy)

    def finish(step, carry):
        scatter_copy(step).wait_send()
        gather_copy(step).wait()
        return carry

    lax.fori_loop(1, group, finish, 0)


part_rows = (256, 256, 256, 128)


def buffer_shapes(half_width):
    shapes = [(r, half_width) for r in part_rows]
    shapes += [(r, half_width) for r in part_rows]
    shapes += [(3, r // 4, half_width) for r in part_rows]
    shapes += [(r // 4, half_width) for r in part_rows]
    shapes += [(3, r // 16, half_width) for r in part_rows]
    shapes += [(8, 8, half_width), (7, 8, half_width), (8, 8, half_width)]
    shapes += [(4, 8, 8, half_width), (4, 4, 8, 8, half_width), (4, 4, 8, 8, half_width)]
    return shapes


def gradient_exchange(parts, out_ref, buffers, sems):
    core_in, sums, x_in, x_sums, y_in = (buffers[4 * i : 4 * i + 4] for i in range(5))
    zone, z_in, z_all, y_all, x_all, core_all = buffers[20:]
    place = Place()
    core, x, y, z = place.core, place.x, place.y, place.z
    device, x_peer, y_peer, z_peer = place.device, place.x_peer, place.y_peer, place.z_peer
    core_peer = device(1 - core, x, y, z)

    used = [0]

    def copy(src, dst, target):
        slot = used[0]
        used[0] += 1
        one = pltpu.make_async_remote_copy(
            src_ref=src,
            dst_ref=dst,
            send_sem=sems.at[0, slot],
            recv_sem=sems.at[1, slot],
            device_id=target,
            device_id_type=MESH,
        )
        one.start()
        return one

    sent = []
    lanes = parts[0].shape[1] // 2
    mine = pl.ds(pl.multiple_of(core * lanes, lanes), lanes)
    other = pl.ds(pl.multiple_of((1 - core) * lanes, lanes), lanes)
    core_copies = [copy(parts[p].at[:, other], core_in[p], core_peer) for p in range(4)]
    sent += core_copies

    x_copies = []
    for p in range(4):
        core_copies[p].wait_recv()
        sums[p][...] = parts[p][:, mine] + core_in[p][...]
        size = part_rows[p] // 4
        x_copies.append([
            copy(
                sums[p].at[pl.ds(pl.multiple_of(x_peer(s) * size, size), size)],
                x_in[p].at[s - 1],
                device(core, x_peer(s), y, z),
            )
            for s in range(1, 4)
        ])
        sent += x_copies[p]

    y_copies = []
    for p in range(4):
        for one in x_copies[p]:
            one.wait_recv()
        size = part_rows[p] // 4
        own = sums[p][pl.ds(pl.multiple_of(x * size, size), size)]
        x_sums[p][...] = own + x_in[p][0] + x_in[p][1] + x_in[p][2]
        size = part_rows[p] // 16
        y_copies.append([
            copy(
                x_sums[p].at[pl.ds(pl.multiple_of(y_peer(s) * size, size), size)],
                y_in[p].at[s - 1],
                device(core, x, y_peer(s), z),
            )
            for s in range(1, 4)
        ])
        sent += y_copies[p]

    at = 0
    for p in range(4):
        for one in y_copies[p]:
            one.wait_recv()
        size = part_rows[p] // 16
        own = x_sums[p][pl.ds(pl.multiple_of(y * size, size), size)]
        total = own + y_in[p][0] + y_in[p][1] + y_in[p][2]
        for row in range(0, size, 8):
            zone[at // 8] = total[row : row + 8]
            at += 8
    zone[7] = jnp.zeros_like(zone[7])

    z_copies = [
        copy(zone.at[z_peer(s)], z_in.at[s - 1], device(core, x, y, z_peer(s))) for s in range(1, 8)
    ]
    sent += z_copies
    total = zone[z]
    for s in range(1, 8):
        z_copies[s - 1].wait_recv()
        total = total + z_in[s - 1]
    z_all[z] = total
    z_gather = [
        copy(z_all.at[z], z_all.at[z], device(core, x, y, z_peer(s))) for s in range(1, 8)
    ]
    sent += z_gather
    for one in z_gather:
        one.wait_recv()

    y_all[y] = z_all[...]
    y_gather = [
        copy(y_all.at[y], y_all.at[y], device(core, x, y_peer(s), z)) for s in range(1, 4)
    ]
    sent += y_gather
    for one in y_gather:
        one.wait_recv()

    x_all[x] = y_all[...]
    x_gather = [
        copy(x_all.at[x], x_all.at[x], device(core, x_peer(s), y, z)) for s in range(1, 4)
    ]
    sent += x_gather
    core_gather = [copy(x_all.at[x], core_all.at[x], core_peer)]
    for s in range(1, 4):
        x_gather[s - 1].wait_recv()
        came_from = lax.rem(x + 4 - s, 4)
        core_gather.append(copy(x_all.at[came_from], core_all.at[came_from], core_peer))
    sent += core_gather
    for one in core_gather:
        one.wait_recv()

    starts = (0, 2, 4, 6)
    for p in range(4):
        quarter, size = part_rows[p] // 4, part_rows[p] // 16
        base = p * 256
        for px in range(4):
            for py in range(4):
                for row in range(0, size, 8):
                    at = base + px * quarter + py * size + row
                    tile = starts[p] + row // 8
                    out_ref[at : at + 8, mine] = x_all[px, py, tile]
                    out_ref[at : at + 8, other] = core_all[px, py, tile]
    for one in sent:
        one.wait_send()


def kernel(names, group, *refs):
    img, screens_hbm, embed, first, second, head = refs[:6]
    tables, (alpha_ref, total_ref), scratch = refs[6:15], refs[15:17], refs[17:]
    s = types.SimpleNamespace(**dict(zip(names, scratch)))
    buffers = scratch[len(names) : -3]
    screens_sem, spectral_sems, gradient_sems = scratch[-3:]
    greeted = greet(group)
    fetch = pltpu.make_async_copy(
        screens_hbm.at[:, pl.ds(half // 2 * side, span * side)], s.screens, screens_sem
    )
    fetch.start()
    s.wait_screens = fetch.wait
    forward(img, s.screens, embed, first, second, head, tables, s)
    pl.semaphore_wait(pltpu.get_barrier_semaphore(), greeted)
    spectral_exchange(s, group, spectral_sems)
    d_alpha, losses = backward(s.screens, tables, s)
    alpha_ref[...] = d_alpha
    encoder_gradients(d_alpha, s.tiles, embed, first, second, head, s)
    s.grad_tail[:, 0:side] = s.grad_head[0:side, :]
    s.grad_tail[:, side : 2 * side] = s.grad_head[side : 2 * side, :]
    lane = lax.broadcasted_iota(jnp.int32, (1, side), 1)
    top = s.grad_tail[0:1, 0:side]
    for p in range(len(losses)):
        at = loss_lane + lax.axis_index("dp") * len(losses) + p
        top = jnp.where(lane == at, losses[p], top)
    s.grad_tail[0:1, 0:side] = top
    parts = (s.grad_embed, s.grad_first, s.grad_second, s.grad_tail)
    gradient_exchange(parts, total_ref, buffers, gradient_sems)


def local(recorded_exposures, screens, embed, first, second, head):
    regions = recorded_exposures.shape[0]
    group = lax.axis_size("frame")
    f32 = jnp.float32
    names = list(state_shapes) + list(gradient_shapes)
    shapes = list(state_shapes.values()) + list(gradient_shapes.values()) + buffer_shapes(side)
    vmem = pl.BlockSpec(memory_space=pltpu.VMEM)
    d_alpha, total = pl.pallas_call(
        functools.partial(kernel, names, group),
        out_shape=[
            jax.ShapeDtypeStruct((images, side), f32),
            jax.ShapeDtypeStruct((sum(part_rows), 2 * side), f32),
        ],
        in_specs=[vmem, pl.BlockSpec(memory_space=pl.ANY)] + [vmem] * 13,
        out_specs=[vmem] * 2,
        scratch_shapes=[pltpu.VMEM(shape, f32) for shape in shapes]
        + [
            pltpu.SemaphoreType.DMA(()),
            pltpu.SemaphoreType.DMA((4, group)),
            pltpu.SemaphoreType.DMA((2, 64)),
        ],
        compiler_params=pltpu.CompilerParams(
            collective_id=0, has_side_effects=True, vmem_limit_bytes=48 << 20
        ),
    )(
        recorded_exposures.reshape(images, side, side),
        screens, embed, first, second, head, *transform_tables(),
    )
    tail = total[768:]
    start = loss_lane + lax.axis_index("dp") * regions
    losses = lax.dynamic_slice(tail, (0, start), (1, regions))[0]
    return (
        d_alpha[:, :modes].reshape(regions, -1, modes),
        total[:256],
        total[256:512],
        total[512:768],
        jnp.concatenate([tail[:, :modes], tail[:, side : side + modes]], axis=0),
        losses / (group * frames_here),
    )


def solution(mesh):
    return jax.shard_map(
        local,
        mesh=mesh,
        in_specs=(P("dp", "frame", None, None), P(), P(), P(), P(), P()),
        out_specs=(P("dp", "frame", None), P(), P(), P(), P(), P("dp")),
        check_vma=False,
    )
```

```python
import functools
import types

import jax
import jax.numpy as jnp
import numpy as np
from jax import lax
from jax.experimental import pallas as pl
from jax.experimental.pallas import tpu as pltpu
from jax.sharding import PartitionSpec as P

entry_block_length = 16
regularizer_relative = 0.001
MESH = pl.DeviceIdType.MESH
HIGH = lax.Precision.HIGH
HIGHEST = lax.Precision.HIGHEST
side = 128
half = side // 2
span = half + 1
pad_span = 72
images = 8
frames_here = 4
modes = 44
tiles_each = 64
loss_row = 44


def dot(a, b, precision=HIGH):
    return jnp.dot(a, b, precision=precision, preferred_element_type=jnp.float32)


def dot_tn(a, b, precision=HIGH):
    return lax.dot_general(
        a, b, (((0,), (0,)), ((), ())), precision=precision, preferred_element_type=jnp.float32
    )


def dot_nt(a, b, precision=HIGH):
    return lax.dot_general(
        a, b, (((1,), (1,)), ((), ())), precision=precision, preferred_element_type=jnp.float32
    )


def transform_tables():
    index = np.arange(side)
    angle = 2.0 * np.pi / side * (index[:, None] * index[None, :] % side)
    c, s = np.cos(angle), np.sin(angle)
    both = np.block([[c, -s], [s, c]])
    lo = slice(0, half)
    half_plane = np.concatenate([both[:, lo], both[:, side : side + half]], axis=1)
    swapped = np.concatenate([half_plane, half_plane[:, half:], half_plane[:, :half]], axis=1)
    rows = slice(half // 2, half // 2 + span)
    pupil = np.zeros((2 * side, 2 * pad_span))
    pupil[:side, :span], pupil[:side, pad_span : pad_span + span] = c[:, rows], s[:, rows]
    pupil[side:, :span], pupil[side:, pad_span : pad_span + span] = -s[:, rows], c[:, rows]
    real = np.concatenate([c, -s], axis=0)
    narrow = np.concatenate([real, half_plane], axis=1)
    pupil_wide = np.concatenate([pupil, np.zeros((2 * side, 2 * side - 2 * pad_span))], axis=1)
    tables = (swapped / side, narrow, both, pupil_wide, both.T, pupil.T, real.T, half_plane.T)
    return np.concatenate(tables).astype(np.float32)


def split_tables(ref):
    sizes = (256, 256, 256, 256, 256, 2 * pad_span, side, side)
    views, at = [], 0
    for size in sizes:
        views.append(ref.at[at : at + size])
        at += size
    swapped, narrow, both, pupil, both_t, pupil_t, real_t, half_plane_t = views
    return types.SimpleNamespace(
        swapped=swapped, real=narrow.at[:, 0:side], half_plane=narrow.at[:, side:], both=both,
        pupil=pupil.at[:, 0 : 2 * pad_span], both_t=both_t, pupil_t=pupil_t, real_t=real_t,
        half_plane_t=half_plane_t,
    )


def aperture_area():
    at = np.arange(side) - half
    return float(np.sum(at[:, None] ** 2 + at[None, :] ** 2 <= (side // 4) ** 2))


def sigmoid(value):
    return 1.0 / (1.0 + jnp.exp(-value))


def silu_act(value):
    return value / (1.0 + jnp.exp(-value))


def silu_slope(value):
    gate = sigmoid(value)
    return gate * (1.0 + value * (1.0 - gate))


def alternating(rows):
    lane = lax.broadcasted_iota(jnp.int32, (rows, side), 1)
    return jnp.where(lax.rem(lane, 2) == 0, 1.0, -1.0).astype(jnp.float32)


def corner(rows):
    row = lax.broadcasted_iota(jnp.int32, (rows, side), 0)
    lane = lax.broadcasted_iota(jnp.int32, (rows, side), 1)
    return jnp.logical_and(row == 0, lax.rem(lane, half) == 0)


def cut_tiles(img, tiles):
    group = lax.broadcasted_iota(jnp.int32, (8, side), 1) // 16

    def one(n, carry):
        for g in range(2):
            x = [img[n, pl.ds(8 * g + j, 8, stride=16), :] for j in range(8)]
            for bit in (1, 2, 4):
                low = lax.rem(group // bit, 2) == 0
                y = list(x)
                for p in range(8):
                    if p & bit == 0:
                        q = p + bit
                        y[p] = jnp.where(low, x[p], pltpu.roll(x[q], 16 * bit, 1))
                        y[q] = jnp.where(low, pltpu.roll(x[p], side - 16 * bit, 1), x[q])
                x = y
            for c in range(8):
                tiles[pl.ds(pl.multiple_of(n * 64 + c * 8, 8), 8), g * side : (g + 1) * side] = x[c]
        return carry

    lax.fori_loop(0, images, one, 0)


def tile_sum(value):
    return jnp.sum(value.reshape(images, tiles_each, value.shape[1]), axis=1)


def encode(s):
    s.wait("embed")
    pre = dot(s.tiles[...], s.embed[...], HIGHEST)
    s.hid_pre[...] = pre
    hidden = silu_act(pre)
    s.wait("first")
    pre = dot(hidden, s.first[...], HIGHEST)
    s.inn_pre[...] = pre
    total = tile_sum(silu_act(pre))
    s.inner_sum[...] = total
    s.wait("second")
    mean = (tile_sum(hidden) + dot(total, s.second[...], HIGHEST)) * (1.0 / tiles_each)
    s.pooled[...] = mean
    s.wait("head")
    return dot_nt(mean, s.head[...], HIGHEST)


def pupil_field(alpha, screens, spread, field):
    for m in range(modes):
        spread[m] = jnp.broadcast_to(alpha[:, m : m + 1], (images, side))
    lane = lax.broadcasted_iota(jnp.int32, (images, side), 1) - half
    width = 5

    def rows(block, carry):
        at = [pl.multiple_of((block * width + i) * side, side) for i in range(width)]
        total = [jnp.zeros((images, side), jnp.float32) for _ in range(width)]
        for m in range(modes):
            weight = spread[m]
            for i in range(width):
                total[i] = total[i] + weight * screens[m : m + 1, pl.ds(at[i], side)]
        for i in range(width):
            up = block * width + i - half // 2
            inside = lane * lane + up * up <= (side // 4) ** 2
            field[block * width + i, :, 0:side] = jnp.where(inside, jnp.cos(total[i]), 0.0)
            field[block * width + i, :, side : 2 * side] = jnp.where(inside, jnp.sin(total[i]), 0.0)
        return carry

    lax.fori_loop(0, span // width, rows, 0)
    for i in range(span, pad_span):
        field[i] = jnp.zeros((images, 2 * side), jnp.float32)


def real_transform(planes, real, table, staged, out, alt):
    staged[...] = dot(real[...], planes)
    edge = []
    for n in range(images):
        lanes = slice(n * side, (n + 1) * side)
        edge.append(jnp.sum(staged[0:1, lanes] * alt, axis=1, keepdims=True))
        pair = jnp.concatenate([staged[0:side, lanes], staged[side : 2 * side, lanes]], axis=1)
        out[n] = dot(pair, table[...])
    return edge


def forward(s, t):
    img = s.img
    alt = alternating(1)
    slot = jnp.logical_and(
        lax.broadcasted_iota(jnp.int32, (8, 2 * side), 0) == 0,
        lax.broadcasted_iota(jnp.int32, (8, 2 * side), 1) == half,
    )
    s.wait("img")
    cut_tiles(img, s.tiles)
    alpha = encode(s)
    s.wait("tables")
    planes = jnp.concatenate([img[n] for n in range(images)], axis=1)
    edge = real_transform(planes, t.real, t.swapped, s.staged, s.spec, alt)
    for n in range(images):
        s.spec[n, 0:8, :] = jnp.where(slot, edge[n] * (1.0 / side), s.spec[n, 0:8, :])
        s.energy[n : n + 1, :] = jnp.sum(img[n] * img[n], axis=0, keepdims=True)
    s.wait("screens")
    pupil_field(alpha, s.screens, s.spread, s.field)
    rowed = dot(s.field[...].reshape(pad_span * images, 2 * side), t.both[...])
    s.rowed_r[...] = rowed[:, 0:side]
    s.rowed_i[...] = rowed[:, side : 2 * side]
    for n in range(images):
        lanes = slice(n * side, (n + 1) * side)
        rows = pl.ds(n, pad_span, stride=images)
        s.stack[0:pad_span, lanes] = s.rowed_r[rows, :]
        s.stack[pad_span : 2 * pad_span, lanes] = s.rowed_i[rows, :]
    s.focal[...] = dot(t.pupil[...], s.stack[...])
    scale = 1.0 / (side * side * aperture_area())
    fr, fi = s.focal[0:side, :], s.focal[side : 2 * side, :]
    spot = (fr * fr + fi * fi) * scale
    edge = real_transform(spot, t.real, t.half_plane, s.staged, s.otf, alt)
    lane = lax.broadcasted_iota(jnp.int32, (side, side), 1)
    real_slot, at_corner = lane < half, corner(side)
    for n in range(images):
        s.otf[n, 0:8, :] = jnp.where(slot[:, :side], edge[n], s.otf[n, 0:8, :])
    for p in range(images // frames_here):
        t1 = t2 = t3 = None
        for f in range(frames_here):
            n = p * frames_here + f
            o, a, b = s.otf[n], s.spec[n, :, 0:side], s.spec[n, :, side : 2 * side]
            t1 = a * o if t1 is None else t1 + a * o
            t2 = b * o if t2 is None else t2 + b * o
            t3 = o * o if t3 is None else t3 + o * o
        turned = pltpu.roll(t2, half, 1)
        num = jnp.where(real_slot, t1 + pltpu.roll(t1, half, 1), turned - t2)
        num = jnp.where(at_corner, t1, num)
        den = jnp.where(at_corner, t3, t3 + pltpu.roll(t3, half, 1))
        s.part[p * 16 : (p + 1) * 16, 0:8, :] = num.reshape(16, 8, side)
        s.part[p * 16 : (p + 1) * 16, 8:16, :] = den.reshape(16, 8, side)


def backward(s, t):
    screens = s.screens
    lane = lax.broadcasted_iota(jnp.int32, (side, side), 1)
    real_slot, at_corner = lane < half, corner(side)
    alt = alternating(1)
    per_pixel = 1.0 / (side * side)
    weight = jnp.where(lax.rem(lane, half) == 0, per_pixel, 2.0 * per_pixel)
    losses = []
    for p in range(images // frames_here):
        rho = s.ratio[p * 16 : (p + 1) * 16].reshape(side, side)
        num = s.part[p * 16 : (p + 1) * 16, 0:8, :].reshape(side, side)
        turned = pltpu.roll(rho, half, 1)
        square = rho * rho
        a = jnp.where(jnp.logical_or(real_slot, at_corner), rho, turned) * (-2.0 * weight)
        b = jnp.where(real_slot, turned, -rho)
        b = jnp.where(at_corner, 0.0, b) * (-2.0 * weight)
        m = jnp.where(at_corner, square, square + turned * turned) * (2.0 * weight)
        explained = jnp.sum(jnp.sum(weight * rho * num, axis=0, keepdims=True), axis=1, keepdims=True)
        energy = s.energy[p * frames_here : (p + 1) * frames_here, :]
        energy = jnp.sum(jnp.sum(energy, axis=0, keepdims=True), axis=1, keepdims=True)
        losses.append(energy * per_pixel - explained)
        for f in range(frames_here):
            n = p * frames_here + f
            lanes = slice(n * side, (n + 1) * side)
            g = a * s.spec[n, :, 0:side] + b * s.spec[n, :, side : 2 * side] + m * s.otf[n]
            y = dot(g, t.half_plane_t[...])
            s.staged[0:side, lanes] = y[:, 0:side]
            s.staged[side : 2 * side, lanes] = y[:, side : 2 * side]
            s.staged[0:1, lanes] = y[0:1, 0:side] + g[0:1, half : half + 1] * alt
    d_spot = dot(t.real_t[...], s.staged[...]) * (2.0 / (side * side * aperture_area()))
    d_focal = jnp.concatenate([s.focal[0:side, :] * d_spot, s.focal[side : 2 * side, :] * d_spot], axis=0)
    s.stack[...] = dot(t.pupil_t[...], d_focal)
    for n in range(images):
        lanes = slice(n * side, (n + 1) * side)
        rows = pl.ds(n, pad_span, stride=images)
        s.rowed_r[rows, :] = s.stack[0:pad_span, lanes]
        s.rowed_i[rows, :] = s.stack[pad_span : 2 * pad_span, lanes]
    rowed = jnp.concatenate([s.rowed_r[...], s.rowed_i[...]], axis=1)
    d_field = dot(rowed, t.both_t[...]).reshape(pad_span, images, 2 * side)
    f_r, f_i = s.field[:, :, 0:side], s.field[:, :, side : 2 * side]
    s.phase[...] = d_field[:, :, side : 2 * side] * f_r - d_field[:, :, 0:side] * f_i

    alpha_lane = lax.broadcasted_iota(jnp.int32, (images, side), 1)
    d_alpha = jnp.zeros((images, side), jnp.float32)
    chunk = 11
    for start in range(0, modes, chunk):

        def rows(i, total, start=start):
            value = s.phase[i]
            at = pl.multiple_of(i * side, side)
            return tuple(
                total[m] + value * screens[start + m : start + m + 1, pl.ds(at, side)]
                for m in range(chunk)
            )

        zero = tuple(jnp.zeros((images, side), jnp.float32) for _ in range(chunk))
        total = lax.fori_loop(0, span, rows, zero)
        for m in range(chunk):
            d_alpha = jnp.where(
                alpha_lane == start + m, jnp.sum(total[m], axis=1, keepdims=True), d_alpha
            )
    return d_alpha, losses


def encoder_gradients(d_alpha, s):
    d_pooled = dot(d_alpha[:, 0:modes], s.head[...]) * (1.0 / tiles_each)
    s.grad_tail[...] = dot_tn(d_alpha, s.pooled[...])
    s.grad_second[...] = dot_tn(s.inner_sum[...], d_pooled)
    d_inner = dot_nt(d_pooled, s.second[...])
    width = s.embed.shape[1]

    def spread(value):
        return jnp.broadcast_to(value[:, None, :], (images, tiles_each, width)).reshape(-1, width)

    d_inner_pre = spread(d_inner) * silu_slope(s.inn_pre[...])
    s.grad_first[...] = dot_tn(silu_act(s.hid_pre[...]), d_inner_pre)
    d_hidden = spread(d_pooled) + dot_nt(d_inner_pre, s.first[...])
    s.grad_embed[...] = dot_tn(s.tiles[...], d_hidden * silu_slope(s.hid_pre[...]))


state_shapes = dict(
    tiles=(images * tiles_each, 256),
    hid_pre=(images * tiles_each, 256),
    inn_pre=(images * tiles_each, 256),
    inner_sum=(images, 256),
    pooled=(images, 256),
    energy=(images, side),
    spread=(modes, images, side),
    field=(pad_span, images, 2 * side),
    rowed_r=(pad_span * images, side),
    rowed_i=(pad_span * images, side),
    stack=(2 * pad_span, images * side),
    focal=(2 * side, images * side),
    staged=(2 * side, images * side),
    spec=(images, side, 2 * side),
    otf=(images, side, side),
    part=(32, 16, side),
    inbox=(32, 16, side),
    ratio=(32, 8, side),
    phase=(pad_span, images, side),
    screens=(modes, span * side),
    img=(images, side, side),
    embed=(256, 256),
    first=(256, 256),
    second=(256, 256),
    head=(modes, 256),
    tables=(1680, 256),
)
gradient_shapes = dict(
    grad_embed=(256, 256), grad_first=(256, 256), grad_second=(256, 256), grad_tail=(128, 256)
)


class Place:
    def __init__(self):
        self.dp, self.frame = lax.axis_index("dp"), lax.axis_index("frame")
        self.core, self.x = lax.rem(self.frame, 2), lax.rem(self.frame // 2, 4)
        self.y, self.z_lo = self.dp // 2, lax.rem(self.dp, 2)
        self.z = (self.frame // 8) * 2 + self.z_lo

    def device(self, core, x, y, z):
        return {"dp": y * 2 + lax.rem(z, 2), "frame": (z // 2) * 8 + x * 2 + core}

    def x_peer(self, step):
        return lax.rem(self.x + step, 4)

    def y_peer(self, step):
        return lax.rem(self.y + step, 4)

    def z_peer(self, step):
        return lax.rem(self.z + step, 8)


def greet(group):
    place = Place()
    barrier = pltpu.get_barrier_semaphore()

    def one(step, carry):
        target = {"frame": lax.rem(place.frame + step, group)}
        pl.semaphore_signal(barrier, inc=1, device_id=target, device_id_type=MESH)
        return carry

    lax.fori_loop(1, group, one, 0)
    others = [place.device(place.core, place.x, place.y_peer(s), place.z) for s in range(1, 4)]
    others += [place.device(place.core, place.x, place.y, place.z_peer(s)) for s in (1, 3, 5, 7)]
    for target in others:
        pl.semaphore_signal(barrier, inc=1, device_id=target, device_id_type=MESH)
    return group - 1 + len(others)


def spectral_exchange(s, group, sems):
    me = lax.axis_index("frame")

    def peer(step):
        return lax.rem(me + step, group)

    def scatter_copy(step):
        return pltpu.make_async_remote_copy(
            src_ref=s.part.at[peer(step)],
            dst_ref=s.inbox.at[step],
            send_sem=sems.at[0, step],
            recv_sem=sems.at[1, step],
            device_id={"frame": peer(step)},
            device_id_type=MESH,
        )

    def gather_copy(step):
        return pltpu.make_async_remote_copy(
            src_ref=s.ratio.at[me],
            dst_ref=s.ratio.at[me],
            send_sem=sems.at[2, step],
            recv_sem=sems.at[3, step],
            device_id={"frame": peer(step)},
            device_id_type=MESH,
        )

    def start(copy):
        def one(step, carry):
            copy(step).start()
            return carry

        lax.fori_loop(1, group, one, 0)

    start(scatter_copy)

    def add(step, total):
        scatter_copy(step).wait_recv()
        return total + s.inbox[step]

    total = lax.fori_loop(1, group, add, s.part[me])
    s.ratio[me] = total[0:8] / (total[8:16] + regularizer_relative * (group * frames_here))
    start(gather_copy)

    def finish(step, carry):
        scatter_copy(step).wait_send()
        gather_copy(step).wait()
        return carry

    lax.fori_loop(1, group, finish, 0)


part_rows = (256, 256, 256, 128)


def buffer_shapes(half_width):
    shapes = [(r, half_width) for r in part_rows]
    shapes += [(r, half_width) for r in part_rows]
    shapes += [(3, r // 4, half_width) for r in part_rows]
    shapes += [(r // 4, half_width) for r in part_rows]
    shapes += [(3, r // 16, half_width) for r in part_rows]
    shapes += [(8, 8, half_width), (7, 8, half_width), (8, 8, half_width)]
    shapes += [(4, 8, 8, half_width), (4, 4, 8, 8, half_width), (4, 4, 8, 8, half_width)]
    return shapes


def gradient_exchange(parts, out_ref, buffers, sems):
    core_in, sums, x_in, x_sums, y_in = (buffers[4 * i : 4 * i + 4] for i in range(5))
    zone, z_in, z_all, y_all, x_all, core_all = buffers[20:]
    place = Place()
    core, x, y, z = place.core, place.x, place.y, place.z
    device, x_peer, y_peer, z_peer = place.device, place.x_peer, place.y_peer, place.z_peer
    core_peer = device(1 - core, x, y, z)

    used = [0]

    def copy(src, dst, target):
        slot = used[0]
        used[0] += 1
        one = pltpu.make_async_remote_copy(
            src_ref=src,
            dst_ref=dst,
            send_sem=sems.at[0, slot],
            recv_sem=sems.at[1, slot],
            device_id=target,
            device_id_type=MESH,
        )
        one.start()
        return one

    sent = []
    lanes = parts[0].shape[1] // 2
    mine = pl.ds(pl.multiple_of(core * lanes, lanes), lanes)
    other = pl.ds(pl.multiple_of((1 - core) * lanes, lanes), lanes)
    core_copies = [copy(parts[p].at[:, other], core_in[p], core_peer) for p in range(4)]
    sent += core_copies

    x_copies = []
    for p in range(4):
        core_copies[p].wait_recv()
        sums[p][...] = parts[p][:, mine] + core_in[p][...]
        size = part_rows[p] // 4
        x_copies.append([
            copy(
                sums[p].at[pl.ds(pl.multiple_of(x_peer(s) * size, size), size)],
                x_in[p].at[s - 1],
                device(core, x_peer(s), y, z),
            )
            for s in range(1, 4)
        ])
        sent += x_copies[p]

    y_copies = []
    for p in range(4):
        for one in x_copies[p]:
            one.wait_recv()
        size = part_rows[p] // 4
        own = sums[p][pl.ds(pl.multiple_of(x * size, size), size)]
        x_sums[p][...] = own + x_in[p][0] + x_in[p][1] + x_in[p][2]
        size = part_rows[p] // 16
        y_copies.append([
            copy(
                x_sums[p].at[pl.ds(pl.multiple_of(y_peer(s) * size, size), size)],
                y_in[p].at[s - 1],
                device(core, x, y_peer(s), z),
            )
            for s in range(1, 4)
        ])
        sent += y_copies[p]

    at = 0
    for p in range(4):
        for one in y_copies[p]:
            one.wait_recv()
        size = part_rows[p] // 16
        own = x_sums[p][pl.ds(pl.multiple_of(y * size, size), size)]
        total = own + y_in[p][0] + y_in[p][1] + y_in[p][2]
        for row in range(0, size, 8):
            zone[at // 8] = total[row : row + 8]
            at += 8
    zone[7] = jnp.zeros_like(zone[7])

    z_copies = [
        copy(zone.at[z_peer(s)], z_in.at[s - 1], device(core, x, y, z_peer(s))) for s in range(1, 8)
    ]
    sent += z_copies
    total = zone[z]
    for s in range(1, 8):
        z_copies[s - 1].wait_recv()
        total = total + z_in[s - 1]
    z_all[z] = total
    z_gather = [
        copy(z_all.at[z], z_all.at[z], device(core, x, y, z_peer(s))) for s in range(1, 8)
    ]
    sent += z_gather
    for one in z_gather:
        one.wait_recv()

    y_all[y] = z_all[...]
    y_gather = [
        copy(y_all.at[y], y_all.at[y], device(core, x, y_peer(s), z)) for s in range(1, 4)
    ]
    sent += y_gather
    for one in y_gather:
        one.wait_recv()

    x_all[x] = y_all[...]
    x_gather = [
        copy(x_all.at[x], x_all.at[x], device(core, x_peer(s), y, z)) for s in range(1, 4)
    ]
    sent += x_gather
    core_gather = [copy(x_all.at[x], core_all.at[x], core_peer)]
    for s in range(1, 4):
        x_gather[s - 1].wait_recv()
        came_from = lax.rem(x + 4 - s, 4)
        core_gather.append(copy(x_all.at[came_from], core_all.at[came_from], core_peer))
    sent += core_gather
    for one in core_gather:
        one.wait_recv()

    starts = (0, 2, 4, 6)
    for p in range(4):
        quarter, size = part_rows[p] // 4, part_rows[p] // 16
        base = p * 256
        for px in range(4):
            for py in range(4):
                for row in range(0, size, 8):
                    at = base + px * quarter + py * size + row
                    tile = starts[p] + row // 8
                    out_ref[at : at + 8, mine] = x_all[px, py, tile]
                    out_ref[at : at + 8, other] = core_all[px, py, tile]
    for one in sent:
        one.wait_send()


operands = ("img", "embed", "first", "second", "head", "tables", "screens")


def kernel(names, group, *refs):
    sources, (alpha_ref, total_ref), scratch = refs[:7], refs[7:9], refs[9:]
    s = types.SimpleNamespace(**dict(zip(names, scratch)))
    buffers = scratch[len(names) : -3]
    fetch_sems, spectral_sems, gradient_sems = scratch[-3:]
    fetches = {}
    for i, name in enumerate(operands):
        source = sources[i]
        if name == "screens":
            source = source.at[:, pl.ds(half // 2 * side, span * side)]
        fetches[name] = pltpu.make_async_copy(source, getattr(s, name), fetch_sems.at[i])
        fetches[name].start()
    s.wait = lambda name: fetches[name].wait()
    greeted = greet(group)
    t = split_tables(s.tables)
    forward(s, t)
    pl.semaphore_wait(pltpu.get_barrier_semaphore(), greeted)
    spectral_exchange(s, group, spectral_sems)
    d_alpha, losses = backward(s, t)
    alpha_ref[...] = d_alpha
    encoder_gradients(d_alpha, s)
    lane = lax.broadcasted_iota(jnp.int32, (1, side), 1)
    row = jnp.zeros((1, side), jnp.float32)
    for p in range(len(losses)):
        at = lax.axis_index("dp") * len(losses) + p
        row = jnp.where(lane == at, losses[p], row)
    s.grad_tail[loss_row : loss_row + 1, 0:side] = row
    parts = (s.grad_embed, s.grad_first, s.grad_second, s.grad_tail)
    gradient_exchange(parts, total_ref, buffers, gradient_sems)


def local(recorded_exposures, screens, embed, first, second, head):
    regions = recorded_exposures.shape[0]
    group = lax.axis_size("frame")
    f32 = jnp.float32
    names = list(state_shapes) + list(gradient_shapes)
    shapes = list(state_shapes.values()) + list(gradient_shapes.values()) + buffer_shapes(side)
    vmem = pl.BlockSpec(memory_space=pltpu.VMEM)
    d_alpha, total = pl.pallas_call(
        functools.partial(kernel, names, group),
        out_shape=[
            jax.ShapeDtypeStruct((images, side), f32),
            jax.ShapeDtypeStruct((sum(part_rows), 2 * side), f32),
        ],
        in_specs=[pl.BlockSpec(memory_space=pltpu.HBM)] * len(operands),
        out_specs=[vmem] * 2,
        scratch_shapes=[pltpu.VMEM(shape, f32) for shape in shapes]
        + [
            pltpu.SemaphoreType.DMA((len(operands),)),
            pltpu.SemaphoreType.DMA((4, group)),
            pltpu.SemaphoreType.DMA((2, 64)),
        ],
        compiler_params=pltpu.CompilerParams(
            collective_id=0, has_side_effects=True, vmem_limit_bytes=63 << 20
        ),
    )(
        recorded_exposures.reshape(images, side, side),
        embed, first, second, head.T, transform_tables(), screens,
    )
    start = lax.axis_index("dp") * regions
    losses = lax.dynamic_slice(total, (768 + loss_row, start), (1, regions))[0]
    return (
        d_alpha[:, :modes].reshape(regions, -1, modes),
        total[:256],
        total[256:512],
        total[512:768],
        total[768 : 768 + modes].T,
        losses / (group * frames_here),
    )


def solution(mesh):
    return jax.shard_map(
        local,
        mesh=mesh,
        in_specs=(P("dp", "frame", None, None), P(), P(), P(), P(), P()),
        out_specs=(P("dp", "frame", None), P(), P(), P(), P(), P("dp")),
        check_vma=False,
    )
```

```python
import functools
import types

import jax
import jax.numpy as jnp
import numpy as np
from jax import lax
from jax.experimental import pallas as pl
from jax.experimental.pallas import tpu as pltpu
from jax.sharding import PartitionSpec as P

entry_block_length = 16
regularizer_relative = 0.001
MESH = pl.DeviceIdType.MESH
HIGH = lax.Precision.HIGH
HIGHEST = lax.Precision.HIGHEST
side = 128
half = side // 2
span = half + 1
pad_span = 72
images = 8
frames_here = 4
modes = 44
tiles_each = 64
loss_row = 44


def dot(a, b, precision=HIGH):
    return jnp.dot(a, b, precision=precision, preferred_element_type=jnp.float32)


def dot_tn(a, b, precision=HIGH):
    return lax.dot_general(
        a, b, (((0,), (0,)), ((), ())), precision=precision, preferred_element_type=jnp.float32
    )


def dot_nt(a, b, precision=HIGH):
    return lax.dot_general(
        a, b, (((1,), (1,)), ((), ())), precision=precision, preferred_element_type=jnp.float32
    )


def transform_tables():
    index = np.arange(side)
    angle = 2.0 * np.pi / side * (index[:, None] * index[None, :] % side)
    c, s = np.cos(angle), np.sin(angle)
    both = np.block([[c, -s], [s, c]])
    lo = slice(0, half)
    half_plane = np.concatenate([both[:, lo], both[:, side : side + half]], axis=1)
    swapped = np.concatenate([half_plane, half_plane[:, half:], half_plane[:, :half]], axis=1)
    rows = slice(half // 2, half // 2 + span)
    pupil = np.zeros((2 * side, 2 * pad_span))
    pupil[:side, :span], pupil[:side, pad_span : pad_span + span] = c[:, rows], s[:, rows]
    pupil[side:, :span], pupil[side:, pad_span : pad_span + span] = -s[:, rows], c[:, rows]
    real = np.concatenate([c, -s], axis=0)
    narrow = np.concatenate([real, half_plane], axis=1)
    pupil_wide = np.concatenate([pupil, np.zeros((2 * side, 2 * side - 2 * pad_span))], axis=1)
    tables = (swapped / side, narrow, both, pupil_wide, both.T, pupil.T, real.T, half_plane.T)
    return np.concatenate(tables).astype(np.float32)


def split_tables(ref):
    sizes = (256, 256, 256, 256, 256, 2 * pad_span, side, side)
    views, at = [], 0
    for size in sizes:
        views.append(ref.at[at : at + size])
        at += size
    swapped, narrow, both, pupil, both_t, pupil_t, real_t, half_plane_t = views
    return types.SimpleNamespace(
        swapped=swapped, real=narrow.at[:, 0:side], half_plane=narrow.at[:, side:], both=both,
        pupil=pupil.at[:, 0 : 2 * pad_span], both_t=both_t, pupil_t=pupil_t, real_t=real_t,
        half_plane_t=half_plane_t,
    )


def aperture_area():
    at = np.arange(side) - half
    return float(np.sum(at[:, None] ** 2 + at[None, :] ** 2 <= (side // 4) ** 2))


def sigmoid(value):
    return 1.0 / (1.0 + jnp.exp(-value))


def silu_act(value):
    return value / (1.0 + jnp.exp(-value))


def silu_slope(value):
    gate = sigmoid(value)
    return gate * (1.0 + value * (1.0 - gate))


def alternating(rows):
    lane = lax.broadcasted_iota(jnp.int32, (rows, side), 1)
    return jnp.where(lax.rem(lane, 2) == 0, 1.0, -1.0).astype(jnp.float32)


def corner(rows):
    row = lax.broadcasted_iota(jnp.int32, (rows, side), 0)
    lane = lax.broadcasted_iota(jnp.int32, (rows, side), 1)
    return jnp.logical_and(row == 0, lax.rem(lane, half) == 0)


def cut_tiles(img, tiles):
    group = lax.broadcasted_iota(jnp.int32, (8, side), 1) // 16

    def one(n, carry):
        for g in range(2):
            x = [img[n, pl.ds(8 * g + j, 8, stride=16), :] for j in range(8)]
            for bit in (1, 2, 4):
                low = lax.rem(group // bit, 2) == 0
                y = list(x)
                for p in range(8):
                    if p & bit == 0:
                        q = p + bit
                        y[p] = jnp.where(low, x[p], pltpu.roll(x[q], 16 * bit, 1))
                        y[q] = jnp.where(low, pltpu.roll(x[p], side - 16 * bit, 1), x[q])
                x = y
            for c in range(8):
                tiles[pl.ds(pl.multiple_of(n * 64 + c * 8, 8), 8), g * side : (g + 1) * side] = x[c]
        return carry

    lax.fori_loop(0, images, one, 0)


def tile_sum(value):
    return jnp.sum(value.reshape(images, tiles_each, value.shape[1]), axis=1)


def encode(s):
    s.wait("embed")
    pre = dot(s.tiles[...], s.embed[...], HIGHEST)
    s.hid_pre[...] = pre
    hidden = silu_act(pre)
    s.wait("first")
    pre = dot(hidden, s.first[...], HIGHEST)
    s.inn_pre[...] = pre
    total = tile_sum(silu_act(pre))
    s.inner_sum[...] = total
    s.wait("second")
    mean = (tile_sum(hidden) + dot(total, s.second[...], HIGHEST)) * (1.0 / tiles_each)
    s.pooled[...] = mean
    s.wait("head")
    return dot_nt(mean, s.head[...], HIGHEST)


def pupil_field(alpha, screens, spread, field):
    for m in range(modes):
        spread[m] = jnp.broadcast_to(alpha[:, m : m + 1], (images, side))
    lane = lax.broadcasted_iota(jnp.int32, (images, side), 1) - half
    width = 5

    def rows(block, carry):
        at = [pl.multiple_of((block * width + i) * side, side) for i in range(width)]
        total = [jnp.zeros((images, side), jnp.float32) for _ in range(width)]
        for m in range(modes):
            weight = spread[m]
            for i in range(width):
                total[i] = total[i] + weight * screens[m : m + 1, pl.ds(at[i], side)]
        for i in range(width):
            up = block * width + i - half // 2
            inside = lane * lane + up * up <= (side // 4) ** 2
            field[block * width + i, :, 0:side] = jnp.where(inside, jnp.cos(total[i]), 0.0)
            field[block * width + i, :, side : 2 * side] = jnp.where(inside, jnp.sin(total[i]), 0.0)
        return carry

    lax.fori_loop(0, span // width, rows, 0)
    for i in range(span, pad_span):
        field[i] = jnp.zeros((images, 2 * side), jnp.float32)


def patch_lanes(p):
    return slice(p * frames_here * side, (p + 1) * frames_here * side)


def real_transform(planes, first_table, second_table, s, p, out):
    lanes = patch_lanes(p)
    s.staged[:, lanes] = dot(first_table[...], planes)
    edge = []
    for n in range(p * frames_here, (p + 1) * frames_here):
        lanes = slice(n * side, (n + 1) * side)
        edge.append(jnp.sum(s.staged[0:1, lanes] * alternating(1), axis=1, keepdims=True))
        pair = jnp.concatenate([s.staged[0:side, lanes], s.staged[side : 2 * side, lanes]], axis=1)
        out[n] = dot(pair, second_table[...])
    return edge


def edge_slot(width):
    row = lax.broadcasted_iota(jnp.int32, (8, width), 0)
    lane = lax.broadcasted_iota(jnp.int32, (8, width), 1)
    return jnp.logical_and(row == 0, lane == half)


def frame_spectra(s, t, p):
    here = range(p * frames_here, (p + 1) * frames_here)
    planes = jnp.concatenate([s.img[n] for n in here], axis=1)
    edge = real_transform(planes, t.real, t.swapped, s, p, s.spec)
    for n in here:
        value = edge[n - here[0]] * (1.0 / side)
        s.spec[n, 0:8, :] = jnp.where(edge_slot(2 * side), value, s.spec[n, 0:8, :])


def frame_energy(s):
    for n in range(images):
        s.energy[n : n + 1, :] = jnp.sum(s.img[n] * s.img[n], axis=0, keepdims=True)


def pupil_rows(s, t):
    rowed = dot(s.field[...].reshape(pad_span * images, 2 * side), t.both[...])
    s.rowed_r[...] = rowed[:, 0:side]
    s.rowed_i[...] = rowed[:, side : 2 * side]
    for n in range(images):
        lanes = slice(n * side, (n + 1) * side)
        rows = pl.ds(n, pad_span, stride=images)
        s.stack[0:pad_span, lanes] = s.rowed_r[rows, :]
        s.stack[pad_span : 2 * pad_span, lanes] = s.rowed_i[rows, :]


def spectral_sums(s, t, p):
    lanes = patch_lanes(p)
    s.focal[:, lanes] = dot(t.pupil[...], s.stack[:, lanes])
    fr, fi = s.focal[0:side, lanes], s.focal[side : 2 * side, lanes]
    spot = (fr * fr + fi * fi) * (1.0 / (side * side * aperture_area()))
    edge = real_transform(spot, t.real, t.half_plane, s, p, s.otf)
    real_slot = lax.broadcasted_iota(jnp.int32, (side, side), 1) < half
    at_corner = corner(side)
    t1 = t2 = t3 = 0.0
    for f in range(frames_here):
        n = p * frames_here + f
        s.otf[n, 0:8, :] = jnp.where(edge_slot(side), edge[f], s.otf[n, 0:8, :])
        o, a, b = s.otf[n], s.spec[n, :, 0:side], s.spec[n, :, side : 2 * side]
        t1, t2, t3 = t1 + a * o, t2 + b * o, t3 + o * o
    turned = pltpu.roll(t2, half, 1)
    num = jnp.where(real_slot, t1 + pltpu.roll(t1, half, 1), turned - t2)
    num = jnp.where(at_corner, t1, num)
    den = jnp.where(at_corner, t3, t3 + pltpu.roll(t3, half, 1))
    s.part[p * 16 : (p + 1) * 16, 0:8, :] = num.reshape(16, 8, side)
    s.part[p * 16 : (p + 1) * 16, 8:16, :] = den.reshape(16, 8, side)


def total_of(value):
    return jnp.sum(jnp.sum(value, axis=0, keepdims=True), axis=1, keepdims=True)


def focal_adjoint(s, t, p):
    lane = lax.broadcasted_iota(jnp.int32, (side, side), 1)
    real_slot, at_corner = lane < half, corner(side)
    per_pixel = 1.0 / (side * side)
    weight = jnp.where(lax.rem(lane, half) == 0, per_pixel, 2.0 * per_pixel)
    rho = s.ratio[p * 16 : (p + 1) * 16].reshape(side, side)
    num = s.part[p * 16 : (p + 1) * 16, 0:8, :].reshape(side, side)
    turned = pltpu.roll(rho, half, 1)
    square = rho * rho
    a = jnp.where(jnp.logical_or(real_slot, at_corner), rho, turned) * (-2.0 * weight)
    b = jnp.where(real_slot, turned, -rho)
    b = jnp.where(at_corner, 0.0, b) * (-2.0 * weight)
    m = jnp.where(at_corner, square, square + turned * turned) * (2.0 * weight)
    energy = total_of(s.energy[p * frames_here : (p + 1) * frames_here, :])
    loss = energy * per_pixel - total_of(weight * rho * num)
    for f in range(frames_here):
        n = p * frames_here + f
        lanes = slice(n * side, (n + 1) * side)
        g = a * s.spec[n, :, 0:side] + b * s.spec[n, :, side : 2 * side] + m * s.otf[n]
        y = dot(g, t.half_plane_t[...])
        s.staged[0:side, lanes] = y[:, 0:side]
        s.staged[side : 2 * side, lanes] = y[:, side : 2 * side]
        s.staged[0:1, lanes] = y[0:1, 0:side] + g[0:1, half : half + 1] * alternating(1)
    lanes = patch_lanes(p)
    d_spot = dot(t.real_t[...], s.staged[:, lanes]) * (2.0 / (side * side * aperture_area()))
    d_focal = jnp.concatenate(
        [s.focal[0:side, lanes] * d_spot, s.focal[side : 2 * side, lanes] * d_spot], axis=0
    )
    s.stack[:, lanes] = dot(t.pupil_t[...], d_focal)
    return loss


def alpha_adjoint(s, t):
    screens = s.screens
    for n in range(images):
        lanes = slice(n * side, (n + 1) * side)
        rows = pl.ds(n, pad_span, stride=images)
        s.rowed_r[rows, :] = s.stack[0:pad_span, lanes]
        s.rowed_i[rows, :] = s.stack[pad_span : 2 * pad_span, lanes]
    rowed = jnp.concatenate([s.rowed_r[...], s.rowed_i[...]], axis=1)
    d_field = dot(rowed, t.both_t[...]).reshape(pad_span, images, 2 * side)
    f_r, f_i = s.field[:, :, 0:side], s.field[:, :, side : 2 * side]
    s.phase[...] = d_field[:, :, side : 2 * side] * f_r - d_field[:, :, 0:side] * f_i

    alpha_lane = lax.broadcasted_iota(jnp.int32, (images, side), 1)
    d_alpha = jnp.zeros((images, side), jnp.float32)
    chunk = 11
    for start in range(0, modes, chunk):

        def rows(i, total, start=start):
            value = s.phase[i]
            at = pl.multiple_of(i * side, side)
            return tuple(
                total[m] + value * screens[start + m : start + m + 1, pl.ds(at, side)]
                for m in range(chunk)
            )

        zero = tuple(jnp.zeros((images, side), jnp.float32) for _ in range(chunk))
        total = lax.fori_loop(0, span, rows, zero)
        for m in range(chunk):
            d_alpha = jnp.where(
                alpha_lane == start + m, jnp.sum(total[m], axis=1, keepdims=True), d_alpha
            )
    return d_alpha


def spread(value):
    return jnp.broadcast_to(value[:, None, :], (images, tiles_each, 256)).reshape(-1, 256)


def gradients_after_mean(s, d_alpha):
    s.grad_tail[...] = dot_tn(d_alpha, s.pooled[...])
    d_pooled = dot(d_alpha[:, 0:modes], s.head[...]) * (1.0 / tiles_each)
    s.grad_second[...] = dot_tn(s.inner_sum[...], d_pooled)
    return d_pooled


def gradient_first(s, d_pooled):
    d_inner = spread(dot_nt(d_pooled, s.second[...])) * silu_slope(s.inn_pre[...])
    s.grad_first[...] = dot_tn(silu_act(s.hid_pre[...]), d_inner)
    return d_inner


def gradient_embed(s, d_pooled, d_inner):
    d_hidden = spread(d_pooled) + dot_nt(d_inner, s.first[...])
    s.grad_embed[...] = dot_tn(s.tiles[...], d_hidden * silu_slope(s.hid_pre[...]))


state_shapes = dict(
    tiles=(images * tiles_each, 256),
    hid_pre=(images * tiles_each, 256),
    inn_pre=(images * tiles_each, 256),
    inner_sum=(images, 256),
    pooled=(images, 256),
    energy=(images, side),
    spread=(modes, images, side),
    field=(pad_span, images, 2 * side),
    rowed_r=(pad_span * images, side),
    rowed_i=(pad_span * images, side),
    stack=(2 * pad_span, images * side),
    focal=(2 * side, images * side),
    staged=(2 * side, images * side),
    spec=(images, side, 2 * side),
    otf=(images, side, side),
    part=(32, 16, side),
    core_part=(16, 16, side),
    merged=(16, 16, side),
    inbox=(15, 16, side),
    ratio=(32, 8, side),
    phase=(pad_span, images, side),
    screens=(modes, span * side),
    img=(images, side, side),
    embed=(256, 256),
    first=(256, 256),
    second=(256, 256),
    head=(modes, 256),
    tables=(1680, 256),
)
gradient_shapes = dict(
    grad_embed=(256, 256), grad_first=(256, 256), grad_second=(256, 256), grad_tail=(128, 256)
)


def ring_distance(step, size):
    return min(step, size - step)


plane_steps = sorted(
    ((dx, dy) for dx in range(4) for dy in range(4) if dx or dy),
    key=lambda d: ring_distance(d[0], 4) + ring_distance(d[1], 4),
)
burst_steps = sorted(
    ((dx, dz) for dx in range(4) for dz in range(4) if dx or dz),
    key=lambda d: ring_distance(d[0], 4) + 2 * ring_distance(d[1], 4),
)
column_steps = sorted(range(1, 8), key=lambda d: ring_distance(d, 8))


class Place:
    def __init__(self):
        self.dp, self.frame = lax.axis_index("dp"), lax.axis_index("frame")
        self.core, self.x = lax.rem(self.frame, 2), lax.rem(self.frame // 2, 4)
        self.y, self.z_lo = self.dp // 2, lax.rem(self.dp, 2)
        self.z_hi = self.frame // 8
        self.z = self.z_hi * 2 + self.z_lo
        self.spot = self.x * 4 + self.y
        self.seat = self.z_hi * 4 + self.x

    def device(self, core, x, y, z):
        return {"dp": y * 2 + lax.rem(z, 2), "frame": (z // 2) * 8 + x * 2 + core}

    def sibling(self):
        return self.device(1 - self.core, self.x, self.y, self.z)

    def plane(self, step, sign=1):
        x = lax.rem(self.x + 4 + sign * step[0], 4)
        y = lax.rem(self.y + 4 + sign * step[1], 4)
        return x * 4 + y, self.device(self.core, x, y, self.z)

    def burst(self, step, sign=1):
        x = lax.rem(self.x + 4 + sign * step[0], 4)
        z_hi = lax.rem(self.z_hi + 4 + sign * step[1], 4)
        return z_hi * 4 + x, self.device(self.core, x, self.y, z_hi * 2 + self.z_lo)

    def column(self, step):
        return self.device(self.core, self.x, self.y, lax.rem(self.z + step, 8))


def greet():
    place = Place()
    targets = [place.sibling()]
    targets += [place.burst(step)[1] for step in burst_steps]
    targets += [place.plane(step)[1] for step in plane_steps if step[1]]
    targets += [place.column(step) for step in column_steps if step % 2]
    for target in targets:
        pl.semaphore_signal(
            pltpu.get_barrier_semaphore(), inc=1, device_id=target, device_id_type=MESH
        )
    return len(targets)


class Mail:
    def __init__(self, sems):
        self.sems, self.used, self.sent = sems, 0, []

    def send(self, src, dst, target):
        slot = self.used
        self.used += 1
        copy = pltpu.make_async_remote_copy(
            src_ref=src,
            dst_ref=dst,
            send_sem=self.sems.at[0, slot],
            recv_sem=self.sems.at[1, slot],
            device_id=target,
            device_id_type=MESH,
        )
        copy.start()
        self.sent.append(copy)
        return copy

    def finish(self):
        for copy in self.sent:
            copy.wait_send()


def spectral_exchange(s, regularizer_strength, sems):
    place, mail = Place(), Mail(sems)
    core, seat = place.core, place.seat
    swap = mail.send(s.part.at[pl.ds((1 - core) * 16, 16)], s.core_part, place.sibling())
    swap.wait_recv()
    s.merged[...] = s.part[pl.ds(core * 16, 16)] + s.core_part[...]
    copies = {}
    for i, step in reversed(list(enumerate(burst_steps))):
        there, device = place.burst(step)
        copies[i] = mail.send(s.merged.at[there], s.inbox.at[i], device)
    total = s.merged[seat]
    for i in range(len(burst_steps)):
        copies[i].wait_recv()
        total = total + s.inbox[i]
    mine = core * 16 + seat
    s.ratio[mine] = total[0:8] / (total[8:16] + regularizer_strength)
    copies = {}
    for i, step in reversed(list(enumerate(burst_steps))):
        copies[i] = mail.send(s.ratio.at[mine], s.ratio.at[mine], place.burst(step)[1])
    passed = [mail.send(s.ratio.at[mine], s.ratio.at[mine], place.sibling())]
    for i, step in enumerate(burst_steps):
        copies[i].wait_recv()
        came = core * 16 + place.burst(step, -1)[0]
        passed.append(mail.send(s.ratio.at[came], s.ratio.at[came], place.sibling()))
    for copy in passed:
        copy.wait_recv()
    mail.finish()


class GradientGroup:
    def __init__(self, parts, buffers, sems):
        self.parts = parts
        self.core_in, self.sums, self.inbox, self.column_in, self.full, self.other = buffers
        self.place, self.mail = Place(), Mail(sems)
        core = self.place.core
        self.mine = pl.ds(pl.multiple_of(core * side, side), side)
        self.theirs = pl.ds(pl.multiple_of((1 - core) * side, side), side)
        self.swaps = []

    def send_core(self, part):
        ref, at = self.parts[part]
        rows = ref.shape[0]
        self.swaps.append(
            self.mail.send(
                ref.at[:, self.theirs], self.core_in.at[at : at + rows], self.place.sibling()
            )
        )

    def send_plane(self):
        row = 0
        for swap, (ref, at) in zip(self.swaps, self.parts):
            swap.wait_recv()
            rows = ref.shape[0]
            total = ref[:, self.mine] + self.core_in[at : at + rows]
            each = rows // 16
            self.sums[:, row : row + each, :] = total.reshape(16, each, side)
            row += each
        self.copies = {}
        for i, step in reversed(list(enumerate(plane_steps))):
            there, device = self.place.plane(step)
            self.copies[i] = self.mail.send(self.sums.at[there], self.inbox.at[i], device)

    def send_column(self):
        total = self.sums[self.place.spot]
        for i in range(len(plane_steps)):
            self.copies[i].wait_recv()
            total = total + self.inbox[i]
        z = self.place.z
        self.column_in[z] = total
        self.copies = [
            self.mail.send(self.column_in.at[z], self.column_in.at[z], self.place.column(step))
            for step in reversed(column_steps)
        ]

    def send_back(self):
        for copy in self.copies:
            copy.wait_recv()
        total = self.column_in[0]
        for z in range(1, 8):
            total = total + self.column_in[z]
        spot = self.place.spot
        self.full[spot] = total
        self.copies = {}
        for i, step in reversed(list(enumerate(plane_steps))):
            device = self.place.plane(step)[1]
            self.copies[i] = self.mail.send(self.full.at[spot], self.full.at[spot], device)
        self.passed = [
            self.mail.send(self.full.at[spot], self.other.at[spot], self.place.sibling())
        ]

    def pass_on(self):
        for i, step in enumerate(plane_steps):
            self.copies[i].wait_recv()
            came = self.place.plane(step, -1)[0]
            self.passed.append(
                self.mail.send(self.full.at[came], self.other.at[came], self.place.sibling())
            )

    def finish(self, outs):
        for copy in self.passed:
            copy.wait_recv()
        row = 0
        for (ref, _), out in zip(self.parts, outs):
            each = ref.shape[0] // 16
            for values, lanes in ((self.full, self.mine), (self.other, self.theirs)):
                out[:, lanes] = values[:, row : row + each, :].reshape(16 * each, side)
            row += each
        self.mail.finish()


def group_buffers(rows):
    each = rows // 16
    return [
        (rows, side), (16, each, side), (15, each, side), (8, each, side), (16, each, side),
        (16, each, side),
    ]


operands = ("img", "embed", "first", "second", "head", "tables", "screens")
early_rows = (256, 128)
late_rows = (256, 256)


def kernel(names, frames_total, *refs):
    sources, (alpha_ref, loss_ref, total_ref), scratch = refs[:7], refs[7:10], refs[10:]
    s = types.SimpleNamespace(**dict(zip(names, scratch)))
    buffers = scratch[len(names) : -4]
    fetch_sems, spectral_sems, early_sems, late_sems = scratch[-4:]
    fetches = {}
    for i, name in enumerate(operands):
        source = sources[i]
        if name == "screens":
            source = source.at[:, pl.ds(half // 2 * side, span * side)]
        fetches[name] = pltpu.make_async_copy(source, getattr(s, name), fetch_sems.at[i])
        fetches[name].start()
    s.wait = lambda name: fetches[name].wait()
    greeted = greet()
    t = split_tables(s.tables)

    s.wait("img")
    cut_tiles(s.img, s.tiles)
    alpha = encode(s)
    s.wait("screens")
    pupil_field(alpha, s.screens, s.spread, s.field)
    s.wait("tables")
    pupil_rows(s, t)
    patches = range(images // frames_here)
    for p in patches:
        frame_spectra(s, t, p)
        spectral_sums(s, t, p)
    frame_energy(s)
    pl.semaphore_wait(pltpu.get_barrier_semaphore(), greeted)
    spectral_exchange(s, regularizer_relative * frames_total, spectral_sems)
    losses = [focal_adjoint(s, t, p) for p in patches]
    d_alpha = alpha_adjoint(s, t)
    alpha_ref[...] = d_alpha

    early = GradientGroup(((s.grad_second, 0), (s.grad_tail, 256)), buffers[:6], early_sems)
    late = GradientGroup(((s.grad_first, 0), (s.grad_embed, 256)), buffers[6:], late_sems)
    d_pooled = gradients_after_mean(s, d_alpha)
    lane = lax.broadcasted_iota(jnp.int32, (1, side), 1)
    row = jnp.zeros((1, side), jnp.float32)
    for p in patches:
        at = lax.axis_index("dp") * len(patches) + p
        row = jnp.where(lane == at, losses[p], row)
    s.grad_tail[loss_row : loss_row + 1, 0:side] = row
    early.send_core(0)
    early.send_core(1)
    d_inner = gradient_first(s, d_pooled)
    late.send_core(0)
    early.send_plane()
    gradient_embed(s, d_pooled, d_inner)
    late.send_core(1)
    late.send_plane()
    early.send_column()
    late.send_column()
    early.send_back()
    late.send_back()
    early.pass_on()
    late.pass_on()
    early.finish((total_ref.at[512:768], total_ref.at[768:896]))
    late.finish((total_ref.at[256:512], total_ref.at[0:256]))
    at = 768 + loss_row
    loss_ref[...] = total_ref[at : at + 1, 0:side] * (1.0 / frames_total)


def local(recorded_exposures, screens, embed, first, second, head):
    regions = recorded_exposures.shape[0]
    frames_total = recorded_exposures.shape[1] * lax.axis_size("frame")
    f32 = jnp.float32
    names = list(state_shapes) + list(gradient_shapes)
    shapes = list(state_shapes.values()) + list(gradient_shapes.values())
    shapes += group_buffers(sum(early_rows)) + group_buffers(sum(late_rows))
    vmem = pl.BlockSpec(memory_space=pltpu.VMEM)
    d_alpha, losses, total = pl.pallas_call(
        functools.partial(kernel, names, frames_total),
        out_shape=[
            jax.ShapeDtypeStruct((images, side), f32),
            jax.ShapeDtypeStruct((1, side), f32),
            jax.ShapeDtypeStruct((896, 2 * side), f32),
        ],
        in_specs=[pl.BlockSpec(memory_space=pltpu.HBM)] * len(operands),
        out_specs=[vmem] * 3,
        scratch_shapes=[pltpu.VMEM(shape, f32) for shape in shapes]
        + [pltpu.SemaphoreType.DMA((len(operands),))]
        + [pltpu.SemaphoreType.DMA((2, 64))] * 3,
        compiler_params=pltpu.CompilerParams(
            collective_id=0, has_side_effects=True, vmem_limit_bytes=63 << 20
        ),
    )(
        recorded_exposures.reshape(images, side, side),
        embed, first, second, head.T, transform_tables(), screens,
    )
    start = lax.axis_index("dp") * regions
    return (
        d_alpha[:, :modes].reshape(regions, -1, modes),
        total[:256],
        total[256:512],
        total[512:768],
        total[768 : 768 + modes].T,
        lax.dynamic_slice(losses, (0, start), (1, regions))[0],
    )


def solution(mesh):
    return jax.shard_map(
        local,
        mesh=mesh,
        in_specs=(P("dp", "frame", None, None), P(), P(), P(), P(), P()),
        out_specs=(P("dp", "frame", None), P(), P(), P(), P(), P("dp")),
        check_vma=False,
    )
```

```python
import functools
import types

import jax
import jax.numpy as jnp
import numpy as np
from jax import lax
from jax.experimental import pallas as pl
from jax.experimental.pallas import tpu as pltpu
from jax.sharding import PartitionSpec as P

entry_block_length = 16
regularizer_relative = 0.001
MESH = pl.DeviceIdType.MESH
HIGH = lax.Precision.HIGH
HIGHEST = lax.Precision.HIGHEST
side = 128
half = side // 2
span = half + 1
pad_span = 72
images = 8
frames_here = 4
modes = 44
tiles_each = 64
loss_row = 44


def dot(a, b, precision=HIGH):
    return jnp.dot(a, b, precision=precision, preferred_element_type=jnp.float32)


def dot_tn(a, b, precision=HIGH):
    return lax.dot_general(
        a, b, (((0,), (0,)), ((), ())), precision=precision, preferred_element_type=jnp.float32
    )


def dot_nt(a, b, precision=HIGH):
    return lax.dot_general(
        a, b, (((1,), (1,)), ((), ())), precision=precision, preferred_element_type=jnp.float32
    )


def transform_tables():
    index = np.arange(side)
    angle = 2.0 * np.pi / side * (index[:, None] * index[None, :] % side)
    c, s = np.cos(angle), np.sin(angle)
    both = np.block([[c, -s], [s, c]])
    lo = slice(0, half)
    half_plane = np.concatenate([both[:, lo], both[:, side : side + half]], axis=1)
    swapped = np.concatenate([half_plane, half_plane[:, half:], half_plane[:, :half]], axis=1)
    rows = slice(half // 2, half // 2 + span)
    pupil = np.zeros((2 * side, 2 * pad_span))
    pupil[:side, :span], pupil[:side, pad_span : pad_span + span] = c[:, rows], s[:, rows]
    pupil[side:, :span], pupil[side:, pad_span : pad_span + span] = -s[:, rows], c[:, rows]
    real = np.concatenate([c, -s], axis=0)
    narrow = np.concatenate([real, half_plane], axis=1)
    pupil_wide = np.concatenate([pupil, np.zeros((2 * side, 2 * side - 2 * pad_span))], axis=1)
    tables = (swapped / side, narrow, both, pupil_wide, both.T, pupil.T, real.T, half_plane.T)
    return np.concatenate(tables).astype(np.float32)


def split_tables(ref):
    sizes = (256, 256, 256, 256, 256, 2 * pad_span, side, side)
    views, at = [], 0
    for size in sizes:
        views.append(ref.at[at : at + size])
        at += size
    swapped, narrow, both, pupil, both_t, pupil_t, real_t, half_plane_t = views
    return types.SimpleNamespace(
        swapped=swapped, real=narrow.at[:, 0:side], half_plane=narrow.at[:, side:], both=both,
        pupil=pupil.at[:, 0 : 2 * pad_span], both_t=both_t, pupil_t=pupil_t, real_t=real_t,
        half_plane_t=half_plane_t,
    )


def aperture_area():
    at = np.arange(side) - half
    return float(np.sum(at[:, None] ** 2 + at[None, :] ** 2 <= (side // 4) ** 2))


def sigmoid(value):
    return 1.0 / (1.0 + jnp.exp(-value))


def silu_act(value):
    return value / (1.0 + jnp.exp(-value))


def silu_slope(value):
    gate = sigmoid(value)
    return gate * (1.0 + value * (1.0 - gate))


def alternating(rows):
    lane = lax.broadcasted_iota(jnp.int32, (rows, side), 1)
    return jnp.where(lax.rem(lane, 2) == 0, 1.0, -1.0).astype(jnp.float32)


def corner(rows):
    row = lax.broadcasted_iota(jnp.int32, (rows, side), 0)
    lane = lax.broadcasted_iota(jnp.int32, (rows, side), 1)
    return jnp.logical_and(row == 0, lax.rem(lane, half) == 0)


def cut_tiles(img, tiles):
    group = lax.broadcasted_iota(jnp.int32, (8, side), 1) // 16

    def one(n, carry):
        for g in range(2):
            x = [img[n, pl.ds(8 * g + j, 8, stride=16), :] for j in range(8)]
            for bit in (1, 2, 4):
                low = lax.rem(group // bit, 2) == 0
                y = list(x)
                for p in range(8):
                    if p & bit == 0:
                        q = p + bit
                        y[p] = jnp.where(low, x[p], pltpu.roll(x[q], 16 * bit, 1))
                        y[q] = jnp.where(low, pltpu.roll(x[p], side - 16 * bit, 1), x[q])
                x = y
            for c in range(8):
                tiles[pl.ds(pl.multiple_of(n * 64 + c * 8, 8), 8), g * side : (g + 1) * side] = x[c]
        return carry

    lax.fori_loop(0, images, one, 0)


def tile_sum(value):
    return jnp.sum(value.reshape(images, tiles_each, value.shape[1]), axis=1)


def encode(s):
    s.wait("embed")
    pre = dot(s.tiles[...], s.embed[...], HIGHEST)
    s.hid_pre[...] = pre
    hidden = silu_act(pre)
    s.wait("first")
    pre = dot(hidden, s.first[...], HIGHEST)
    s.inn_pre[...] = pre
    total = tile_sum(silu_act(pre))
    s.inner_sum[...] = total
    s.wait("second")
    mean = (tile_sum(hidden) + dot(total, s.second[...], HIGHEST)) * (1.0 / tiles_each)
    s.pooled[...] = mean
    s.wait("head")
    return dot_nt(mean, s.head[...], HIGHEST)


def pupil_field(alpha, screens, spread, field):
    for m in range(modes):
        spread[m] = jnp.broadcast_to(alpha[:, m : m + 1], (images, side))
    lane = lax.broadcasted_iota(jnp.int32, (images, side), 1) - half
    width = 5

    def rows(block, carry):
        at = [pl.multiple_of((block * width + i) * side, side) for i in range(width)]
        total = [jnp.zeros((images, side), jnp.float32) for _ in range(width)]
        for m in range(modes):
            weight = spread[m]
            for i in range(width):
                total[i] = total[i] + weight * screens[m : m + 1, pl.ds(at[i], side)]
        for i in range(width):
            up = block * width + i - half // 2
            inside = lane * lane + up * up <= (side // 4) ** 2
            field[block * width + i, :, 0:side] = jnp.where(inside, jnp.cos(total[i]), 0.0)
            field[block * width + i, :, side : 2 * side] = jnp.where(inside, jnp.sin(total[i]), 0.0)
        return carry

    lax.fori_loop(0, span // width, rows, 0)
    for i in range(span, pad_span):
        field[i] = jnp.zeros((images, 2 * side), jnp.float32)


def patch_lanes(p):
    return slice(p * frames_here * side, (p + 1) * frames_here * side)


def real_transform(planes, first_table, second_table, s, p, out):
    lanes = patch_lanes(p)
    s.staged[:, lanes] = dot(first_table[...], planes)
    edge = []
    for n in range(p * frames_here, (p + 1) * frames_here):
        lanes = slice(n * side, (n + 1) * side)
        edge.append(jnp.sum(s.staged[0:1, lanes] * alternating(1), axis=1, keepdims=True))
        pair = jnp.concatenate([s.staged[0:side, lanes], s.staged[side : 2 * side, lanes]], axis=1)
        out[n] = dot(pair, second_table[...])
    return edge


def edge_slot(width):
    row = lax.broadcasted_iota(jnp.int32, (8, width), 0)
    lane = lax.broadcasted_iota(jnp.int32, (8, width), 1)
    return jnp.logical_and(row == 0, lane == half)


def frame_spectra(s, t, p):
    here = range(p * frames_here, (p + 1) * frames_here)
    planes = jnp.concatenate([s.img[n] for n in here], axis=1)
    edge = real_transform(planes, t.real, t.swapped, s, p, s.spec)
    for n in here:
        value = edge[n - here[0]] * (1.0 / side)
        s.spec[n, 0:8, :] = jnp.where(edge_slot(2 * side), value, s.spec[n, 0:8, :])


def frame_energy(s):
    for n in range(images):
        s.energy[n : n + 1, :] = jnp.sum(s.img[n] * s.img[n], axis=0, keepdims=True)


def pupil_rows(s, t):
    rowed = dot(s.field[...].reshape(pad_span * images, 2 * side), t.both[...])
    s.rowed_r[...] = rowed[:, 0:side]
    s.rowed_i[...] = rowed[:, side : 2 * side]
    for n in range(images):
        lanes = slice(n * side, (n + 1) * side)
        rows = pl.ds(n, pad_span, stride=images)
        s.stack[0:pad_span, lanes] = s.rowed_r[rows, :]
        s.stack[pad_span : 2 * pad_span, lanes] = s.rowed_i[rows, :]


def spectral_sums(s, t, p):
    lanes = patch_lanes(p)
    s.focal[:, lanes] = dot(t.pupil[...], s.stack[:, lanes])
    fr, fi = s.focal[0:side, lanes], s.focal[side : 2 * side, lanes]
    spot = (fr * fr + fi * fi) * (1.0 / (side * side * aperture_area()))
    edge = real_transform(spot, t.real, t.half_plane, s, p, s.otf)
    real_slot = lax.broadcasted_iota(jnp.int32, (side, side), 1) < half
    at_corner = corner(side)
    t1 = t2 = t3 = 0.0
    for f in range(frames_here):
        n = p * frames_here + f
        s.otf[n, 0:8, :] = jnp.where(edge_slot(side), edge[f], s.otf[n, 0:8, :])
        o, a, b = s.otf[n], s.spec[n, :, 0:side], s.spec[n, :, side : 2 * side]
        t1, t2, t3 = t1 + a * o, t2 + b * o, t3 + o * o
    turned = pltpu.roll(t2, half, 1)
    num = jnp.where(real_slot, t1 + pltpu.roll(t1, half, 1), turned - t2)
    num = jnp.where(at_corner, t1, num)
    den = jnp.where(at_corner, t3, t3 + pltpu.roll(t3, half, 1))
    s.part[p * 16 : (p + 1) * 16, 0:8, :] = num.reshape(16, 8, side)
    s.part[p * 16 : (p + 1) * 16, 8:16, :] = den.reshape(16, 8, side)


def total_of(value):
    return jnp.sum(jnp.sum(value, axis=0, keepdims=True), axis=1, keepdims=True)


def focal_adjoint(s, t, p):
    lane = lax.broadcasted_iota(jnp.int32, (side, side), 1)
    real_slot, at_corner = lane < half, corner(side)
    per_pixel = 1.0 / (side * side)
    weight = jnp.where(lax.rem(lane, half) == 0, per_pixel, 2.0 * per_pixel)
    rho = s.ratio[p * 16 : (p + 1) * 16].reshape(side, side)
    num = s.part[p * 16 : (p + 1) * 16, 0:8, :].reshape(side, side)
    turned = pltpu.roll(rho, half, 1)
    square = rho * rho
    a = jnp.where(jnp.logical_or(real_slot, at_corner), rho, turned) * (-2.0 * weight)
    b = jnp.where(real_slot, turned, -rho)
    b = jnp.where(at_corner, 0.0, b) * (-2.0 * weight)
    m = jnp.where(at_corner, square, square + turned * turned) * (2.0 * weight)
    energy = total_of(s.energy[p * frames_here : (p + 1) * frames_here, :])
    loss = energy * per_pixel - total_of(weight * rho * num)
    for f in range(frames_here):
        n = p * frames_here + f
        lanes = slice(n * side, (n + 1) * side)
        g = a * s.spec[n, :, 0:side] + b * s.spec[n, :, side : 2 * side] + m * s.otf[n]
        y = dot(g, t.half_plane_t[...])
        s.staged[0:side, lanes] = y[:, 0:side]
        s.staged[side : 2 * side, lanes] = y[:, side : 2 * side]
        s.staged[0:1, lanes] = y[0:1, 0:side] + g[0:1, half : half + 1] * alternating(1)
    lanes = patch_lanes(p)
    d_spot = dot(t.real_t[...], s.staged[:, lanes]) * (2.0 / (side * side * aperture_area()))
    d_focal = jnp.concatenate(
        [s.focal[0:side, lanes] * d_spot, s.focal[side : 2 * side, lanes] * d_spot], axis=0
    )
    s.stack[:, lanes] = dot(t.pupil_t[...], d_focal)
    return loss


def alpha_adjoint(s, t):
    screens = s.screens
    for n in range(images):
        lanes = slice(n * side, (n + 1) * side)
        rows = pl.ds(n, pad_span, stride=images)
        s.rowed_r[rows, :] = s.stack[0:pad_span, lanes]
        s.rowed_i[rows, :] = s.stack[pad_span : 2 * pad_span, lanes]
    rowed = jnp.concatenate([s.rowed_r[...], s.rowed_i[...]], axis=1)
    d_field = dot(rowed, t.both_t[...]).reshape(pad_span, images, 2 * side)
    f_r, f_i = s.field[:, :, 0:side], s.field[:, :, side : 2 * side]
    s.phase[...] = d_field[:, :, side : 2 * side] * f_r - d_field[:, :, 0:side] * f_i

    alpha_lane = lax.broadcasted_iota(jnp.int32, (images, side), 1)
    d_alpha = jnp.zeros((images, side), jnp.float32)
    chunk = 11
    for start in range(0, modes, chunk):

        def rows(i, total, start=start):
            value = s.phase[i]
            at = pl.multiple_of(i * side, side)
            return tuple(
                total[m] + value * screens[start + m : start + m + 1, pl.ds(at, side)]
                for m in range(chunk)
            )

        zero = tuple(jnp.zeros((images, side), jnp.float32) for _ in range(chunk))
        total = lax.fori_loop(0, span, rows, zero)
        for m in range(chunk):
            d_alpha = jnp.where(
                alpha_lane == start + m, jnp.sum(total[m], axis=1, keepdims=True), d_alpha
            )
    return d_alpha


def spread(value):
    return jnp.broadcast_to(value[:, None, :], (images, tiles_each, 256)).reshape(-1, 256)


def gradients_after_mean(s, d_alpha):
    s.grad_tail[...] = dot_tn(d_alpha, s.pooled[...])
    d_pooled = dot(d_alpha[:, 0:modes], s.head[...]) * (1.0 / tiles_each)
    s.grad_second[...] = dot_tn(s.inner_sum[...], d_pooled)
    return d_pooled


def gradient_first(s, d_pooled):
    d_inner = spread(dot_nt(d_pooled, s.second[...])) * silu_slope(s.inn_pre[...])
    s.grad_first[...] = dot_tn(silu_act(s.hid_pre[...]), d_inner)
    return d_inner


def gradient_embed(s, d_pooled, d_inner):
    d_hidden = spread(d_pooled) + dot_nt(d_inner, s.first[...])
    s.grad_embed[...] = dot_tn(s.tiles[...], d_hidden * silu_slope(s.hid_pre[...]))


state_shapes = dict(
    tiles=(images * tiles_each, 256),
    hid_pre=(images * tiles_each, 256),
    inn_pre=(images * tiles_each, 256),
    inner_sum=(images, 256),
    pooled=(images, 256),
    energy=(images, side),
    spread=(modes, images, side),
    field=(pad_span, images, 2 * side),
    rowed_r=(pad_span * images, side),
    rowed_i=(pad_span * images, side),
    stack=(2 * pad_span, images * side),
    focal=(2 * side, images * side),
    staged=(2 * side, images * side),
    spec=(images, side, 2 * side),
    otf=(images, side, side),
    part=(32, 16, side),
    core_part=(16, 16, side),
    merged=(16, 16, side),
    inbox=(15, 16, side),
    ratio=(32, 8, side),
    phase=(pad_span, images, side),
    screens=(modes, span * side),
    img=(images, side, side),
    embed=(256, 256),
    first=(256, 256),
    second=(256, 256),
    head=(modes, 256),
    tables=(1680, 256),
)
gradient_shapes = dict(
    grad_embed=(256, 256), grad_first=(256, 256), grad_second=(256, 256), grad_tail=(128, 256)
)


def ring_distance(step, size):
    return min(step, size - step)


plane_steps = sorted(
    ((dx, dy) for dx in range(4) for dy in range(4) if dx or dy),
    key=lambda d: ring_distance(d[0], 4) + ring_distance(d[1], 4),
)
burst_steps = sorted(
    ((dx, dz) for dx in range(4) for dz in range(4) if dx or dz),
    key=lambda d: ring_distance(d[0], 4) + 2 * ring_distance(d[1], 4),
)
column_steps = sorted(range(1, 8), key=lambda d: ring_distance(d, 8))


class Place:
    def __init__(self):
        self.dp, self.frame = lax.axis_index("dp"), lax.axis_index("frame")
        self.core, self.x = lax.rem(self.frame, 2), lax.rem(self.frame // 2, 4)
        self.y, self.z_lo = self.dp // 2, lax.rem(self.dp, 2)
        self.z_hi = self.frame // 8
        self.z = self.z_hi * 2 + self.z_lo
        self.spot = self.x * 4 + self.y
        self.seat = self.z_hi * 4 + self.x

    def device(self, core, x, y, z):
        return {"dp": y * 2 + lax.rem(z, 2), "frame": (z // 2) * 8 + x * 2 + core}

    def sibling(self):
        return self.device(1 - self.core, self.x, self.y, self.z)

    def plane(self, step, sign=1):
        x = lax.rem(self.x + 4 + sign * step[0], 4)
        y = lax.rem(self.y + 4 + sign * step[1], 4)
        return x * 4 + y, self.device(self.core, x, y, self.z)

    def burst(self, step, sign=1):
        x = lax.rem(self.x + 4 + sign * step[0], 4)
        z_hi = lax.rem(self.z_hi + 4 + sign * step[1], 4)
        return z_hi * 4 + x, self.device(self.core, x, self.y, z_hi * 2 + self.z_lo)

    def column(self, step):
        return self.device(self.core, self.x, self.y, lax.rem(self.z + step, 8))


def greet():
    place = Place()
    targets = [place.sibling()]
    targets += [place.burst(step)[1] for step in burst_steps]
    targets += [place.plane(step)[1] for step in plane_steps if step[1]]
    targets += [place.column(step) for step in column_steps if step % 2]
    for target in targets:
        pl.semaphore_signal(
            pltpu.get_barrier_semaphore(), inc=1, device_id=target, device_id_type=MESH
        )
    return len(targets)


class Mail:
    def __init__(self, sems):
        self.sems, self.used, self.sent = sems, 0, []

    def send(self, src, dst, target):
        slot = self.used
        self.used += 1
        copy = pltpu.make_async_remote_copy(
            src_ref=src,
            dst_ref=dst,
            send_sem=self.sems.at[0, slot],
            recv_sem=self.sems.at[1, slot],
            device_id=target,
            device_id_type=MESH,
        )
        copy.start()
        self.sent.append(copy)
        return copy

    def finish(self):
        for copy in self.sent:
            copy.wait_send()


def spectral_exchange(s, regularizer_strength, sems):
    place, mail = Place(), Mail(sems)
    core, seat = place.core, place.seat
    swap = mail.send(s.part.at[pl.ds((1 - core) * 16, 16)], s.core_part, place.sibling())
    swap.wait_recv()
    s.merged[...] = s.part[pl.ds(core * 16, 16)] + s.core_part[...]
    copies = {}
    for i, step in reversed(list(enumerate(burst_steps))):
        there, device = place.burst(step)
        copies[i] = mail.send(s.merged.at[there], s.inbox.at[i], device)
    total = s.merged[seat]
    for i in range(len(burst_steps)):
        copies[i].wait_recv()
        total = total + s.inbox[i]
    mine = core * 16 + seat
    s.ratio[mine] = total[0:8] / (total[8:16] + regularizer_strength)
    copies = {}
    for i, step in reversed(list(enumerate(burst_steps))):
        copies[i] = mail.send(s.ratio.at[mine], s.ratio.at[mine], place.burst(step)[1])
    passed = [mail.send(s.ratio.at[mine], s.ratio.at[mine], place.sibling())]
    for i, step in enumerate(burst_steps):
        copies[i].wait_recv()
        came = core * 16 + place.burst(step, -1)[0]
        passed.append(mail.send(s.ratio.at[came], s.ratio.at[came], place.sibling()))
    for copy in passed:
        copy.wait_recv()
    mail.finish()


class GradientGroup:
    def __init__(self, parts, buffers, sems):
        self.parts = parts
        self.core_in, self.sums, self.inbox, self.column_in, self.full, self.other = buffers
        self.place, self.mail = Place(), Mail(sems)
        core = self.place.core
        self.mine = pl.ds(pl.multiple_of(core * side, side), side)
        self.theirs = pl.ds(pl.multiple_of((1 - core) * side, side), side)
        self.swaps = []

    def send_core(self, part):
        ref, at = self.parts[part]
        rows = ref.shape[0]
        self.swaps.append(
            self.mail.send(
                ref.at[:, self.theirs], self.core_in.at[at : at + rows], self.place.sibling()
            )
        )

    def send_plane(self):
        row = 0
        for swap, (ref, at) in zip(self.swaps, self.parts):
            swap.wait_recv()
            rows = ref.shape[0]
            total = ref[:, self.mine] + self.core_in[at : at + rows]
            each = rows // 16
            self.sums[:, row : row + each, :] = total.reshape(16, each, side)
            row += each
        self.copies = {}
        for i, step in reversed(list(enumerate(plane_steps))):
            there, device = self.place.plane(step)
            self.copies[i] = self.mail.send(self.sums.at[there], self.inbox.at[i], device)

    def send_column(self):
        total = self.sums[self.place.spot]
        for i in range(len(plane_steps)):
            self.copies[i].wait_recv()
            total = total + self.inbox[i]
        z = self.place.z
        self.column_in[z] = total
        self.copies = [
            self.mail.send(self.column_in.at[z], self.column_in.at[z], self.place.column(step))
            for step in reversed(column_steps)
        ]

    def send_back(self):
        for copy in self.copies:
            copy.wait_recv()
        total = self.column_in[0]
        for z in range(1, 8):
            total = total + self.column_in[z]
        spot = self.place.spot
        self.full[spot] = total
        self.copies = {}
        for i, step in reversed(list(enumerate(plane_steps))):
            device = self.place.plane(step)[1]
            self.copies[i] = self.mail.send(self.full.at[spot], self.full.at[spot], device)
        self.passed = [
            self.mail.send(self.full.at[spot], self.other.at[spot], self.place.sibling())
        ]

    def pass_on(self):
        for i, step in enumerate(plane_steps):
            self.copies[i].wait_recv()
            came = self.place.plane(step, -1)[0]
            self.passed.append(
                self.mail.send(self.full.at[came], self.other.at[came], self.place.sibling())
            )

    def finish(self, outs):
        for copy in self.passed:
            copy.wait_recv()
        row = 0
        for (ref, _), out in zip(self.parts, outs):
            each = ref.shape[0] // 16
            for values, lanes in ((self.full, self.mine), (self.other, self.theirs)):
                out[:, lanes] = values[:, row : row + each, :].reshape(16 * each, side)
            row += each
        self.mail.finish()


def group_buffers(rows):
    each = rows // 16
    return [
        (rows, side), (16, each, side), (15, each, side), (8, each, side), (16, each, side),
        (16, each, side),
    ]


operands = ("img", "embed", "first", "second", "head", "tables", "screens")
early_rows = (256, 128)
late_rows = (256, 256)


def kernel(names, frames_total, *refs):
    sources, (alpha_ref, loss_ref, total_ref), scratch = refs[:7], refs[7:10], refs[10:]
    s = types.SimpleNamespace(**dict(zip(names, scratch)))
    buffers = scratch[len(names) : -4]
    fetch_sems, spectral_sems, early_sems, late_sems = scratch[-4:]
    fetches = {}
    for i, name in enumerate(operands):
        source = sources[i]
        if name == "screens":
            source = source.at[:, pl.ds(half // 2 * side, span * side)]
        fetches[name] = pltpu.make_async_copy(source, getattr(s, name), fetch_sems.at[i])
        fetches[name].start()
    s.wait = lambda name: fetches[name].wait()
    greeted = greet()
    t = split_tables(s.tables)

    s.wait("img")
    cut_tiles(s.img, s.tiles)
    alpha = encode(s)
    s.wait("screens")
    pupil_field(alpha, s.screens, s.spread, s.field)
    s.wait("tables")
    pupil_rows(s, t)
    patches = range(images // frames_here)
    for p in patches:
        frame_spectra(s, t, p)
        spectral_sums(s, t, p)
    frame_energy(s)
    pl.semaphore_wait(pltpu.get_barrier_semaphore(), greeted)
    spectral_exchange(s, regularizer_relative * frames_total, spectral_sems)
    losses = [focal_adjoint(s, t, p) for p in patches]
    d_alpha = alpha_adjoint(s, t)
    alpha_ref[...] = d_alpha

    early = GradientGroup(((s.grad_second, 0), (s.grad_tail, 256)), buffers[:6], early_sems)
    late = GradientGroup(((s.grad_first, 0), (s.grad_embed, 256)), buffers[6:], late_sems)
    d_pooled = gradients_after_mean(s, d_alpha)
    lane = lax.broadcasted_iota(jnp.int32, (1, side), 1)
    row = jnp.zeros((1, side), jnp.float32)
    for p in patches:
        at = lax.axis_index("dp") * len(patches) + p
        row = jnp.where(lane == at, losses[p], row)
    s.grad_tail[loss_row : loss_row + 1, 0:side] = row
    early.send_core(0)
    early.send_core(1)
    d_inner = gradient_first(s, d_pooled)
    late.send_core(0)
    early.send_plane()
    gradient_embed(s, d_pooled, d_inner)
    late.send_core(1)
    late.send_plane()
    early.send_column()
    late.send_column()
    early.send_back()
    late.send_back()
    early.pass_on()
    late.pass_on()
    early.finish((total_ref.at[512:768], total_ref.at[768:896]))
    late.finish((total_ref.at[256:512], total_ref.at[0:256]))
    at = 768 + loss_row
    loss_ref[...] = total_ref[at : at + 1, 0:side] * (1.0 / frames_total)


def hand_out(
    alpha_ref, loss_ref, total_ref, embed_ref, first_ref, second_ref, head_ref, out_alpha_ref,
    out_loss_ref, head, alpha, loss, sems,
):
    outs = (embed_ref, first_ref, second_ref)
    copies = [
        pltpu.make_async_copy(total_ref.at[256 * i : 256 * (i + 1)], out, sems.at[i])
        for i, out in enumerate(outs)
    ]
    for copy in copies:
        copy.start()
    head[...] = total_ref[768 : 768 + modes, :]
    regions = alpha.shape[0]
    lane = lax.broadcasted_iota(jnp.int32, (1, side), 1)
    at = lax.axis_index("dp") * regions
    for p in range(regions):
        alpha[p] = alpha_ref[p * frames_here : (p + 1) * frames_here, 0:modes]
        one = jnp.where(lane == at + p, loss_ref[...], 0.0)
        loss[:, p : p + 1] = jnp.sum(one, axis=1, keepdims=True)
    small = ((head, head_ref), (alpha, out_alpha_ref), (loss, out_loss_ref))
    for i, (src, dst) in enumerate(small):
        copies.append(pltpu.make_async_copy(src, dst, sems.at[3 + i]))
        copies[-1].start()
    for copy in copies:
        copy.wait()


def local(recorded_exposures, screens, embed, first, second, head):
    regions = recorded_exposures.shape[0]
    frames_total = recorded_exposures.shape[1] * lax.axis_size("frame")
    f32 = jnp.float32
    names = list(state_shapes) + list(gradient_shapes)
    shapes = list(state_shapes.values()) + list(gradient_shapes.values())
    shapes += group_buffers(sum(early_rows)) + group_buffers(sum(late_rows))
    vmem = pl.BlockSpec(memory_space=pltpu.VMEM)
    d_alpha, losses, total = pl.pallas_call(
        functools.partial(kernel, names, frames_total),
        out_shape=[
            jax.ShapeDtypeStruct((images, side), f32),
            jax.ShapeDtypeStruct((1, side), f32),
            jax.ShapeDtypeStruct((896, 2 * side), f32),
        ],
        in_specs=[pl.BlockSpec(memory_space=pltpu.HBM)] * len(operands),
        out_specs=[vmem] * 3,
        scratch_shapes=[pltpu.VMEM(shape, f32) for shape in shapes]
        + [pltpu.SemaphoreType.DMA((len(operands),))]
        + [pltpu.SemaphoreType.DMA((2, 64))] * 3,
        compiler_params=pltpu.CompilerParams(
            collective_id=0, has_side_effects=True, vmem_limit_bytes=40 << 20
        ),
    )(
        *(
            pltpu.with_memory_space_constraint(operand, pltpu.HBM)
            for operand in (
                recorded_exposures.reshape(images, side, side),
                embed, first, second, head.T, jnp.asarray(transform_tables()), screens,
            )
        )
    )
    out = pl.pallas_call(
        hand_out,
        out_shape=[jax.ShapeDtypeStruct((256, 256), f32)] * 3
        + [
            jax.ShapeDtypeStruct((modes, 256), f32),
            jax.ShapeDtypeStruct((regions, frames_here, modes), f32),
            jax.ShapeDtypeStruct((1, regions), f32),
        ],
        in_specs=[vmem] * 3,
        out_specs=[pl.BlockSpec(memory_space=pltpu.HBM)] * 6,
        scratch_shapes=[
            pltpu.VMEM((modes, 256), f32),
            pltpu.VMEM((regions, frames_here, modes), f32),
            pltpu.VMEM((1, regions), f32),
            pltpu.SemaphoreType.DMA((6,)),
        ],
    )(d_alpha, losses, total)
    return (out[4], out[0], out[1], out[2], out[3].T, out[5].reshape(regions))


def solution(mesh):
    return jax.shard_map(
        local,
        mesh=mesh,
        in_specs=(P("dp", "frame", None, None), P(), P(), P(), P(), P()),
        out_specs=(P("dp", "frame", None), P(), P(), P(), P(), P("dp")),
        check_vma=False,
    )
```

```python
import functools
import math
import types

import jax
import jax.numpy as jnp
import numpy as np
from jax import lax
from jax.experimental import pallas as pl
from jax.experimental.pallas import tpu as pltpu
from jax.sharding import PartitionSpec as P

entry_block_length = 16
regularizer_relative = 0.001
MESH = pl.DeviceIdType.MESH
HIGH = lax.Precision.HIGH
HIGHEST = lax.Precision.HIGHEST
side = 128
half = side // 2
span = half + 1
pad_span = 72
images = 8
frames_here = 4
modes = 44
tiles_each = 64
loss_row = 44


def dot(a, b, precision=HIGH):
    return jnp.dot(a, b, precision=precision, preferred_element_type=jnp.float32)


def dot_tn(a, b, precision=HIGH):
    return lax.dot_general(
        a, b, (((0,), (0,)), ((), ())), precision=precision, preferred_element_type=jnp.float32
    )


def dot_nt(a, b, precision=HIGH):
    return lax.dot_general(
        a, b, (((1,), (1,)), ((), ())), precision=precision, preferred_element_type=jnp.float32
    )


def transform_tables():
    index = np.arange(side)
    angle = 2.0 * np.pi / side * (index[:, None] * index[None, :] % side)
    c, s = np.cos(angle), np.sin(angle)
    both = np.block([[c, -s], [s, c]])
    lo = slice(0, half)
    half_plane = np.concatenate([both[:, lo], both[:, side : side + half]], axis=1)
    swapped = np.concatenate([half_plane, half_plane[:, half:], half_plane[:, :half]], axis=1)
    rows = slice(half // 2, half // 2 + span)
    pupil = np.zeros((2 * side, 2 * pad_span))
    pupil[:side, :span], pupil[:side, pad_span : pad_span + span] = c[:, rows], s[:, rows]
    pupil[side:, :span], pupil[side:, pad_span : pad_span + span] = -s[:, rows], c[:, rows]
    real = np.concatenate([c, -s], axis=0)
    narrow = np.concatenate([real, half_plane], axis=1)
    pupil_wide = np.concatenate([pupil, np.zeros((2 * side, 2 * side - 2 * pad_span))], axis=1)
    tables = (swapped / side, narrow, both, pupil_wide, both.T, pupil.T, real.T, half_plane.T)
    return np.concatenate(tables).astype(np.float32)


def split_tables(ref):
    sizes = (256, 256, 256, 256, 256, 2 * pad_span, side, side)
    views, at = [], 0
    for size in sizes:
        views.append(ref.at[at : at + size])
        at += size
    swapped, narrow, both, pupil, both_t, pupil_t, real_t, half_plane_t = views
    return types.SimpleNamespace(
        swapped=swapped, real=narrow.at[:, 0:side], half_plane=narrow.at[:, side:], both=both,
        pupil=pupil.at[:, 0 : 2 * pad_span], both_t=both_t, pupil_t=pupil_t, real_t=real_t,
        half_plane_t=half_plane_t,
    )


def aperture_area():
    at = np.arange(side) - half
    return float(np.sum(at[:, None] ** 2 + at[None, :] ** 2 <= (side // 4) ** 2))


def sigmoid(value):
    return 1.0 / (1.0 + jnp.exp(-value))


def silu_act(value):
    return value / (1.0 + jnp.exp(-value))


def silu_slope(value):
    gate = sigmoid(value)
    return gate * (1.0 + value * (1.0 - gate))


def alternating(rows):
    lane = lax.broadcasted_iota(jnp.int32, (rows, side), 1)
    return jnp.where(lax.rem(lane, 2) == 0, 1.0, -1.0).astype(jnp.float32)


def corner(rows):
    row = lax.broadcasted_iota(jnp.int32, (rows, side), 0)
    lane = lax.broadcasted_iota(jnp.int32, (rows, side), 1)
    return jnp.logical_and(row == 0, lax.rem(lane, half) == 0)


def cut_tiles(img, tiles):
    group = lax.broadcasted_iota(jnp.int32, (8, side), 1) // 16
    for n in range(images):
        for g in range(2):
            x = [img[n, pl.ds(8 * g + j, 8, stride=16), :] for j in range(8)]
            for bit in (1, 2, 4):
                low = lax.rem(group // bit, 2) == 0
                y = list(x)
                for p in range(8):
                    if p & bit == 0:
                        q = p + bit
                        y[p] = jnp.where(low, x[p], pltpu.roll(x[q], 16 * bit, 1))
                        y[q] = jnp.where(low, pltpu.roll(x[p], side - 16 * bit, 1), x[q])
                x = y
            for c in range(8):
                row = n * tiles_each + c * 8
                tiles[row : row + 8, g * side : (g + 1) * side] = x[c]


def tile_sum(value):
    return jnp.sum(value.reshape(images, tiles_each, value.shape[1]), axis=1)


def encode(s):
    s.wait("embed")
    pre = dot(s.tiles[...], s.embed[...], HIGHEST)
    s.hid_pre[...] = pre
    hidden = silu_act(pre)
    s.wait("first")
    pre = dot(hidden, s.first[...], HIGHEST)
    s.inn_pre[...] = pre
    total = tile_sum(silu_act(pre))
    s.inner_sum[...] = total
    s.wait("second")
    mean = (tile_sum(hidden) + dot(total, s.second[...], HIGHEST)) * (1.0 / tiles_each)
    s.pooled[...] = mean
    s.wait("head")
    return dot_nt(mean, s.head[...], HIGHEST)


def chop(value, bits):
    mantissa, exponent = math.frexp(value)
    return math.ldexp(math.floor(mantissa * 2**bits), exponent - bits)


def pieces(value, bits, number):
    out = []
    for _ in range(number - 1):
        out.append(chop(value, bits))
        value -= out[-1]
    return out + [value]


def cos_sin(x):
    turns = jnp.round(x * (1.0 / (512.0 * math.pi)))
    for piece in pieces(512.0 * math.pi, 8, 4):
        x = x - turns * piece
    quarter = jnp.round(x * (2.0 / math.pi))
    for piece in pieces(0.5 * math.pi, 12, 3):
        x = x - quarter * piece
    z = x * x
    sin = x + x * z * (-1.6666654611e-1 + z * (8.3321608736e-3 + z * -1.9515295891e-4))
    cos = 1.0 - 0.5 * z + z * z * (4.166664568298827e-2 + z * (-1.388731625493765e-3 + z * 2.443315711809948e-5))
    quadrant = quarter.astype(jnp.int32)
    odd = (quadrant & 1) != 0
    cos, sin = jnp.where(odd, sin, cos), jnp.where(odd, cos, sin)
    cos = jnp.where(((quadrant + 1) & 2) != 0, -cos, cos)
    sin = jnp.where((quadrant & 2) != 0, -sin, sin)
    return cos, sin


def pupil_field(alpha, screens, spread, field):
    for m in range(modes):
        spread[m] = jnp.broadcast_to(alpha[:, m : m + 1], (images, side))
    lane = lax.broadcasted_iota(jnp.int32, (images, side), 1) - half
    width = 13

    def rows(block, carry):
        at = [pl.multiple_of((block * width + i) * side, side) for i in range(width)]
        total = [jnp.zeros((images, side), jnp.float32) for _ in range(width)]
        for m in range(modes):
            weight = spread[m]
            for i in range(width):
                total[i] = total[i] + weight * screens[m : m + 1, pl.ds(at[i], side)]
        for i in range(width):
            up = block * width + i - half // 2
            inside = lane * lane + up * up <= (side // 4) ** 2
            cos, sin = cos_sin(total[i])
            at = pl.ds(pl.multiple_of((block * width + i) * images, images), images)
            field[at, 0:side] = jnp.where(inside, cos, 0.0)
            field[at, side : 2 * side] = jnp.where(inside, sin, 0.0)
        return carry

    lax.fori_loop(0, span // width, rows, 0)
    field[span * images :, :] = jnp.zeros(((pad_span - span) * images, 2 * side), jnp.float32)


def patch_lanes(p):
    return slice(p * frames_here * side, (p + 1) * frames_here * side)


def real_transform(planes, first_table, second_table, s, p, out):
    lanes = patch_lanes(p)
    s.staged[:, lanes] = dot(first_table[...], planes)
    edge = []
    for n in range(p * frames_here, (p + 1) * frames_here):
        lanes = slice(n * side, (n + 1) * side)
        edge.append(jnp.sum(s.staged[0:1, lanes] * alternating(1), axis=1, keepdims=True))
        pair = jnp.concatenate([s.staged[0:side, lanes], s.staged[side : 2 * side, lanes]], axis=1)
        out[n] = dot(pair, second_table[...])
    return edge


def edge_slot(width):
    row = lax.broadcasted_iota(jnp.int32, (8, width), 0)
    lane = lax.broadcasted_iota(jnp.int32, (8, width), 1)
    return jnp.logical_and(row == 0, lane == half)


def frame_spectra(s, t, p):
    here = range(p * frames_here, (p + 1) * frames_here)
    planes = jnp.concatenate([s.img[n] for n in here], axis=1)
    edge = real_transform(planes, t.real, t.swapped, s, p, s.spec)
    for n in here:
        value = edge[n - here[0]] * (1.0 / side)
        s.spec[n, 0:8, :] = jnp.where(edge_slot(2 * side), value, s.spec[n, 0:8, :])


def prepare_backward(s):
    for n in range(images):
        s.energy[n : n + 1, :] = jnp.sum(s.img[n] * s.img[n], axis=0, keepdims=True)
    s.tiles_t[...] = s.tiles[...].T
    s.hidden_t[...] = silu_act(s.hid_pre[...]).T
    s.hid_pre[...] = silu_slope(s.hid_pre[...])
    s.inn_pre[...] = silu_slope(s.inn_pre[...])


def pupil_rows(s, t):
    rowed = dot(s.field[...], t.both[...])
    s.rowed_r[...] = rowed[:, 0:side]
    s.rowed_i[...] = rowed[:, side : 2 * side]
    for n in range(images):
        lanes = slice(n * side, (n + 1) * side)
        rows = pl.ds(n, pad_span, stride=images)
        s.stack[0:pad_span, lanes] = s.rowed_r[rows, :]
        s.stack[pad_span : 2 * pad_span, lanes] = s.rowed_i[rows, :]


def spectral_sums(s, t, p):
    lanes = patch_lanes(p)
    s.focal[:, lanes] = dot(t.pupil[...], s.stack[:, lanes])
    fr, fi = s.focal[0:side, lanes], s.focal[side : 2 * side, lanes]
    spot = (fr * fr + fi * fi) * (1.0 / (side * side * aperture_area()))
    edge = real_transform(spot, t.real, t.half_plane, s, p, s.otf)
    real_slot = lax.broadcasted_iota(jnp.int32, (side, side), 1) < half
    at_corner = corner(side)
    t1 = t2 = t3 = 0.0
    for f in range(frames_here):
        n = p * frames_here + f
        s.otf[n, 0:8, :] = jnp.where(edge_slot(side), edge[f], s.otf[n, 0:8, :])
        o, a, b = s.otf[n], s.spec[n, :, 0:side], s.spec[n, :, side : 2 * side]
        t1, t2, t3 = t1 + a * o, t2 + b * o, t3 + o * o
    turned = pltpu.roll(t2, half, 1)
    num = jnp.where(real_slot, t1 + pltpu.roll(t1, half, 1), turned - t2)
    num = jnp.where(at_corner, t1, num)
    den = jnp.where(at_corner, t3, t3 + pltpu.roll(t3, half, 1))
    s.part[p * 16 : (p + 1) * 16, 0:8, :] = num.reshape(16, 8, side)
    s.part[p * 16 : (p + 1) * 16, 8:16, :] = den.reshape(16, 8, side)


def total_of(value):
    return jnp.sum(jnp.sum(value, axis=0, keepdims=True), axis=1, keepdims=True)


def focal_adjoint(s, t, p):
    lane = lax.broadcasted_iota(jnp.int32, (side, side), 1)
    real_slot, at_corner = lane < half, corner(side)
    per_pixel = 1.0 / (side * side)
    weight = jnp.where(lax.rem(lane, half) == 0, per_pixel, 2.0 * per_pixel)
    rho = s.ratio[p * 16 : (p + 1) * 16].reshape(side, side)
    num = s.part[p * 16 : (p + 1) * 16, 0:8, :].reshape(side, side)
    turned = pltpu.roll(rho, half, 1)
    square = rho * rho
    a = jnp.where(jnp.logical_or(real_slot, at_corner), rho, turned) * (-2.0 * weight)
    b = jnp.where(real_slot, turned, -rho)
    b = jnp.where(at_corner, 0.0, b) * (-2.0 * weight)
    m = jnp.where(at_corner, square, square + turned * turned) * (2.0 * weight)
    energy = total_of(s.energy[p * frames_here : (p + 1) * frames_here, :])
    loss = energy * per_pixel - total_of(weight * rho * num)
    for f in range(frames_here):
        n = p * frames_here + f
        lanes = slice(n * side, (n + 1) * side)
        g = a * s.spec[n, :, 0:side] + b * s.spec[n, :, side : 2 * side] + m * s.otf[n]
        y = dot(g, t.half_plane_t[...])
        s.staged[0:side, lanes] = y[:, 0:side]
        s.staged[side : 2 * side, lanes] = y[:, side : 2 * side]
        s.staged[0:1, lanes] = y[0:1, 0:side] + g[0:1, half : half + 1] * alternating(1)
    lanes = patch_lanes(p)
    d_spot = dot(t.real_t[...], s.staged[:, lanes]) * (2.0 / (side * side * aperture_area()))
    d_focal = jnp.concatenate(
        [s.focal[0:side, lanes] * d_spot, s.focal[side : 2 * side, lanes] * d_spot], axis=0
    )
    s.stack[:, lanes] = dot(t.pupil_t[...], d_focal)
    return loss


def alpha_adjoint(s, t):
    for n in range(images):
        lanes = slice(n * side, (n + 1) * side)
        rows = pl.ds(n, pad_span, stride=images)
        s.rowed_r[rows, :] = s.stack[0:pad_span, lanes]
        s.rowed_i[rows, :] = s.stack[pad_span : 2 * pad_span, lanes]
    rowed = jnp.concatenate([s.rowed_r[...], s.rowed_i[...]], axis=1)
    d_field = dot(rowed, t.both_t[...])
    f_r, f_i = s.field[:, 0:side], s.field[:, side : 2 * side]
    phase = d_field[:, side : 2 * side] * f_r - d_field[:, 0:side] * f_i

    phase = jnp.concatenate([phase[i * images : (i + 1) * images] for i in range(span)], axis=1)
    return dot_nt(s.screens[...], phase)


def spread(value):
    return jnp.broadcast_to(value[:, None, :], (images, tiles_each, 256)).reshape(-1, 256)


def gradients_after_mean(s, d_alpha):
    s.grad_tail[0:modes, :] = dot(d_alpha, s.pooled[...])
    d_pooled = dot_tn(d_alpha, s.head[...]) * (1.0 / tiles_each)
    s.grad_second[...] = dot_tn(s.inner_sum[...], d_pooled)
    return d_pooled


def gradient_first(s, d_pooled):
    d_inner = spread(dot_nt(d_pooled, s.second[...])) * s.inn_pre[...]
    s.grad_first[...] = dot(s.hidden_t[...], d_inner)
    return d_inner


def gradient_embed(s, d_pooled, d_inner):
    d_hidden = spread(d_pooled) + dot_nt(d_inner, s.first[...])
    s.grad_embed[...] = dot(s.tiles_t[...], d_hidden * s.hid_pre[...])


state_shapes = dict(
    tiles=(images * tiles_each, 256),
    hid_pre=(images * tiles_each, 256),
    inn_pre=(images * tiles_each, 256),
    tiles_t=(256, images * tiles_each),
    hidden_t=(256, images * tiles_each),
    inner_sum=(images, 256),
    pooled=(images, 256),
    energy=(images, side),
    spread=(modes, images, side),
    field=(pad_span * images, 2 * side),
    rowed_r=(pad_span * images, side),
    rowed_i=(pad_span * images, side),
    stack=(2 * pad_span, images * side),
    focal=(2 * side, images * side),
    staged=(2 * side, images * side),
    spec=(images, side, 2 * side),
    otf=(images, side, side),
    part=(32, 16, side),
    core_part=(16, 16, side),
    merged=(16, 16, side),
    inbox=(15, 16, side),
    ratio=(32, 8, side),
    screens=(modes, span * side),
    img=(images, side, side),
    embed=(256, 256),
    first=(256, 256),
    second=(256, 256),
    head=(modes, 256),
    tables=(1680, 256),
)
gradient_shapes = dict(
    grad_embed=(256, 256), grad_first=(256, 256), grad_second=(256, 256), grad_tail=(128, 256)
)


def ring_distance(step, size):
    return min(step, size - step)


plane_steps = sorted(
    ((dx, dy) for dx in range(4) for dy in range(4) if dx or dy),
    key=lambda d: ring_distance(d[0], 4) + ring_distance(d[1], 4),
)
burst_steps = sorted(
    ((dx, dz) for dx in range(4) for dz in range(4) if dx or dz),
    key=lambda d: ring_distance(d[0], 4) + 2 * ring_distance(d[1], 4),
)
column_steps = sorted(range(1, 8), key=lambda d: ring_distance(d, 8))


class Place:
    def __init__(self):
        self.dp, self.frame = lax.axis_index("dp"), lax.axis_index("frame")
        self.core, self.x = lax.rem(self.frame, 2), lax.rem(self.frame // 2, 4)
        self.y, self.z_lo = self.dp // 2, lax.rem(self.dp, 2)
        self.z_hi = self.frame // 8
        self.z = self.z_hi * 2 + self.z_lo
        self.spot = self.x * 4 + self.y
        self.seat = self.z_hi * 4 + self.x

    def device(self, core, x, y, z):
        return {"dp": y * 2 + lax.rem(z, 2), "frame": (z // 2) * 8 + x * 2 + core}

    def sibling(self):
        return self.device(1 - self.core, self.x, self.y, self.z)

    def plane(self, step, sign=1):
        x = lax.rem(self.x + 4 + sign * step[0], 4)
        y = lax.rem(self.y + 4 + sign * step[1], 4)
        return x * 4 + y, self.device(self.core, x, y, self.z)

    def burst(self, step, sign=1):
        x = lax.rem(self.x + 4 + sign * step[0], 4)
        z_hi = lax.rem(self.z_hi + 4 + sign * step[1], 4)
        return z_hi * 4 + x, self.device(self.core, x, self.y, z_hi * 2 + self.z_lo)

    def column(self, step):
        return self.device(self.core, self.x, self.y, lax.rem(self.z + step, 8))


def greet():
    place = Place()
    targets = [place.sibling()]
    targets += [place.burst(step)[1] for step in burst_steps]
    targets += [place.plane(step)[1] for step in plane_steps if step[1]]
    targets += [place.column(step) for step in column_steps if step % 2]
    for target in targets:
        pl.semaphore_signal(
            pltpu.get_barrier_semaphore(), inc=1, device_id=target, device_id_type=MESH
        )
    return len(targets)


class Mail:
    def __init__(self, sems):
        self.sems, self.used, self.sent = sems, 0, []

    def send(self, src, dst, target):
        slot = self.used
        self.used += 1
        copy = pltpu.make_async_remote_copy(
            src_ref=src,
            dst_ref=dst,
            send_sem=self.sems.at[0, slot],
            recv_sem=self.sems.at[1, slot],
            device_id=target,
            device_id_type=MESH,
        )
        copy.start()
        self.sent.append(copy)
        return copy

    def finish(self):
        for copy in self.sent:
            copy.wait_send()


def spectral_exchange(s, regularizer_strength, sems, meanwhile):
    place, mail = Place(), Mail(sems)
    core, seat = place.core, place.seat
    swap = mail.send(s.part.at[pl.ds((1 - core) * 16, 16)], s.core_part, place.sibling())
    swap.wait_recv()
    s.merged[...] = s.part[pl.ds(core * 16, 16)] + s.core_part[...]
    copies = {}
    for i, step in reversed(list(enumerate(burst_steps))):
        there, device = place.burst(step)
        copies[i] = mail.send(s.merged.at[there], s.inbox.at[i], device)
    meanwhile()
    total = s.merged[seat]
    for i in range(len(burst_steps)):
        copies[i].wait_recv()
        total = total + s.inbox[i]
    mine = core * 16 + seat
    s.ratio[mine] = total[0:8] / (total[8:16] + regularizer_strength)
    copies = {}
    for i, step in reversed(list(enumerate(burst_steps))):
        copies[i] = mail.send(s.ratio.at[mine], s.ratio.at[mine], place.burst(step)[1])
    passed = [mail.send(s.ratio.at[mine], s.ratio.at[mine], place.sibling())]
    for i, step in enumerate(burst_steps):
        copies[i].wait_recv()
        came = core * 16 + place.burst(step, -1)[0]
        passed.append(mail.send(s.ratio.at[came], s.ratio.at[came], place.sibling()))
    for copy in passed:
        copy.wait_recv()
    mail.finish()


class GradientGroup:
    def __init__(self, parts, buffers, sems):
        self.parts = parts
        self.core_in, self.sums, self.inbox, self.column_in, self.full, self.other = buffers
        self.place, self.mail = Place(), Mail(sems)
        core = self.place.core
        self.mine = pl.ds(pl.multiple_of(core * side, side), side)
        self.theirs = pl.ds(pl.multiple_of((1 - core) * side, side), side)
        self.swaps = []

    def send_core(self, part):
        ref, at = self.parts[part]
        rows = ref.shape[0]
        self.swaps.append(
            self.mail.send(
                ref.at[:, self.theirs], self.core_in.at[at : at + rows], self.place.sibling()
            )
        )

    def send_plane(self):
        row = 0
        for swap, (ref, at) in zip(self.swaps, self.parts):
            swap.wait_recv()
            rows = ref.shape[0]
            total = ref[:, self.mine] + self.core_in[at : at + rows]
            each = rows // 16
            self.sums[:, row : row + each, :] = total.reshape(16, each, side)
            row += each
        self.copies = {}
        for i, step in reversed(list(enumerate(plane_steps))):
            there, device = self.place.plane(step)
            self.copies[i] = self.mail.send(self.sums.at[there], self.inbox.at[i], device)

    def send_column(self):
        total = self.sums[self.place.spot]
        for i in range(len(plane_steps)):
            self.copies[i].wait_recv()
            total = total + self.inbox[i]
        z = self.place.z
        self.column_in[z] = total
        self.copies = [
            self.mail.send(self.column_in.at[z], self.column_in.at[z], self.place.column(step))
            for step in reversed(column_steps)
        ]

    def send_back(self):
        for copy in self.copies:
            copy.wait_recv()
        total = self.column_in[0]
        for z in range(1, 8):
            total = total + self.column_in[z]
        spot = self.place.spot
        self.full[spot] = total
        self.copies = {}
        for i, step in reversed(list(enumerate(plane_steps))):
            device = self.place.plane(step)[1]
            self.copies[i] = self.mail.send(self.full.at[spot], self.full.at[spot], device)
        self.passed = [
            self.mail.send(self.full.at[spot], self.other.at[spot], self.place.sibling())
        ]

    def pass_on(self):
        for i, step in enumerate(plane_steps):
            self.copies[i].wait_recv()
            came = self.place.plane(step, -1)[0]
            self.passed.append(
                self.mail.send(self.full.at[came], self.other.at[came], self.place.sibling())
            )

    def finish(self, outs):
        for copy in self.passed:
            copy.wait_recv()
        row = 0
        for (ref, _), out in zip(self.parts, outs):
            each = ref.shape[0] // 16
            for values, lanes in ((self.full, self.mine), (self.other, self.theirs)):
                out[:, lanes] = values[:, row : row + each, :].reshape(16 * each, side)
            row += each
        self.mail.finish()


def group_buffers(rows):
    each = rows // 16
    return [
        (rows, side), (16, each, side), (15, each, side), (8, each, side), (16, each, side),
        (16, each, side),
    ]


operands = ("img", "embed", "first", "second", "head", "tables", "screens")
early_rows = (256, 128)
late_rows = (256, 256)


def kernel(names, frames_total, *refs):
    sources, (alpha_ref, loss_ref, total_ref), scratch = refs[:7], refs[7:10], refs[10:]
    s = types.SimpleNamespace(**dict(zip(names, scratch)))
    buffers = scratch[len(names) : -4]
    fetch_sems, spectral_sems, early_sems, late_sems = scratch[-4:]
    fetches = {}
    for i, name in enumerate(operands):
        source = sources[i]
        if name == "screens":
            source = source.at[:, pl.ds(half // 2 * side, span * side)]
        fetches[name] = pltpu.make_async_copy(source, getattr(s, name), fetch_sems.at[i])
        fetches[name].start()
    s.wait = lambda name: fetches[name].wait()
    greeted = greet()
    t = split_tables(s.tables)

    s.wait("img")
    cut_tiles(s.img, s.tiles)
    alpha = encode(s)
    s.wait("screens")
    pupil_field(alpha, s.screens, s.spread, s.field)
    s.wait("tables")
    pupil_rows(s, t)
    patches = range(images // frames_here)
    for p in patches:
        frame_spectra(s, t, p)
        spectral_sums(s, t, p)
    pl.semaphore_wait(pltpu.get_barrier_semaphore(), greeted)
    spectral_exchange(
        s, regularizer_relative * frames_total, spectral_sems, lambda: prepare_backward(s)
    )
    losses = [focal_adjoint(s, t, p) for p in patches]
    d_alpha = alpha_adjoint(s, t)
    alpha_ref[:, 0:modes] = d_alpha.T
    s.grad_tail[modes:, :] = jnp.zeros((side - modes, 2 * side), jnp.float32)

    early = GradientGroup(((s.grad_second, 0), (s.grad_tail, 256)), buffers[:6], early_sems)
    late = GradientGroup(((s.grad_first, 0), (s.grad_embed, 256)), buffers[6:], late_sems)
    d_pooled = gradients_after_mean(s, d_alpha)
    lane = lax.broadcasted_iota(jnp.int32, (1, side), 1)
    row = jnp.zeros((1, side), jnp.float32)
    for p in patches:
        at = lax.axis_index("dp") * len(patches) + p
        row = jnp.where(lane == at, losses[p], row)
    s.grad_tail[loss_row : loss_row + 1, 0:side] = row
    early.send_core(0)
    early.send_core(1)
    d_inner = gradient_first(s, d_pooled)
    late.send_core(0)
    early.send_plane()
    gradient_embed(s, d_pooled, d_inner)
    late.send_core(1)
    late.send_plane()
    early.send_column()
    late.send_column()
    early.send_back()
    late.send_back()
    early.pass_on()
    late.pass_on()
    early.finish((total_ref.at[512:768], total_ref.at[768:896]))
    late.finish((total_ref.at[256:512], total_ref.at[0:256]))
    at = 768 + loss_row
    loss_ref[...] = total_ref[at : at + 1, 0:side] * (1.0 / frames_total)


def hand_out(
    alpha_ref, loss_ref, total_ref, embed_ref, first_ref, second_ref, head_ref, out_alpha_ref,
    out_loss_ref, head, alpha, loss, sems,
):
    outs = (embed_ref, first_ref, second_ref)
    copies = [
        pltpu.make_async_copy(total_ref.at[256 * i : 256 * (i + 1)], out, sems.at[i])
        for i, out in enumerate(outs)
    ]
    for copy in copies:
        copy.start()
    head[...] = total_ref[768 : 768 + modes, :]
    regions = alpha.shape[0]
    lane = lax.broadcasted_iota(jnp.int32, (1, side), 1)
    at = lax.axis_index("dp") * regions
    for p in range(regions):
        alpha[p] = alpha_ref[p * frames_here : (p + 1) * frames_here, 0:modes]
        one = jnp.where(lane == at + p, loss_ref[...], 0.0)
        loss[:, p : p + 1] = jnp.sum(one, axis=1, keepdims=True)
    small = ((head, head_ref), (alpha, out_alpha_ref), (loss, out_loss_ref))
    for i, (src, dst) in enumerate(small):
        copies.append(pltpu.make_async_copy(src, dst, sems.at[3 + i]))
        copies[-1].start()
    for copy in copies:
        copy.wait()


def local(recorded_exposures, screens, embed, first, second, head):
    regions = recorded_exposures.shape[0]
    frames_total = recorded_exposures.shape[1] * lax.axis_size("frame")
    f32 = jnp.float32
    names = list(state_shapes) + list(gradient_shapes)
    shapes = list(state_shapes.values()) + list(gradient_shapes.values())
    shapes += group_buffers(sum(early_rows)) + group_buffers(sum(late_rows))
    vmem = pl.BlockSpec(memory_space=pltpu.VMEM)
    d_alpha, losses, total = pl.pallas_call(
        functools.partial(kernel, names, frames_total),
        out_shape=[
            jax.ShapeDtypeStruct((images, side), f32),
            jax.ShapeDtypeStruct((1, side), f32),
            jax.ShapeDtypeStruct((896, 2 * side), f32),
        ],
        in_specs=[pl.BlockSpec(memory_space=pltpu.HBM)] * len(operands),
        out_specs=[vmem] * 3,
        scratch_shapes=[pltpu.VMEM(shape, f32) for shape in shapes]
        + [pltpu.SemaphoreType.DMA((len(operands),))]
        + [pltpu.SemaphoreType.DMA((2, 64))] * 3,
        compiler_params=pltpu.CompilerParams(
            collective_id=0, has_side_effects=True, vmem_limit_bytes=40 << 20
        ),
    )(
        *(
            pltpu.with_memory_space_constraint(operand, pltpu.HBM)
            for operand in (
                recorded_exposures.reshape(images, side, side),
                embed, first, second, head.T, jnp.asarray(transform_tables()), screens,
            )
        )
    )
    out = pl.pallas_call(
        hand_out,
        out_shape=[jax.ShapeDtypeStruct((256, 256), f32)] * 3
        + [
            jax.ShapeDtypeStruct((modes, 256), f32),
            jax.ShapeDtypeStruct((regions, frames_here, modes), f32),
            jax.ShapeDtypeStruct((1, regions), f32),
        ],
        in_specs=[vmem] * 3,
        out_specs=[pl.BlockSpec(memory_space=pltpu.HBM)] * 6,
        scratch_shapes=[
            pltpu.VMEM((modes, 256), f32),
            pltpu.VMEM((regions, frames_here, modes), f32),
            pltpu.VMEM((1, regions), f32),
            pltpu.SemaphoreType.DMA((6,)),
        ],
        compiler_params=pltpu.CompilerParams(vmem_limit_bytes=2 << 20),
    )(d_alpha, losses, total)
    return (out[4], out[0], out[1], out[2], out[3].T, out[5].reshape(regions))


def solution(mesh):
    return jax.shard_map(
        local,
        mesh=mesh,
        in_specs=(P("dp", "frame", None, None), P(), P(), P(), P(), P()),
        out_specs=(P("dp", "frame", None), P(), P(), P(), P(), P("dp")),
        check_vma=False,
    )
```

```python
import functools
import math
import types

import jax
import jax.numpy as jnp
import numpy as np
from jax import lax
from jax.experimental import pallas as pl
from jax.experimental.pallas import tpu as pltpu
from jax.sharding import PartitionSpec as P

entry_block_length = 16
regularizer_relative = 0.001
MESH = pl.DeviceIdType.MESH
HIGH = lax.Precision.HIGH
HIGHEST = lax.Precision.HIGHEST
side = 128
half = side // 2
span = half + 1
pad_span = 72
images = 8
frames_here = 4
modes = 44
tiles_each = 64
loss_row = 44
second_row = 48


def dot(a, b, precision=HIGH):
    return jnp.dot(a, b, precision=precision, preferred_element_type=jnp.float32)


def dot_tn(a, b, precision=HIGH):
    return lax.dot_general(
        a, b, (((0,), (0,)), ((), ())), precision=precision, preferred_element_type=jnp.float32
    )


def dot_nt(a, b, precision=HIGH):
    return lax.dot_general(
        a, b, (((1,), (1,)), ((), ())), precision=precision, preferred_element_type=jnp.float32
    )


def transform_tables():
    index = np.arange(side)
    angle = 2.0 * np.pi / side * (index[:, None] * index[None, :] % side)
    c, s = np.cos(angle), np.sin(angle)
    both = np.block([[c, -s], [s, c]])
    lo = slice(0, half)
    half_plane = np.concatenate([both[:, lo], both[:, side : side + half]], axis=1)
    swapped = np.concatenate([half_plane, half_plane[:, half:], half_plane[:, :half]], axis=1)
    rows = slice(half // 2, half // 2 + span)
    pupil = np.zeros((2 * side, 2 * pad_span))
    pupil[:side, :span], pupil[:side, pad_span : pad_span + span] = c[:, rows], s[:, rows]
    pupil[side:, :span], pupil[side:, pad_span : pad_span + span] = -s[:, rows], c[:, rows]
    real = np.concatenate([c, -s], axis=0)
    narrow = np.concatenate([real, half_plane], axis=1)
    pupil_wide = np.concatenate([pupil, np.zeros((2 * side, 2 * side - 2 * pad_span))], axis=1)
    tables = (swapped / side, narrow, both, pupil_wide, both.T, pupil.T, real.T, half_plane.T)
    return np.concatenate(tables).astype(np.float32)


def split_tables(ref):
    sizes = (256, 256, 256, 256, 256, 2 * pad_span, side, side)
    views, at = [], 0
    for size in sizes:
        views.append(ref.at[at : at + size])
        at += size
    swapped, narrow, both, pupil, both_t, pupil_t, real_t, half_plane_t = views
    return types.SimpleNamespace(
        swapped=swapped, real=narrow.at[:, 0:side], half_plane=narrow.at[:, side:], both=both,
        pupil=pupil.at[:, 0 : 2 * pad_span], both_t=both_t, pupil_t=pupil_t, real_t=real_t,
        half_plane_t=half_plane_t,
    )


def aperture_area():
    at = np.arange(side) - half
    return float(np.sum(at[:, None] ** 2 + at[None, :] ** 2 <= (side // 4) ** 2))


def sigmoid(value):
    return 1.0 / (1.0 + jnp.exp(-value))


def silu_act(value):
    return value / (1.0 + jnp.exp(-value))


def silu_slope(value):
    gate = sigmoid(value)
    return gate * (1.0 + value * (1.0 - gate))


def alternating(rows):
    lane = lax.broadcasted_iota(jnp.int32, (rows, side), 1)
    return jnp.where(lax.rem(lane, 2) == 0, 1.0, -1.0).astype(jnp.float32)


def corner(rows):
    row = lax.broadcasted_iota(jnp.int32, (rows, side), 0)
    lane = lax.broadcasted_iota(jnp.int32, (rows, side), 1)
    return jnp.logical_and(row == 0, lax.rem(lane, half) == 0)


def cut_tiles(img, tiles):
    group = lax.broadcasted_iota(jnp.int32, (8, side), 1) // 16
    for n in range(images):
        for g in range(2):
            x = [img[n, pl.ds(8 * g + j, 8, stride=16), :] for j in range(8)]
            for bit in (1, 2, 4):
                low = lax.rem(group // bit, 2) == 0
                y = list(x)
                for p in range(8):
                    if p & bit == 0:
                        q = p + bit
                        y[p] = jnp.where(low, x[p], pltpu.roll(x[q], 16 * bit, 1))
                        y[q] = jnp.where(low, pltpu.roll(x[p], side - 16 * bit, 1), x[q])
                x = y
            for c in range(8):
                row = n * tiles_each + c * 8
                tiles[row : row + 8, g * side : (g + 1) * side] = x[c]


def tile_sum(value):
    return jnp.sum(value.reshape(images, tiles_each, value.shape[1]), axis=1)


def encode(s):
    s.wait("embed")
    pre = dot(s.tiles[...], s.embed[...], HIGHEST)
    s.hid_pre[...] = pre
    hidden = silu_act(pre)
    s.wait("first")
    pre = dot(hidden, s.first[...], HIGHEST)
    s.inn_pre[...] = pre
    total = tile_sum(silu_act(pre))
    s.inner_sum[...] = total
    s.wait("second")
    mean = (tile_sum(hidden) + dot(total, s.second[...], HIGHEST)) * (1.0 / tiles_each)
    s.pooled[...] = mean
    s.wait("head")
    return dot_nt(mean, s.head[...], HIGHEST)


def chop(value, bits):
    mantissa, exponent = math.frexp(value)
    return math.ldexp(math.floor(mantissa * 2**bits), exponent - bits)


def pieces(value, bits, number):
    out = []
    for _ in range(number - 1):
        out.append(chop(value, bits))
        value -= out[-1]
    return out + [value]


def cos_sin(x):
    turns = jnp.round(x * (1.0 / (512.0 * math.pi)))
    for piece in pieces(512.0 * math.pi, 8, 4):
        x = x - turns * piece
    quarter = jnp.round(x * (2.0 / math.pi))
    for piece in pieces(0.5 * math.pi, 12, 3):
        x = x - quarter * piece
    z = x * x
    sin = x + x * z * (-1.6666654611e-1 + z * (8.3321608736e-3 + z * -1.9515295891e-4))
    cos = 1.0 - 0.5 * z + z * z * (4.166664568298827e-2 + z * (-1.388731625493765e-3 + z * 2.443315711809948e-5))
    quadrant = quarter.astype(jnp.int32)
    odd = (quadrant & 1) != 0
    cos, sin = jnp.where(odd, sin, cos), jnp.where(odd, cos, sin)
    cos = jnp.where(((quadrant + 1) & 2) != 0, -cos, cos)
    sin = jnp.where((quadrant & 2) != 0, -sin, sin)
    return cos, sin


def pupil_field(alpha, screens, spread, field):
    for m in range(modes):
        spread[m] = jnp.broadcast_to(alpha[:, m : m + 1], (images, side))
    lane = lax.broadcasted_iota(jnp.int32, (images, side), 1) - half
    width = 13

    def rows(block, carry):
        at = [pl.multiple_of((block * width + i) * side, side) for i in range(width)]
        total = [jnp.zeros((images, side), jnp.float32) for _ in range(width)]
        for m in range(modes):
            weight = spread[m]
            for i in range(width):
                total[i] = total[i] + weight * screens[m : m + 1, pl.ds(at[i], side)]
        for i in range(width):
            up = block * width + i - half // 2
            inside = lane * lane + up * up <= (side // 4) ** 2
            cos, sin = cos_sin(total[i])
            at = pl.ds(pl.multiple_of((block * width + i) * images, images), images)
            field[at, 0:side] = jnp.where(inside, cos, 0.0)
            field[at, side : 2 * side] = jnp.where(inside, sin, 0.0)
        return carry

    lax.fori_loop(0, span // width, rows, 0)
    field[span * images :, :] = jnp.zeros(((pad_span - span) * images, 2 * side), jnp.float32)


def patch_lanes(p):
    width = frames_here * side
    return pl.ds(pl.multiple_of(p * width, width), width)


def frame_lanes(n):
    return pl.ds(pl.multiple_of(n * side, side), side)


def patch_rows(p):
    return pl.ds(p * 16, 16)


def real_transform(planes, first_table, second_table, s, p, out):
    lanes = patch_lanes(p)
    s.staged[:, lanes] = dot(first_table[...], planes)
    edge = []
    for f in range(frames_here):
        n = p * frames_here + f
        lanes = frame_lanes(n)
        edge.append(jnp.sum(s.staged[0:1, lanes] * alternating(1), axis=1, keepdims=True))
        pair = jnp.concatenate([s.staged[0:side, lanes], s.staged[side : 2 * side, lanes]], axis=1)
        out[n] = dot(pair, second_table[...])
    return edge


def edge_slot(width):
    row = lax.broadcasted_iota(jnp.int32, (8, width), 0)
    lane = lax.broadcasted_iota(jnp.int32, (8, width), 1)
    return jnp.logical_and(row == 0, lane == half)


def frame_spectra(s, t, p):
    here = [p * frames_here + f for f in range(frames_here)]
    planes = jnp.concatenate([s.img[n] for n in here], axis=1)
    edge = real_transform(planes, t.real, t.swapped, s, p, s.spec)
    for f, n in enumerate(here):
        value = edge[f] * (1.0 / side)
        s.spec[n, 0:8, :] = jnp.where(edge_slot(2 * side), value, s.spec[n, 0:8, :])


def prepare_backward(s):
    for n in range(images):
        at = n % frames_here
        s.energy[n // frames_here, at : at + 1, :] = jnp.sum(s.img[n] * s.img[n], axis=0, keepdims=True)
    s.tiles_t[...] = s.tiles[...].T
    s.hidden_t[...] = silu_act(s.hid_pre[...]).T
    s.hid_pre[...] = silu_slope(s.hid_pre[...])
    s.inn_pre[...] = silu_slope(s.inn_pre[...])


def pupil_rows(s, t):
    rowed = dot(s.field[...], t.both[...])
    s.rowed_r[...] = rowed[:, 0:side]
    s.rowed_i[...] = rowed[:, side : 2 * side]
    for n in range(images):
        lanes = slice(n * side, (n + 1) * side)
        rows = pl.ds(n, pad_span, stride=images)
        s.stack[0:pad_span, lanes] = s.rowed_r[rows, :]
        s.stack[pad_span : 2 * pad_span, lanes] = s.rowed_i[rows, :]


def spectral_sums(s, t, p):
    lanes = patch_lanes(p)
    s.focal[:, lanes] = dot(t.pupil[...], s.stack[:, lanes])
    fr, fi = s.focal[0:side, lanes], s.focal[side : 2 * side, lanes]
    spot = (fr * fr + fi * fi) * (1.0 / (side * side * aperture_area()))
    edge = real_transform(spot, t.real, t.half_plane, s, p, s.otf)
    real_slot = lax.broadcasted_iota(jnp.int32, (side, side), 1) < half
    at_corner = corner(side)
    t1 = t2 = t3 = 0.0
    for f in range(frames_here):
        n = p * frames_here + f
        s.otf[n, 0:8, :] = jnp.where(edge_slot(side), edge[f], s.otf[n, 0:8, :])
        o, a, b = s.otf[n], s.spec[n, :, 0:side], s.spec[n, :, side : 2 * side]
        t1, t2, t3 = t1 + a * o, t2 + b * o, t3 + o * o
    turned = pltpu.roll(t2, half, 1)
    num = jnp.where(real_slot, t1 + pltpu.roll(t1, half, 1), turned - t2)
    num = jnp.where(at_corner, t1, num)
    den = jnp.where(at_corner, t3, t3 + pltpu.roll(t3, half, 1))
    s.part[patch_rows(p), 0:8, :] = num.reshape(16, 8, side)
    s.part[patch_rows(p), 8:16, :] = den.reshape(16, 8, side)


def total_of(value):
    return jnp.sum(jnp.sum(value, axis=0, keepdims=True), axis=1, keepdims=True)


def focal_adjoint(s, t, p):
    lane = lax.broadcasted_iota(jnp.int32, (side, side), 1)
    real_slot, at_corner = lane < half, corner(side)
    per_pixel = 1.0 / (side * side)
    weight = jnp.where(lax.rem(lane, half) == 0, per_pixel, 2.0 * per_pixel)
    rho = s.ratio[patch_rows(p)].reshape(side, side)
    num = s.part[patch_rows(p), 0:8, :].reshape(side, side)
    turned = pltpu.roll(rho, half, 1)
    square = rho * rho
    a = jnp.where(jnp.logical_or(real_slot, at_corner), rho, turned) * (-2.0 * weight)
    b = jnp.where(real_slot, turned, -rho)
    b = jnp.where(at_corner, 0.0, b) * (-2.0 * weight)
    m = jnp.where(at_corner, square, square + turned * turned) * (2.0 * weight)
    energy = total_of(s.energy[p])
    loss = energy * per_pixel - total_of(weight * rho * num)
    for f in range(frames_here):
        n = p * frames_here + f
        lanes = frame_lanes(n)
        g = a * s.spec[n, :, 0:side] + b * s.spec[n, :, side : 2 * side] + m * s.otf[n]
        y = dot(g, t.half_plane_t[...])
        s.staged[0:side, lanes] = y[:, 0:side]
        s.staged[side : 2 * side, lanes] = y[:, side : 2 * side]
        s.staged[0:1, lanes] = y[0:1, 0:side] + g[0:1, half : half + 1] * alternating(1)
    lanes = patch_lanes(p)
    d_spot = dot(t.real_t[...], s.staged[:, lanes]) * (2.0 / (side * side * aperture_area()))
    d_focal = jnp.concatenate(
        [s.focal[0:side, lanes] * d_spot, s.focal[side : 2 * side, lanes] * d_spot], axis=0
    )
    s.stack[:, lanes] = dot(t.pupil_t[...], d_focal)
    return loss


def alpha_adjoint(s, t):
    for n in range(images):
        lanes = slice(n * side, (n + 1) * side)
        rows = pl.ds(n, pad_span, stride=images)
        s.rowed_r[rows, :] = s.stack[0:pad_span, lanes]
        s.rowed_i[rows, :] = s.stack[pad_span : 2 * pad_span, lanes]
    rowed = jnp.concatenate([s.rowed_r[...], s.rowed_i[...]], axis=1)
    d_field = dot(rowed, t.both_t[...])
    f_r, f_i = s.field[:, 0:side], s.field[:, side : 2 * side]
    phase = d_field[:, side : 2 * side] * f_r - d_field[:, 0:side] * f_i

    phase = jnp.concatenate([phase[i * images : (i + 1) * images] for i in range(span)], axis=1)
    return dot_nt(s.screens[...], phase)


def spread(value):
    return jnp.broadcast_to(value[:, None, :], (images, tiles_each, 256)).reshape(-1, 256)


def gradients_after_mean(s, d_alpha):
    s.grad_tail[0:modes, :] = dot(d_alpha, s.pooled[...])
    s.grad_tail[second_row : second_row + modes, :] = dot(d_alpha, s.inner_sum[...])
    return dot_tn(d_alpha, s.head[...]) * (1.0 / tiles_each)


def gradient_second(s, tail):
    factor = tail[second_row : second_row + modes, :]
    return dot_tn(factor, s.head[...], HIGHEST) * (1.0 / tiles_each)


def gradient_first(s, d_pooled):
    d_inner = spread(dot_nt(d_pooled, s.second[...])) * s.inn_pre[...]
    s.grad_first[...] = dot(s.hidden_t[...], d_inner)
    return d_inner


def gradient_embed(s, d_pooled, d_inner):
    d_hidden = spread(d_pooled) + dot_nt(d_inner, s.first[...])
    s.grad_embed[...] = dot(s.tiles_t[...], d_hidden * s.hid_pre[...])


state_shapes = dict(
    tiles=(images * tiles_each, 256),
    hid_pre=(images * tiles_each, 256),
    inn_pre=(images * tiles_each, 256),
    tiles_t=(256, images * tiles_each),
    hidden_t=(256, images * tiles_each),
    inner_sum=(images, 256),
    pooled=(images, 256),
    energy=(images // frames_here, frames_here, side),
    spread=(modes, images, side),
    field=(pad_span * images, 2 * side),
    rowed_r=(pad_span * images, side),
    rowed_i=(pad_span * images, side),
    stack=(2 * pad_span, images * side),
    focal=(2 * side, images * side),
    staged=(2 * side, images * side),
    spec=(images, side, 2 * side),
    otf=(images, side, side),
    part=(32, 16, side),
    core_part=(16, 16, side),
    merged=(16, 16, side),
    inbox=(15, 16, side),
    ratio=(32, 8, side),
    screens=(modes, span * side),
    img=(images, side, side),
    embed=(256, 256),
    first=(256, 256),
    second=(256, 256),
    head=(modes, 256),
    tables=(1680, 256),
)
gradient_shapes = dict(
    grad_embed=(256, 256), grad_first=(256, 256), grad_tail=(128, 256), tail=(128, 256)
)


def ring_distance(step, size):
    return min(step, size - step)


plane_steps = sorted(
    ((dx, dy) for dx in range(4) for dy in range(4) if dx or dy),
    key=lambda d: ring_distance(d[0], 4) + ring_distance(d[1], 4),
)
burst_steps = sorted(
    ((dx, dz) for dx in range(4) for dz in range(4) if dx or dz),
    key=lambda d: ring_distance(d[0], 4) + 2 * ring_distance(d[1], 4),
)
column_steps = sorted(range(1, 8), key=lambda d: ring_distance(d, 8))


class Place:
    def __init__(self):
        self.dp, self.frame = lax.axis_index("dp"), lax.axis_index("frame")
        self.core, self.x = lax.rem(self.frame, 2), lax.rem(self.frame // 2, 4)
        self.y, self.z_lo = self.dp // 2, lax.rem(self.dp, 2)
        self.z_hi = self.frame // 8
        self.z = self.z_hi * 2 + self.z_lo
        self.spot = self.x * 4 + self.y
        self.seat = self.z_hi * 4 + self.x

    def device(self, core, x, y, z):
        return {"dp": y * 2 + lax.rem(z, 2), "frame": (z // 2) * 8 + x * 2 + core}

    def sibling(self):
        return self.device(1 - self.core, self.x, self.y, self.z)

    def plane(self, step, sign=1):
        x = lax.rem(self.x + 4 + sign * step[0], 4)
        y = lax.rem(self.y + 4 + sign * step[1], 4)
        return x * 4 + y, self.device(self.core, x, y, self.z)

    def burst(self, step, sign=1):
        x = lax.rem(self.x + 4 + sign * step[0], 4)
        z_hi = lax.rem(self.z_hi + 4 + sign * step[1], 4)
        return z_hi * 4 + x, self.device(self.core, x, self.y, z_hi * 2 + self.z_lo)

    def column(self, step):
        return self.device(self.core, self.x, self.y, lax.rem(self.z + step, 8))


def greet():
    place = Place()
    targets = [place.sibling()]
    targets += [place.burst(step)[1] for step in burst_steps]
    targets += [place.plane(step)[1] for step in plane_steps if step[1]]
    targets += [place.column(step) for step in column_steps if step % 2]
    for target in targets:
        pl.semaphore_signal(
            pltpu.get_barrier_semaphore(), inc=1, device_id=target, device_id_type=MESH
        )
    return len(targets)


class Mail:
    def __init__(self, sems):
        self.sems, self.used, self.sent = sems, 0, []

    def send(self, src, dst, target):
        slot = self.used
        self.used += 1
        copy = pltpu.make_async_remote_copy(
            src_ref=src,
            dst_ref=dst,
            send_sem=self.sems.at[0, slot],
            recv_sem=self.sems.at[1, slot],
            device_id=target,
            device_id_type=MESH,
        )
        copy.start()
        self.sent.append(copy)
        return copy

    def finish(self):
        for copy in self.sent:
            copy.wait_send()


class SpectralExchange:
    def __init__(self, s, sems):
        self.s, self.place, self.mail = s, Place(), Mail(sems)
        self.core, self.seat = self.place.core, self.place.seat

    def send_core(self):
        theirs = pl.ds((1 - self.core) * 16, 16)
        self.swap = self.mail.send(self.s.part.at[theirs], self.s.core_part, self.place.sibling())

    def send_burst(self):
        s = self.s
        self.swap.wait_recv()
        s.merged[...] = s.part[pl.ds(self.core * 16, 16)] + s.core_part[...]
        self.copies = {}
        for i, step in reversed(list(enumerate(burst_steps))):
            there, device = self.place.burst(step)
            self.copies[i] = self.mail.send(s.merged.at[there], s.inbox.at[i], device)

    def send_back(self, regularizer_strength):
        s = self.s
        total = s.merged[self.seat]
        for i in range(len(burst_steps)):
            self.copies[i].wait_recv()
            total = total + s.inbox[i]
        mine = self.core * 16 + self.seat
        s.ratio[mine] = total[0:8] / (total[8:16] + regularizer_strength)
        self.copies = {}
        for i, step in reversed(list(enumerate(burst_steps))):
            device = self.place.burst(step)[1]
            self.copies[i] = self.mail.send(s.ratio.at[mine], s.ratio.at[mine], device)
        self.passed = [self.mail.send(s.ratio.at[mine], s.ratio.at[mine], self.place.sibling())]

    def pass_on(self):
        ratio = self.s.ratio
        for i, step in enumerate(burst_steps):
            self.copies[i].wait_recv()
            came = self.core * 16 + self.place.burst(step, -1)[0]
            self.passed.append(self.mail.send(ratio.at[came], ratio.at[came], self.place.sibling()))

    def finish(self):
        for copy in self.passed:
            copy.wait_recv()
        self.mail.finish()


class GradientGroup:
    def __init__(self, parts, buffers, sems):
        self.parts = parts
        self.core_in, self.sums, self.inbox, self.column_in, self.full, self.other = buffers
        self.place, self.mail = Place(), Mail(sems)
        core = self.place.core
        self.mine = pl.ds(pl.multiple_of(core * side, side), side)
        self.theirs = pl.ds(pl.multiple_of((1 - core) * side, side), side)
        self.swaps = []

    def send_core(self, part):
        ref, at = self.parts[part]
        rows = ref.shape[0]
        self.swaps.append(
            self.mail.send(
                ref.at[:, self.theirs], self.core_in.at[at : at + rows], self.place.sibling()
            )
        )

    def send_plane(self):
        row = 0
        for swap, (ref, at) in zip(self.swaps, self.parts):
            swap.wait_recv()
            rows = ref.shape[0]
            total = ref[:, self.mine] + self.core_in[at : at + rows]
            each = rows // 16
            self.sums[:, row : row + each, :] = total.reshape(16, each, side)
            row += each
        self.copies = {}
        for i, step in reversed(list(enumerate(plane_steps))):
            there, device = self.place.plane(step)
            self.copies[i] = self.mail.send(self.sums.at[there], self.inbox.at[i], device)

    def send_column(self):
        total = self.sums[self.place.spot]
        for i in range(len(plane_steps)):
            self.copies[i].wait_recv()
            total = total + self.inbox[i]
        z = self.place.z
        self.column_in[z] = total
        self.copies = [
            self.mail.send(self.column_in.at[z], self.column_in.at[z], self.place.column(step))
            for step in reversed(column_steps)
        ]

    def send_back(self):
        for copy in self.copies:
            copy.wait_recv()
        total = self.column_in[0]
        for z in range(1, 8):
            total = total + self.column_in[z]
        spot = self.place.spot
        self.full[spot] = total
        self.copies = {}
        for i, step in reversed(list(enumerate(plane_steps))):
            device = self.place.plane(step)[1]
            self.copies[i] = self.mail.send(self.full.at[spot], self.full.at[spot], device)
        self.passed = [
            self.mail.send(self.full.at[spot], self.other.at[spot], self.place.sibling())
        ]

    def pass_on(self):
        for i, step in enumerate(plane_steps):
            self.copies[i].wait_recv()
            came = self.place.plane(step, -1)[0]
            self.passed.append(
                self.mail.send(self.full.at[came], self.other.at[came], self.place.sibling())
            )

    def finish(self, outs):
        for copy in self.passed:
            copy.wait_recv()
        row = 0
        for (ref, _), out in zip(self.parts, outs):
            each = ref.shape[0] // 16
            for values, lanes in ((self.full, self.mine), (self.other, self.theirs)):
                out[:, lanes] = values[:, row : row + each, :].reshape(16 * each, side)
            row += each
        self.mail.finish()


def group_buffers(rows):
    each = rows // 16
    return [
        (rows, side), (16, each, side), (15, each, side), (8, each, side), (16, each, side),
        (16, each, side),
    ]


operands = ("img", "embed", "first", "second", "head", "tables", "screens")
early_rows = (128, 256)
late_rows = (256,)


def kernel(names, frames_total, *refs):
    sources, (alpha_ref, loss_ref, total_ref), scratch = refs[:7], refs[7:10], refs[10:]
    s = types.SimpleNamespace(**dict(zip(names, scratch)))
    buffers = scratch[len(names) : -4]
    fetch_sems, spectral_sems, early_sems, late_sems = scratch[-4:]
    fetches = {}
    for i, name in enumerate(operands):
        source = sources[i]
        if name == "screens":
            source = source.at[:, pl.ds(half // 2 * side, span * side)]
        fetches[name] = pltpu.make_async_copy(source, getattr(s, name), fetch_sems.at[i])
        fetches[name].start()
    s.wait = lambda name: fetches[name].wait()
    greeted = greet()
    t = split_tables(s.tables)

    s.wait("img")
    cut_tiles(s.img, s.tiles)
    alpha = encode(s)
    s.wait("screens")
    pupil_field(alpha, s.screens, s.spread, s.field)
    s.wait("tables")
    pupil_rows(s, t)
    mine = lax.rem(lax.axis_index("frame"), 2)
    burst = SpectralExchange(s, spectral_sems)
    frame_spectra(s, t, 1 - mine)
    spectral_sums(s, t, 1 - mine)
    pl.semaphore_wait(pltpu.get_barrier_semaphore(), greeted)
    burst.send_core()
    frame_spectra(s, t, mine)
    spectral_sums(s, t, mine)
    burst.send_burst()
    prepare_backward(s)
    burst.send_back(regularizer_relative * frames_total)
    burst.pass_on()
    losses = [(mine, focal_adjoint(s, t, mine))]
    burst.finish()
    losses.append((1 - mine, focal_adjoint(s, t, 1 - mine)))
    d_alpha = alpha_adjoint(s, t)
    alpha_ref[:, 0:modes] = d_alpha.T

    early = GradientGroup(((s.grad_tail, 0), (s.grad_first, 128)), buffers[:6], early_sems)
    late = GradientGroup(((s.grad_embed, 0),), buffers[6:], late_sems)
    s.grad_tail[...] = jnp.zeros_like(s.grad_tail)
    d_pooled = gradients_after_mean(s, d_alpha)
    lane = lax.broadcasted_iota(jnp.int32, (1, side), 1)
    row = jnp.zeros((1, side), jnp.float32)
    for p, loss in losses:
        row = jnp.where(lane == lax.axis_index("dp") * len(losses) + p, loss, row)
    s.grad_tail[loss_row : loss_row + 1, 0:side] = row
    early.send_core(0)
    d_inner = gradient_first(s, d_pooled)
    early.send_core(1)
    gradient_embed(s, d_pooled, d_inner)
    late.send_core(0)
    early.send_plane()
    late.send_plane()
    early.send_column()
    late.send_column()
    early.send_back()
    late.send_back()
    early.pass_on()
    early.finish((s.tail, total_ref.at[256:512]))
    total_ref[512:768, :] = gradient_second(s, s.tail)
    total_ref[768 : 768 + modes, :] = s.tail[0:modes, :]
    loss_ref[...] = s.tail[loss_row : loss_row + 1, 0:side] * (1.0 / frames_total)
    late.pass_on()
    late.finish((total_ref.at[0:256],))


def hand_out(
    alpha_ref, loss_ref, total_ref, embed_ref, first_ref, second_ref, head_ref, out_alpha_ref,
    out_loss_ref, head, alpha, loss, sems,
):
    outs = (embed_ref, first_ref, second_ref)
    copies = [
        pltpu.make_async_copy(total_ref.at[256 * i : 256 * (i + 1)], out, sems.at[i])
        for i, out in enumerate(outs)
    ]
    for copy in copies:
        copy.start()
    head[...] = total_ref[768 : 768 + modes, :]
    regions = alpha.shape[0]
    lane = lax.broadcasted_iota(jnp.int32, (1, side), 1)
    at = lax.axis_index("dp") * regions
    for p in range(regions):
        alpha[p] = alpha_ref[p * frames_here : (p + 1) * frames_here, 0:modes]
        one = jnp.where(lane == at + p, loss_ref[...], 0.0)
        loss[:, p : p + 1] = jnp.sum(one, axis=1, keepdims=True)
    small = ((head, head_ref), (alpha, out_alpha_ref), (loss, out_loss_ref))
    for i, (src, dst) in enumerate(small):
        copies.append(pltpu.make_async_copy(src, dst, sems.at[3 + i]))
        copies[-1].start()
    for copy in copies:
        copy.wait()


def local(recorded_exposures, screens, embed, first, second, head):
    regions = recorded_exposures.shape[0]
    frames_total = recorded_exposures.shape[1] * lax.axis_size("frame")
    f32 = jnp.float32
    names = list(state_shapes) + list(gradient_shapes)
    shapes = list(state_shapes.values()) + list(gradient_shapes.values())
    shapes += group_buffers(sum(early_rows)) + group_buffers(sum(late_rows))
    vmem = pl.BlockSpec(memory_space=pltpu.VMEM)
    d_alpha, losses, total = pl.pallas_call(
        functools.partial(kernel, names, frames_total),
        out_shape=[
            jax.ShapeDtypeStruct((images, side), f32),
            jax.ShapeDtypeStruct((1, side), f32),
            jax.ShapeDtypeStruct((816, 2 * side), f32),
        ],
        in_specs=[pl.BlockSpec(memory_space=pltpu.HBM)] * len(operands),
        out_specs=[vmem] * 3,
        scratch_shapes=[pltpu.VMEM(shape, f32) for shape in shapes]
        + [pltpu.SemaphoreType.DMA((len(operands),))]
        + [pltpu.SemaphoreType.DMA((2, 64))] * 3,
        compiler_params=pltpu.CompilerParams(
            collective_id=0, has_side_effects=True, vmem_limit_bytes=40 << 20
        ),
    )(
        *(
            pltpu.with_memory_space_constraint(operand, pltpu.HBM)
            for operand in (
                recorded_exposures.reshape(images, side, side),
                embed, first, second, head.T, jnp.asarray(transform_tables()), screens,
            )
        )
    )
    out = pl.pallas_call(
        hand_out,
        out_shape=[jax.ShapeDtypeStruct((256, 256), f32)] * 3
        + [
            jax.ShapeDtypeStruct((modes, 256), f32),
            jax.ShapeDtypeStruct((regions, frames_here, modes), f32),
            jax.ShapeDtypeStruct((1, regions), f32),
        ],
        in_specs=[vmem] * 3,
        out_specs=[pl.BlockSpec(memory_space=pltpu.HBM)] * 6,
        scratch_shapes=[
            pltpu.VMEM((modes, 256), f32),
            pltpu.VMEM((regions, frames_here, modes), f32),
            pltpu.VMEM((1, regions), f32),
            pltpu.SemaphoreType.DMA((6,)),
        ],
        compiler_params=pltpu.CompilerParams(vmem_limit_bytes=2 << 20),
    )(d_alpha, losses, total)
    return (out[4], out[0], out[1], out[2], out[3].T, out[5].reshape(regions))


def solution(mesh):
    return jax.shard_map(
        local,
        mesh=mesh,
        in_specs=(P("dp", "frame", None, None), P(), P(), P(), P(), P()),
        out_specs=(P("dp", "frame", None), P(), P(), P(), P(), P("dp")),
        check_vma=False,
    )
```

```python
import functools
import math
import types

import jax
import jax.numpy as jnp
import numpy as np
from jax import lax
from jax.experimental import pallas as pl
from jax.experimental.pallas import tpu as pltpu
from jax.sharding import PartitionSpec as P

entry_block_length = 16
regularizer_relative = 0.001
MESH = pl.DeviceIdType.MESH
HIGH = lax.Precision.HIGH
HIGHEST = lax.Precision.HIGHEST
side = 128
half = side // 2
span = half + 1
pad_span = 72
images = 8
frames_here = 4
modes = 44
tiles_each = 64
loss_row = 44
second_row = 48


def dot(a, b, precision=HIGH):
    return jnp.dot(a, b, precision=precision, preferred_element_type=jnp.float32)


def dot_tn(a, b, precision=HIGH):
    return lax.dot_general(
        a, b, (((0,), (0,)), ((), ())), precision=precision, preferred_element_type=jnp.float32
    )


def dot_nt(a, b, precision=HIGH):
    return lax.dot_general(
        a, b, (((1,), (1,)), ((), ())), precision=precision, preferred_element_type=jnp.float32
    )


def transform_tables():
    index = np.arange(side)
    angle = 2.0 * np.pi / side * (index[:, None] * index[None, :] % side)
    c, s = np.cos(angle), np.sin(angle)
    both = np.block([[c, -s], [s, c]])
    lo = slice(0, half)
    half_plane = np.concatenate([both[:, lo], both[:, side : side + half]], axis=1)
    swapped = np.concatenate([half_plane, half_plane[:, half:], half_plane[:, :half]], axis=1)
    rows = slice(half // 2, half // 2 + span)
    pupil = np.zeros((2 * side, 2 * pad_span))
    pupil[:side, :span], pupil[:side, pad_span : pad_span + span] = c[:, rows], s[:, rows]
    pupil[side:, :span], pupil[side:, pad_span : pad_span + span] = -s[:, rows], c[:, rows]
    real = np.concatenate([c, -s], axis=0)
    narrow = np.concatenate([real, half_plane], axis=1)
    pupil_wide = np.concatenate([pupil, np.zeros((2 * side, 2 * side - 2 * pad_span))], axis=1)
    tables = (swapped / side, narrow, both, pupil_wide, both.T, pupil.T, real.T, half_plane.T)
    return np.concatenate(tables).astype(np.float32)


def split_tables(ref):
    sizes = (256, 256, 256, 256, 256, 2 * pad_span, side, side)
    views, at = [], 0
    for size in sizes:
        views.append(ref.at[at : at + size])
        at += size
    swapped, narrow, both, pupil, both_t, pupil_t, real_t, half_plane_t = views
    return types.SimpleNamespace(
        swapped=swapped, real=narrow.at[:, 0:side], half_plane=narrow.at[:, side:], both=both,
        pupil=pupil.at[:, 0 : 2 * pad_span], both_t=both_t, pupil_t=pupil_t, real_t=real_t,
        half_plane_t=half_plane_t,
    )


def aperture_area():
    at = np.arange(side) - half
    return float(np.sum(at[:, None] ** 2 + at[None, :] ** 2 <= (side // 4) ** 2))


def sigmoid(value):
    return 1.0 / (1.0 + jnp.exp(-value))


def silu_act(value):
    return value / (1.0 + jnp.exp(-value))


def silu_slope(value):
    gate = sigmoid(value)
    return gate * (1.0 + value * (1.0 - gate))


def alternating(rows):
    lane = lax.broadcasted_iota(jnp.int32, (rows, side), 1)
    return jnp.where(lax.rem(lane, 2) == 0, 1.0, -1.0).astype(jnp.float32)


def corner(rows):
    row = lax.broadcasted_iota(jnp.int32, (rows, side), 0)
    lane = lax.broadcasted_iota(jnp.int32, (rows, side), 1)
    return jnp.logical_and(row == 0, lax.rem(lane, half) == 0)


def cut_tiles(img, tiles):
    group = lax.broadcasted_iota(jnp.int32, (8, side), 1) // 16
    for n in range(images):
        for g in range(2):
            x = [img[n, pl.ds(8 * g + j, 8, stride=16), :] for j in range(8)]
            for bit in (1, 2, 4):
                low = lax.rem(group // bit, 2) == 0
                y = list(x)
                for p in range(8):
                    if p & bit == 0:
                        q = p + bit
                        y[p] = jnp.where(low, x[p], pltpu.roll(x[q], 16 * bit, 1))
                        y[q] = jnp.where(low, pltpu.roll(x[p], side - 16 * bit, 1), x[q])
                x = y
            for c in range(8):
                row = n * tiles_each + c * 8
                tiles[row : row + 8, g * side : (g + 1) * side] = x[c]


def tile_sum(value):
    return jnp.sum(value.reshape(images, tiles_each, value.shape[1]), axis=1)


def encode(s):
    pre = dot(s.tiles[...], s.embed[...])
    s.hid_pre[...] = pre
    hidden = silu_act(pre)
    pre = dot(hidden, s.first[...])
    s.inn_pre[...] = pre
    total = tile_sum(silu_act(pre))
    s.inner_sum[...] = total
    mean = (tile_sum(hidden) + dot(total, s.second[...], HIGHEST)) * (1.0 / tiles_each)
    s.pooled[...] = mean
    return dot_nt(mean, s.head[...], HIGHEST)


def chop(value, bits):
    mantissa, exponent = math.frexp(value)
    return math.ldexp(math.floor(mantissa * 2**bits), exponent - bits)


def pieces(value, bits, number):
    out = []
    for _ in range(number - 1):
        out.append(chop(value, bits))
        value -= out[-1]
    return out + [value]


def cos_sin(x):
    turns = jnp.round(x * (1.0 / (512.0 * math.pi)))
    for piece in pieces(512.0 * math.pi, 8, 4):
        x = x - turns * piece
    quarter = jnp.round(x * (2.0 / math.pi))
    for piece in pieces(0.5 * math.pi, 12, 3):
        x = x - quarter * piece
    z = x * x
    sin = x + x * z * (-1.6666654611e-1 + z * (8.3321608736e-3 + z * -1.9515295891e-4))
    cos = 1.0 - 0.5 * z + z * z * (4.166664568298827e-2 + z * (-1.388731625493765e-3 + z * 2.443315711809948e-5))
    quadrant = quarter.astype(jnp.int32)
    odd = (quadrant & 1) != 0
    cos, sin = jnp.where(odd, sin, cos), jnp.where(odd, cos, sin)
    cos = jnp.where(((quadrant + 1) & 2) != 0, -cos, cos)
    sin = jnp.where((quadrant & 2) != 0, -sin, sin)
    return cos, sin


def pupil_field(alpha, screens, spread, field):
    for m in range(modes):
        spread[m] = jnp.broadcast_to(alpha[:, m : m + 1], (images, side))
    lane = lax.broadcasted_iota(jnp.int32, (images, side), 1) - half
    width = 13

    def rows(block, carry):
        at = [pl.multiple_of((block * width + i) * side, side) for i in range(width)]
        total = [jnp.zeros((images, side), jnp.float32) for _ in range(width)]
        for m in range(modes):
            weight = spread[m]
            for i in range(width):
                total[i] = total[i] + weight * screens[m : m + 1, pl.ds(at[i], side)]
        for i in range(width):
            up = block * width + i - half // 2
            inside = lane * lane + up * up <= (side // 4) ** 2
            cos, sin = cos_sin(total[i])
            at = pl.ds(pl.multiple_of((block * width + i) * images, images), images)
            field[at, 0:side] = jnp.where(inside, cos, 0.0)
            field[at, side : 2 * side] = jnp.where(inside, sin, 0.0)
        return carry

    lax.fori_loop(0, span // width, rows, 0)
    field[span * images :, :] = jnp.zeros(((pad_span - span) * images, 2 * side), jnp.float32)


def patch_lanes(p):
    width = frames_here * side
    return pl.ds(pl.multiple_of(p * width, width), width)


def frame_lanes(n):
    return pl.ds(pl.multiple_of(n * side, side), side)


def patch_rows(p):
    return pl.ds(p * 16, 16)


def real_transform(planes, first_table, second_table, s, p, out):
    lanes = patch_lanes(p)
    s.staged[:, lanes] = dot(first_table[...], planes)
    edge = []
    for f in range(frames_here):
        n = p * frames_here + f
        lanes = frame_lanes(n)
        edge.append(jnp.sum(s.staged[0:1, lanes] * alternating(1), axis=1, keepdims=True))
        pair = jnp.concatenate([s.staged[0:side, lanes], s.staged[side : 2 * side, lanes]], axis=1)
        out[n] = dot(pair, second_table[...])
    return edge


def edge_slot(width):
    row = lax.broadcasted_iota(jnp.int32, (8, width), 0)
    lane = lax.broadcasted_iota(jnp.int32, (8, width), 1)
    return jnp.logical_and(row == 0, lane == half)


def frame_spectra(s, t, p):
    here = [p * frames_here + f for f in range(frames_here)]
    planes = jnp.concatenate([s.img[n] for n in here], axis=1)
    edge = real_transform(planes, t.real, t.swapped, s, p, s.spec)
    for f, n in enumerate(here):
        value = edge[f] * (1.0 / side)
        s.spec[n, 0:8, :] = jnp.where(edge_slot(2 * side), value, s.spec[n, 0:8, :])


def prepare_backward(s):
    for n in range(images):
        at = n % frames_here
        s.energy[n // frames_here, at : at + 1, :] = jnp.sum(s.img[n] * s.img[n], axis=0, keepdims=True)
    s.grad_tail[...] = jnp.zeros_like(s.grad_tail)
    s.tiles_t[...] = s.tiles[...].T
    s.hidden_t[...] = silu_act(s.hid_pre[...]).T
    s.hid_pre[...] = silu_slope(s.hid_pre[...])
    s.inn_pre[...] = silu_slope(s.inn_pre[...])


def pupil_rows(s, t):
    rowed = dot(s.field[...], t.both[...])
    s.rowed_r[...] = rowed[:, 0:side]
    s.rowed_i[...] = rowed[:, side : 2 * side]
    for n in range(images):
        lanes = slice(n * side, (n + 1) * side)
        rows = pl.ds(n, pad_span, stride=images)
        s.stack[0:pad_span, lanes] = s.rowed_r[rows, :]
        s.stack[pad_span : 2 * pad_span, lanes] = s.rowed_i[rows, :]


def spectral_sums(s, t, p):
    lanes = patch_lanes(p)
    s.focal[:, lanes] = dot(t.pupil[...], s.stack[:, lanes])
    fr, fi = s.focal[0:side, lanes], s.focal[side : 2 * side, lanes]
    spot = (fr * fr + fi * fi) * (1.0 / (side * side * aperture_area()))
    edge = real_transform(spot, t.real, t.half_plane, s, p, s.otf)
    real_slot = lax.broadcasted_iota(jnp.int32, (side, side), 1) < half
    at_corner = corner(side)
    t1 = t2 = t3 = 0.0
    for f in range(frames_here):
        n = p * frames_here + f
        s.otf[n, 0:8, :] = jnp.where(edge_slot(side), edge[f], s.otf[n, 0:8, :])
        o, a, b = s.otf[n], s.spec[n, :, 0:side], s.spec[n, :, side : 2 * side]
        t1, t2, t3 = t1 + a * o, t2 + b * o, t3 + o * o
    turned = pltpu.roll(t2, half, 1)
    num = jnp.where(real_slot, t1 + pltpu.roll(t1, half, 1), turned - t2)
    num = jnp.where(at_corner, t1, num)
    den = jnp.where(at_corner, t3, t3 + pltpu.roll(t3, half, 1))
    s.part[patch_rows(p), 0:8, :] = num.reshape(16, 8, side)
    s.part[patch_rows(p), 8:16, :] = den.reshape(16, 8, side)


def total_of(value):
    return jnp.sum(jnp.sum(value, axis=0, keepdims=True), axis=1, keepdims=True)


def focal_adjoint(s, t, p):
    lane = lax.broadcasted_iota(jnp.int32, (side, side), 1)
    real_slot, at_corner = lane < half, corner(side)
    per_pixel = 1.0 / (side * side)
    weight = jnp.where(lax.rem(lane, half) == 0, per_pixel, 2.0 * per_pixel)
    rho = s.ratio[patch_rows(p)].reshape(side, side)
    num = s.part[patch_rows(p), 0:8, :].reshape(side, side)
    turned = pltpu.roll(rho, half, 1)
    square = rho * rho
    a = jnp.where(jnp.logical_or(real_slot, at_corner), rho, turned) * (-2.0 * weight)
    b = jnp.where(real_slot, turned, -rho)
    b = jnp.where(at_corner, 0.0, b) * (-2.0 * weight)
    m = jnp.where(at_corner, square, square + turned * turned) * (2.0 * weight)
    energy = total_of(s.energy[p])
    loss = energy * per_pixel - total_of(weight * rho * num)
    for f in range(frames_here):
        n = p * frames_here + f
        lanes = frame_lanes(n)
        g = a * s.spec[n, :, 0:side] + b * s.spec[n, :, side : 2 * side] + m * s.otf[n]
        y = dot(g, t.half_plane_t[...])
        s.staged[0:side, lanes] = y[:, 0:side]
        s.staged[side : 2 * side, lanes] = y[:, side : 2 * side]
        s.staged[0:1, lanes] = y[0:1, 0:side] + g[0:1, half : half + 1] * alternating(1)
    lanes = patch_lanes(p)
    d_spot = dot(t.real_t[...], s.staged[:, lanes]) * (2.0 / (side * side * aperture_area()))
    d_focal = jnp.concatenate(
        [s.focal[0:side, lanes] * d_spot, s.focal[side : 2 * side, lanes] * d_spot], axis=0
    )
    s.stack[:, lanes] = dot(t.pupil_t[...], d_focal)
    return loss


def alpha_adjoint(s, t):
    for n in range(images):
        lanes = slice(n * side, (n + 1) * side)
        rows = pl.ds(n, pad_span, stride=images)
        s.rowed_r[rows, :] = s.stack[0:pad_span, lanes]
        s.rowed_i[rows, :] = s.stack[pad_span : 2 * pad_span, lanes]
    rowed = jnp.concatenate([s.rowed_r[...], s.rowed_i[...]], axis=1)
    d_field = dot(rowed, t.both_t[...])
    f_r, f_i = s.field[:, 0:side], s.field[:, side : 2 * side]
    phase = d_field[:, side : 2 * side] * f_r - d_field[:, 0:side] * f_i

    phase = jnp.concatenate([phase[i * images : (i + 1) * images] for i in range(span)], axis=1)
    return dot_nt(s.screens[...], phase)


def spread(value):
    return jnp.broadcast_to(value[:, None, :], (images, tiles_each, 256)).reshape(-1, 256)


def gradients_after_mean(s, d_alpha):
    s.grad_tail[0:modes, :] = dot(d_alpha, s.pooled[...])
    s.grad_tail[second_row : second_row + modes, :] = dot(d_alpha, s.inner_sum[...])
    return dot_tn(d_alpha, s.head[...]) * (1.0 / tiles_each)


def gradient_second(s, tail):
    factor = tail[second_row : second_row + modes, :]
    return dot_tn(factor, s.head[...], HIGHEST) * (1.0 / tiles_each)


def gradient_first(s, d_pooled):
    d_inner = spread(dot_nt(d_pooled, s.second[...])) * s.inn_pre[...]
    s.grad_first[...] = dot(s.hidden_t[...], d_inner)
    return d_inner


def gradient_embed(s, d_pooled, d_inner):
    d_hidden = spread(d_pooled) + dot_nt(d_inner, s.first[...])
    s.grad_embed[...] = dot(s.tiles_t[...], d_hidden * s.hid_pre[...])


state_shapes = dict(
    tiles=(images * tiles_each, 256),
    hid_pre=(images * tiles_each, 256),
    inn_pre=(images * tiles_each, 256),
    tiles_t=(256, images * tiles_each),
    hidden_t=(256, images * tiles_each),
    inner_sum=(images, 256),
    pooled=(images, 256),
    energy=(images // frames_here, frames_here, side),
    spread=(modes, images, side),
    field=(pad_span * images, 2 * side),
    rowed_r=(pad_span * images, side),
    rowed_i=(pad_span * images, side),
    stack=(2 * pad_span, images * side),
    focal=(2 * side, images * side),
    staged=(2 * side, images * side),
    spec=(images, side, 2 * side),
    otf=(images, side, side),
    part=(32, 16, side),
    core_part=(16, 16, side),
    merged=(16, 16, side),
    inbox=(15, 16, side),
    ratio=(32, 8, side),
    screens=(modes, span * side),
    img=(images, side, side),
    embed=(256, 256),
    first=(256, 256),
    second=(256, 256),
    head=(modes, 256),
    tables=(1680, 256),
)
gradient_shapes = dict(
    grad_embed=(256, 256), grad_first=(256, 256), grad_tail=(128, 256), tail=(128, 256)
)


def ring_distance(step, size):
    return min(step, size - step)


plane_steps = sorted(
    ((dx, dy) for dx in range(4) for dy in range(4) if dx or dy),
    key=lambda d: ring_distance(d[0], 4) + ring_distance(d[1], 4),
)
burst_steps = sorted(
    ((dx, dz) for dx in range(4) for dz in range(4) if dx or dz),
    key=lambda d: ring_distance(d[0], 4) + 2 * ring_distance(d[1], 4),
)
column_steps = sorted(range(1, 8), key=lambda d: ring_distance(d, 8))


class Place:
    def __init__(self):
        self.dp, self.frame = lax.axis_index("dp"), lax.axis_index("frame")
        self.core, self.x = lax.rem(self.frame, 2), lax.rem(self.frame // 2, 4)
        self.y, self.z_lo = self.dp // 2, lax.rem(self.dp, 2)
        self.z_hi = self.frame // 8
        self.z = self.z_hi * 2 + self.z_lo
        self.spot = self.x * 4 + self.y
        self.seat = self.z_hi * 4 + self.x

    def device(self, core, x, y, z):
        return {"dp": y * 2 + lax.rem(z, 2), "frame": (z // 2) * 8 + x * 2 + core}

    def sibling(self):
        return self.device(1 - self.core, self.x, self.y, self.z)

    def plane(self, step, sign=1):
        x = lax.rem(self.x + 4 + sign * step[0], 4)
        y = lax.rem(self.y + 4 + sign * step[1], 4)
        return x * 4 + y, self.device(self.core, x, y, self.z)

    def burst(self, step, sign=1):
        x = lax.rem(self.x + 4 + sign * step[0], 4)
        z_hi = lax.rem(self.z_hi + 4 + sign * step[1], 4)
        return z_hi * 4 + x, self.device(self.core, x, self.y, z_hi * 2 + self.z_lo)

    def column(self, step):
        return self.device(self.core, self.x, self.y, lax.rem(self.z + step, 8))


def greet():
    place = Place()
    targets = [place.sibling()]
    targets += [place.burst(step)[1] for step in burst_steps]
    targets += [place.plane(step)[1] for step in plane_steps if step[1]]
    targets += [place.column(step) for step in column_steps if step % 2]
    for target in targets:
        pl.semaphore_signal(
            pltpu.get_barrier_semaphore(), inc=1, device_id=target, device_id_type=MESH
        )
    return len(targets)


class Mail:
    def __init__(self, sems):
        self.sems, self.used, self.sent = sems, 0, []

    def send(self, src, dst, target):
        slot = self.used
        self.used += 1
        copy = pltpu.make_async_remote_copy(
            src_ref=src,
            dst_ref=dst,
            send_sem=self.sems.at[0, slot],
            recv_sem=self.sems.at[1, slot],
            device_id=target,
            device_id_type=MESH,
        )
        copy.start()
        self.sent.append(copy)
        return copy

    def finish(self):
        for copy in self.sent:
            copy.wait_send()


class SpectralExchange:
    def __init__(self, s, sems):
        self.s, self.place, self.mail = s, Place(), Mail(sems)
        self.core, self.seat = self.place.core, self.place.seat

    def send_core(self):
        theirs = pl.ds((1 - self.core) * 16, 16)
        self.swap = self.mail.send(self.s.part.at[theirs], self.s.core_part, self.place.sibling())

    def send_burst(self):
        s = self.s
        self.swap.wait_recv()
        s.merged[...] = s.part[pl.ds(self.core * 16, 16)] + s.core_part[...]
        self.copies = {}
        for i, step in reversed(list(enumerate(burst_steps))):
            there, device = self.place.burst(step)
            self.copies[i] = self.mail.send(s.merged.at[there], s.inbox.at[i], device)

    def send_back(self, regularizer_strength):
        s = self.s
        total = s.merged[self.seat]
        for i in range(len(burst_steps)):
            self.copies[i].wait_recv()
            total = total + s.inbox[i]
        mine = self.core * 16 + self.seat
        s.ratio[mine] = total[0:8] / (total[8:16] + regularizer_strength)
        self.copies = {}
        for i, step in reversed(list(enumerate(burst_steps))):
            device = self.place.burst(step)[1]
            self.copies[i] = self.mail.send(s.ratio.at[mine], s.ratio.at[mine], device)
        self.passed = [self.mail.send(s.ratio.at[mine], s.ratio.at[mine], self.place.sibling())]

    def pass_on(self):
        ratio = self.s.ratio
        for i, step in enumerate(burst_steps):
            self.copies[i].wait_recv()
            came = self.core * 16 + self.place.burst(step, -1)[0]
            self.passed.append(self.mail.send(ratio.at[came], ratio.at[came], self.place.sibling()))

    def finish(self):
        for copy in self.passed:
            copy.wait_recv()
        self.mail.finish()


class GradientGroup:
    def __init__(self, parts, buffers, sems):
        self.parts = parts
        self.core_in, self.sums, self.inbox, self.column_in, self.full, self.other = buffers
        self.place, self.mail = Place(), Mail(sems)
        core = self.place.core
        self.mine = pl.ds(pl.multiple_of(core * side, side), side)
        self.theirs = pl.ds(pl.multiple_of((1 - core) * side, side), side)
        self.swaps = []

    def send_core(self, part):
        ref, at = self.parts[part]
        rows = ref.shape[0]
        self.swaps.append(
            self.mail.send(
                ref.at[:, self.theirs], self.core_in.at[at : at + rows], self.place.sibling()
            )
        )

    def send_plane(self):
        row = 0
        for swap, (ref, at) in zip(self.swaps, self.parts):
            swap.wait_recv()
            rows = ref.shape[0]
            total = ref[:, self.mine] + self.core_in[at : at + rows]
            each = rows // 16
            self.sums[:, row : row + each, :] = total.reshape(16, each, side)
            row += each
        self.copies = {}
        for i, step in reversed(list(enumerate(plane_steps))):
            there, device = self.place.plane(step)
            self.copies[i] = self.mail.send(self.sums.at[there], self.inbox.at[i], device)

    def send_column(self):
        total = self.sums[self.place.spot]
        for i in range(len(plane_steps)):
            self.copies[i].wait_recv()
            total = total + self.inbox[i]
        z = self.place.z
        self.column_in[z] = total
        self.copies = [
            self.mail.send(self.column_in.at[z], self.column_in.at[z], self.place.column(step))
            for step in reversed(column_steps)
        ]

    def send_back(self):
        for copy in self.copies:
            copy.wait_recv()
        total = self.column_in[0]
        for z in range(1, 8):
            total = total + self.column_in[z]
        spot = self.place.spot
        self.full[spot] = total
        self.copies = {}
        for i, step in reversed(list(enumerate(plane_steps))):
            device = self.place.plane(step)[1]
            self.copies[i] = self.mail.send(self.full.at[spot], self.full.at[spot], device)
        self.passed = [
            self.mail.send(self.full.at[spot], self.other.at[spot], self.place.sibling())
        ]

    def pass_on(self):
        for i, step in enumerate(plane_steps):
            self.copies[i].wait_recv()
            came = self.place.plane(step, -1)[0]
            self.passed.append(
                self.mail.send(self.full.at[came], self.other.at[came], self.place.sibling())
            )

    def finish(self, outs):
        for copy in self.passed:
            copy.wait_recv()
        row = 0
        for (ref, _), out in zip(self.parts, outs):
            each = ref.shape[0] // 16
            for values, lanes in ((self.full, self.mine), (self.other, self.theirs)):
                out[:, lanes] = values[:, row : row + each, :].reshape(16 * each, side)
            row += each
        self.mail.finish()


def group_buffers(rows):
    each = rows // 16
    return [
        (rows, side), (16, each, side), (15, each, side), (8, each, side), (16, each, side),
        (16, each, side),
    ]


operands = ("img", "embed", "first", "second", "head", "tables", "screens")
early_rows = (128, 256)
late_rows = (256,)


def kernel(names, frames_total, *refs):
    sources, (alpha_ref, loss_ref, total_ref), scratch = refs[:7], refs[7:10], refs[10:]
    s = types.SimpleNamespace(**dict(zip(names, scratch)))
    buffers = scratch[len(names) : -4]
    fetch_sems, spectral_sems, early_sems, late_sems = scratch[-4:]
    fetches = {}
    for i, name in enumerate(operands):
        source = sources[i]
        if name == "screens":
            source = source.at[:, pl.ds(half // 2 * side, span * side)]
        fetches[name] = pltpu.make_async_copy(source, getattr(s, name), fetch_sems.at[i])
        fetches[name].start()
    s.wait = lambda name: fetches[name].wait()
    greeted = greet()
    t = split_tables(s.tables)

    for name in ("img", "embed", "first", "second", "head"):
        s.wait(name)
    cut_tiles(s.img, s.tiles)
    alpha = encode(s)
    s.wait("screens")
    s.wait("tables")
    pupil_field(alpha, s.screens, s.spread, s.field)
    pupil_rows(s, t)
    mine = lax.rem(lax.axis_index("frame"), 2)
    burst = SpectralExchange(s, spectral_sems)
    frame_spectra(s, t, 1 - mine)
    spectral_sums(s, t, 1 - mine)
    pl.semaphore_wait(pltpu.get_barrier_semaphore(), greeted)
    burst.send_core()
    frame_spectra(s, t, mine)
    spectral_sums(s, t, mine)
    burst.send_burst()
    prepare_backward(s)
    burst.send_back(regularizer_relative * frames_total)
    burst.pass_on()
    losses = [(mine, focal_adjoint(s, t, mine))]
    burst.finish()
    losses.append((1 - mine, focal_adjoint(s, t, 1 - mine)))
    d_alpha = alpha_adjoint(s, t)

    early = GradientGroup(((s.grad_tail, 0), (s.grad_first, 128)), buffers[:6], early_sems)
    late = GradientGroup(((s.grad_embed, 0),), buffers[6:], late_sems)
    d_pooled = gradients_after_mean(s, d_alpha)
    lane = lax.broadcasted_iota(jnp.int32, (1, side), 1)
    row = jnp.zeros((1, side), jnp.float32)
    for p, loss in losses:
        row = jnp.where(lane == lax.axis_index("dp") * len(losses) + p, loss, row)
    s.grad_tail[loss_row : loss_row + 1, 0:side] = row
    early.send_core(0)
    d_inner = gradient_first(s, d_pooled)
    early.send_core(1)
    gradient_embed(s, d_pooled, d_inner)
    late.send_core(0)
    early.send_plane()
    late.send_plane()
    alpha_ref[:, 0:modes] = d_alpha.T
    early.send_column()
    late.send_column()
    early.send_back()
    late.send_back()
    early.pass_on()
    late.pass_on()
    early.finish((s.tail, total_ref.at[256:512]))
    total_ref[512:768, :] = gradient_second(s, s.tail)
    total_ref[768 : 768 + modes, :] = s.tail[0:modes, :]
    loss_ref[...] = s.tail[loss_row : loss_row + 1, 0:side] * (1.0 / frames_total)
    late.finish((total_ref.at[0:256],))


def hand_out(
    alpha_ref, loss_ref, total_ref, embed_ref, first_ref, second_ref, head_ref, out_alpha_ref,
    out_loss_ref, head, alpha, loss, sems,
):
    outs = (embed_ref, first_ref, second_ref)
    copies = [
        pltpu.make_async_copy(total_ref.at[256 * i : 256 * (i + 1)], out, sems.at[i])
        for i, out in enumerate(outs)
    ]
    for copy in copies:
        copy.start()
    head[...] = total_ref[768 : 768 + modes, :]
    regions = alpha.shape[0]
    lane = lax.broadcasted_iota(jnp.int32, (1, side), 1)
    at = lax.axis_index("dp") * regions
    for p in range(regions):
        alpha[p] = alpha_ref[p * frames_here : (p + 1) * frames_here, 0:modes]
        one = jnp.where(lane == at + p, loss_ref[...], 0.0)
        loss[:, p : p + 1] = jnp.sum(one, axis=1, keepdims=True)
    small = ((head, head_ref), (alpha, out_alpha_ref), (loss, out_loss_ref))
    for i, (src, dst) in enumerate(small):
        copies.append(pltpu.make_async_copy(src, dst, sems.at[3 + i]))
        copies[-1].start()
    for copy in copies:
        copy.wait()


def local(recorded_exposures, screens, embed, first, second, head):
    regions = recorded_exposures.shape[0]
    frames_total = recorded_exposures.shape[1] * lax.axis_size("frame")
    f32 = jnp.float32
    names = list(state_shapes) + list(gradient_shapes)
    shapes = list(state_shapes.values()) + list(gradient_shapes.values())
    shapes += group_buffers(sum(early_rows)) + group_buffers(sum(late_rows))
    vmem = pl.BlockSpec(memory_space=pltpu.VMEM)
    d_alpha, losses, total = pl.pallas_call(
        functools.partial(kernel, names, frames_total),
        out_shape=[
            jax.ShapeDtypeStruct((images, side), f32),
            jax.ShapeDtypeStruct((1, side), f32),
            jax.ShapeDtypeStruct((816, 2 * side), f32),
        ],
        in_specs=[pl.BlockSpec(memory_space=pltpu.HBM)] * len(operands),
        out_specs=[vmem] * 3,
        scratch_shapes=[pltpu.VMEM(shape, f32) for shape in shapes]
        + [pltpu.SemaphoreType.DMA((len(operands),))]
        + [pltpu.SemaphoreType.DMA((2, 64))] * 3,
        compiler_params=pltpu.CompilerParams(
            collective_id=0, has_side_effects=True, vmem_limit_bytes=40 << 20
        ),
    )(
        *(
            pltpu.with_memory_space_constraint(operand, pltpu.HBM)
            for operand in (
                recorded_exposures.reshape(images, side, side),
                embed, first, second, head.T, jnp.asarray(transform_tables()), screens,
            )
        )
    )
    out = pl.pallas_call(
        hand_out,
        out_shape=[jax.ShapeDtypeStruct((256, 256), f32)] * 3
        + [
            jax.ShapeDtypeStruct((modes, 256), f32),
            jax.ShapeDtypeStruct((regions, frames_here, modes), f32),
            jax.ShapeDtypeStruct((1, regions), f32),
        ],
        in_specs=[vmem] * 3,
        out_specs=[pl.BlockSpec(memory_space=pltpu.HBM)] * 6,
        scratch_shapes=[
            pltpu.VMEM((modes, 256), f32),
            pltpu.VMEM((regions, frames_here, modes), f32),
            pltpu.VMEM((1, regions), f32),
            pltpu.SemaphoreType.DMA((6,)),
        ],
        compiler_params=pltpu.CompilerParams(vmem_limit_bytes=2 << 20),
    )(d_alpha, losses, total)
    return (out[4], out[0], out[1], out[2], out[3].T, out[5].reshape(regions))


def solution(mesh):
    return jax.shard_map(
        local,
        mesh=mesh,
        in_specs=(P("dp", "frame", None, None), P(), P(), P(), P(), P()),
        out_specs=(P("dp", "frame", None), P(), P(), P(), P(), P("dp")),
        check_vma=False,
    )
```

```python
import functools
import math
import types

import jax
import jax.numpy as jnp
import numpy as np
from jax import lax
from jax.experimental import pallas as pl
from jax.experimental.pallas import tpu as pltpu
from jax.sharding import PartitionSpec as P

entry_block_length = 16
regularizer_relative = 0.001
MESH = pl.DeviceIdType.MESH
HIGH = lax.Precision.HIGH
HIGHEST = lax.Precision.HIGHEST
side = 128
half = side // 2
span = half + 1
pad_span = 72
images = 8
frames_here = 4
modes = 44
tiles_each = 64
loss_row = 44
second_row = 48


def dot(a, b, precision=HIGH):
    return jnp.dot(a, b, precision=precision, preferred_element_type=jnp.float32)


def dot_tn(a, b, precision=HIGH):
    return lax.dot_general(
        a, b, (((0,), (0,)), ((), ())), precision=precision, preferred_element_type=jnp.float32
    )


def dot_nt(a, b, precision=HIGH):
    return lax.dot_general(
        a, b, (((1,), (1,)), ((), ())), precision=precision, preferred_element_type=jnp.float32
    )


def transform_tables():
    index = np.arange(side)
    angle = 2.0 * np.pi / side * (index[:, None] * index[None, :] % side)
    c, s = np.cos(angle), np.sin(angle)
    both = np.block([[c, -s], [s, c]])
    lo = slice(0, half)
    half_plane = np.concatenate([both[:, lo], both[:, side : side + half]], axis=1)
    swapped = np.concatenate([half_plane, half_plane[:, half:], half_plane[:, :half]], axis=1)
    rows = slice(half // 2, half // 2 + span)
    pupil = np.zeros((2 * side, 2 * pad_span))
    pupil[:side, :span], pupil[:side, pad_span : pad_span + span] = c[:, rows], s[:, rows]
    pupil[side:, :span], pupil[side:, pad_span : pad_span + span] = -s[:, rows], c[:, rows]
    real = np.concatenate([c, -s], axis=0)
    narrow = np.concatenate([real, half_plane], axis=1)
    pupil_wide = np.concatenate([pupil, np.zeros((2 * side, 2 * side - 2 * pad_span))], axis=1)
    tables = (swapped / side, narrow, both, pupil_wide, both.T, pupil.T, real.T, half_plane.T)
    return np.concatenate(tables).astype(np.float32)


def split_tables(ref):
    sizes = (256, 256, 256, 256, 256, 2 * pad_span, side, side)
    views, at = [], 0
    for size in sizes:
        views.append(ref.at[at : at + size])
        at += size
    swapped, narrow, both, pupil, both_t, pupil_t, real_t, half_plane_t = views
    return types.SimpleNamespace(
        swapped=swapped, real=narrow.at[:, 0:side], half_plane=narrow.at[:, side:], both=both,
        pupil=pupil.at[:, 0 : 2 * pad_span], both_t=both_t, pupil_t=pupil_t, real_t=real_t,
        half_plane_t=half_plane_t,
    )


def aperture_area():
    at = np.arange(side) - half
    return float(np.sum(at[:, None] ** 2 + at[None, :] ** 2 <= (side // 4) ** 2))


def sigmoid(value):
    return 1.0 / (1.0 + jnp.exp(-value))


def silu_act(value):
    return value / (1.0 + jnp.exp(-value))


def silu_slope(value):
    gate = sigmoid(value)
    return gate * (1.0 + value * (1.0 - gate))


def alternating(rows):
    lane = lax.broadcasted_iota(jnp.int32, (rows, side), 1)
    return jnp.where(lax.rem(lane, 2) == 0, 1.0, -1.0).astype(jnp.float32)


def corner(rows):
    row = lax.broadcasted_iota(jnp.int32, (rows, side), 0)
    lane = lax.broadcasted_iota(jnp.int32, (rows, side), 1)
    return jnp.logical_and(row == 0, lax.rem(lane, half) == 0)


def cut_tiles(img, tiles):
    group = lax.broadcasted_iota(jnp.int32, (8, side), 1) // 16
    for n in range(images):
        for g in range(2):
            x = [img[n, pl.ds(8 * g + j, 8, stride=16), :] for j in range(8)]
            for bit in (1, 2, 4):
                low = lax.rem(group // bit, 2) == 0
                y = list(x)
                for p in range(8):
                    if p & bit == 0:
                        q = p + bit
                        y[p] = jnp.where(low, x[p], pltpu.roll(x[q], 16 * bit, 1))
                        y[q] = jnp.where(low, pltpu.roll(x[p], side - 16 * bit, 1), x[q])
                x = y
            for c in range(8):
                row = n * tiles_each + c * 8
                tiles[row : row + 8, g * side : (g + 1) * side] = x[c]


def tile_sum(value):
    return jnp.sum(value.reshape(images, tiles_each, value.shape[1]), axis=1)


def encode(s):
    pre = dot(s.tiles[...], s.embed[...])
    s.hid_pre[...] = pre
    hidden = silu_act(pre)
    pre = dot(hidden, s.first[...])
    s.inn_pre[...] = pre
    total = tile_sum(silu_act(pre))
    s.inner_sum[...] = total
    hidden_sum = tile_sum(hidden)
    s.hidden_sum[...] = hidden_sum
    alpha = dot_nt(hidden_sum, s.head[...], HIGHEST) + dot_nt(total, s.second_head[...], HIGHEST)
    return alpha * (1.0 / tiles_each)


def chop(value, bits):
    mantissa, exponent = math.frexp(value)
    return math.ldexp(math.floor(mantissa * 2**bits), exponent - bits)


def pieces(value, bits, number):
    out = []
    for _ in range(number - 1):
        out.append(chop(value, bits))
        value -= out[-1]
    return out + [value]


def cos_sin(x):
    turns = jnp.round(x * (1.0 / (512.0 * math.pi)))
    for piece in pieces(512.0 * math.pi, 8, 4):
        x = x - turns * piece
    quarter = jnp.round(x * (2.0 / math.pi))
    for piece in pieces(0.5 * math.pi, 12, 3):
        x = x - quarter * piece
    z = x * x
    sin = x + x * z * (-1.6666654611e-1 + z * (8.3321608736e-3 + z * -1.9515295891e-4))
    cos = 1.0 - 0.5 * z + z * z * (4.166664568298827e-2 + z * (-1.388731625493765e-3 + z * 2.443315711809948e-5))
    quadrant = quarter.astype(jnp.int32)
    odd = (quadrant & 1) != 0
    cos, sin = jnp.where(odd, sin, cos), jnp.where(odd, cos, sin)
    cos = jnp.where(((quadrant + 1) & 2) != 0, -cos, cos)
    sin = jnp.where((quadrant & 2) != 0, -sin, sin)
    return cos, sin


def pupil_field(alpha, screens, spread, field):
    for m in range(modes):
        spread[m] = jnp.broadcast_to(alpha[:, m : m + 1], (images, side))
    lane = lax.broadcasted_iota(jnp.int32, (images, side), 1) - half
    width = 13

    def rows(block, carry):
        at = [(block * width + i) * side for i in range(width)]
        total = [jnp.zeros((images, side), jnp.float32) for _ in range(width)]
        for m in range(modes):
            weight = spread[m]
            for i in range(width):
                total[i] = total[i] + weight * screens[m : m + 1, pl.ds(at[i], side)]
        for i in range(width):
            up = block * width + i - half // 2
            inside = lane * lane + up * up <= (side // 4) ** 2
            cos, sin = cos_sin(total[i])
            at = pl.ds((block * width + i) * images, images)
            field[at, 0:side] = jnp.where(inside, cos, 0.0)
            field[at, side : 2 * side] = jnp.where(inside, sin, 0.0)
        return carry

    for block in range(span // width):
        rows(block, 0)
    field[span * images :, :] = jnp.zeros(((pad_span - span) * images, 2 * side), jnp.float32)


def patch_lanes(p):
    width = frames_here * side
    return pl.ds(pl.multiple_of(p * width, width), width)


def frame_lanes(n):
    return pl.ds(pl.multiple_of(n * side, side), side)


def patch_rows(p):
    return pl.ds(p * 16, 16)


def real_transform(planes, first_table, second_table, s, p, out):
    lanes = patch_lanes(p)
    s.staged[:, lanes] = dot(first_table[...], planes)
    edge = []
    for f in range(frames_here):
        n = p * frames_here + f
        lanes = frame_lanes(n)
        edge.append(jnp.sum(s.staged[0:1, lanes] * alternating(1), axis=1, keepdims=True))
        pair = jnp.concatenate([s.staged[0:side, lanes], s.staged[side : 2 * side, lanes]], axis=1)
        out[n] = dot(pair, second_table[...])
    return edge


def edge_slot(width):
    row = lax.broadcasted_iota(jnp.int32, (8, width), 0)
    lane = lax.broadcasted_iota(jnp.int32, (8, width), 1)
    return jnp.logical_and(row == 0, lane == half)


def frame_spectra(s, t, p):
    here = [p * frames_here + f for f in range(frames_here)]
    planes = jnp.concatenate([s.img[n] for n in here], axis=1)
    edge = real_transform(planes, t.real, t.swapped, s, p, s.spec)
    for f, n in enumerate(here):
        value = edge[f] * (1.0 / side)
        s.spec[n, 0:8, :] = jnp.where(edge_slot(2 * side), value, s.spec[n, 0:8, :])


def prepare_backward(s):
    for n in range(images):
        at = n % frames_here
        s.energy[n // frames_here, at : at + 1, :] = jnp.sum(s.img[n] * s.img[n], axis=0, keepdims=True)
    pooled = s.hidden_sum[...] + dot(s.inner_sum[...], s.second[...])
    s.pooled[...] = pooled * (1.0 / tiles_each)
    s.grad_tail[...] = jnp.zeros_like(s.grad_tail)
    s.tiles_t[...] = s.tiles[...].T
    s.hidden_t[...] = silu_act(s.hid_pre[...]).T
    s.hid_pre[...] = silu_slope(s.hid_pre[...])
    s.inn_pre[...] = silu_slope(s.inn_pre[...])


def pupil_rows(s, t):
    rowed = dot(s.field[...], t.both[...])
    s.rowed_r[...] = rowed[:, 0:side]
    s.rowed_i[...] = rowed[:, side : 2 * side]
    for n in range(images):
        lanes = slice(n * side, (n + 1) * side)
        rows = pl.ds(n, pad_span, stride=images)
        s.stack[0:pad_span, lanes] = s.rowed_r[rows, :]
        s.stack[pad_span : 2 * pad_span, lanes] = s.rowed_i[rows, :]


def spectral_sums(s, t, p):
    lanes = patch_lanes(p)
    s.focal[:, lanes] = dot(t.pupil[...], s.stack[:, lanes])
    fr, fi = s.focal[0:side, lanes], s.focal[side : 2 * side, lanes]
    spot = (fr * fr + fi * fi) * (1.0 / (side * side * aperture_area()))
    edge = real_transform(spot, t.real, t.half_plane, s, p, s.otf)
    real_slot = lax.broadcasted_iota(jnp.int32, (side, side), 1) < half
    at_corner = corner(side)
    t1 = t2 = t3 = 0.0
    for f in range(frames_here):
        n = p * frames_here + f
        s.otf[n, 0:8, :] = jnp.where(edge_slot(side), edge[f], s.otf[n, 0:8, :])
        o, a, b = s.otf[n], s.spec[n, :, 0:side], s.spec[n, :, side : 2 * side]
        t1, t2, t3 = t1 + a * o, t2 + b * o, t3 + o * o
    turned = pltpu.roll(t2, half, 1)
    num = jnp.where(real_slot, t1 + pltpu.roll(t1, half, 1), turned - t2)
    num = jnp.where(at_corner, t1, num)
    den = jnp.where(at_corner, t3, t3 + pltpu.roll(t3, half, 1))
    s.part[patch_rows(p), 0:8, :] = num.reshape(16, 8, side)
    s.part[patch_rows(p), 8:16, :] = den.reshape(16, 8, side)


def total_of(value):
    return jnp.sum(jnp.sum(value, axis=0, keepdims=True), axis=1, keepdims=True)


def focal_adjoint(s, t, p):
    lane = lax.broadcasted_iota(jnp.int32, (side, side), 1)
    real_slot, at_corner = lane < half, corner(side)
    per_pixel = 1.0 / (side * side)
    weight = jnp.where(lax.rem(lane, half) == 0, per_pixel, 2.0 * per_pixel)
    rho = s.ratio[patch_rows(p)].reshape(side, side)
    num = s.part[patch_rows(p), 0:8, :].reshape(side, side)
    turned = pltpu.roll(rho, half, 1)
    square = rho * rho
    a = jnp.where(jnp.logical_or(real_slot, at_corner), rho, turned) * (-2.0 * weight)
    b = jnp.where(real_slot, turned, -rho)
    b = jnp.where(at_corner, 0.0, b) * (-2.0 * weight)
    m = jnp.where(at_corner, square, square + turned * turned) * (2.0 * weight)
    energy = total_of(s.energy[p])
    loss = energy * per_pixel - total_of(weight * rho * num)
    for f in range(frames_here):
        n = p * frames_here + f
        lanes = frame_lanes(n)
        g = a * s.spec[n, :, 0:side] + b * s.spec[n, :, side : 2 * side] + m * s.otf[n]
        y = dot(g, t.half_plane_t[...])
        s.staged[0:side, lanes] = y[:, 0:side]
        s.staged[side : 2 * side, lanes] = y[:, side : 2 * side]
        s.staged[0:1, lanes] = y[0:1, 0:side] + g[0:1, half : half + 1] * alternating(1)
    lanes = patch_lanes(p)
    d_spot = dot(t.real_t[...], s.staged[:, lanes]) * (2.0 / (side * side * aperture_area()))
    d_focal = jnp.concatenate(
        [s.focal[0:side, lanes] * d_spot, s.focal[side : 2 * side, lanes] * d_spot], axis=0
    )
    s.stack[:, lanes] = dot(t.pupil_t[...], d_focal)
    return loss


def alpha_adjoint(s, t):
    for n in range(images):
        lanes = slice(n * side, (n + 1) * side)
        rows = pl.ds(n, pad_span, stride=images)
        s.rowed_r[rows, :] = s.stack[0:pad_span, lanes]
        s.rowed_i[rows, :] = s.stack[pad_span : 2 * pad_span, lanes]
    rowed = jnp.concatenate([s.rowed_r[...], s.rowed_i[...]], axis=1)
    d_field = dot(rowed, t.both_t[...])
    f_r, f_i = s.field[:, 0:side], s.field[:, side : 2 * side]
    phase = d_field[:, side : 2 * side] * f_r - d_field[:, 0:side] * f_i

    phase = jnp.concatenate([phase[i * images : (i + 1) * images] for i in range(span)], axis=1)
    return dot_nt(s.screens[...], phase)


def spread(value):
    return jnp.broadcast_to(value[:, None, :], (images, tiles_each, 256)).reshape(-1, 256)


def gradients_after_mean(s, d_alpha):
    s.grad_tail[0:modes, :] = dot(d_alpha, s.pooled[...])
    s.grad_tail[second_row : second_row + modes, :] = dot(d_alpha, s.inner_sum[...])
    d_pooled = dot_tn(d_alpha, s.head[...]) * (1.0 / tiles_each)
    return d_pooled, dot_tn(d_alpha, s.second_head[...]) * (1.0 / tiles_each)


def gradient_second(s, tail):
    factor = tail[second_row : second_row + modes, :]
    return dot_tn(factor, s.head[...], HIGHEST) * (1.0 / tiles_each)


def gradient_first(s, d_inner):
    d_inner = spread(d_inner) * s.inn_pre[...]
    s.grad_first[...] = dot(s.hidden_t[...], d_inner)
    return d_inner


def gradient_embed(s, d_pooled, d_inner):
    d_hidden = spread(d_pooled) + dot_nt(d_inner, s.first[...])
    s.grad_embed[...] = dot(s.tiles_t[...], d_hidden * s.hid_pre[...])


state_shapes = dict(
    tiles=(images * tiles_each, 256),
    hid_pre=(images * tiles_each, 256),
    inn_pre=(images * tiles_each, 256),
    tiles_t=(256, images * tiles_each),
    hidden_t=(256, images * tiles_each),
    inner_sum=(images, 256),
    pooled=(images, 256),
    hidden_sum=(images, 256),
    second_head=(modes, 256),
    energy=(images // frames_here, frames_here, side),
    spread=(modes, images, side),
    field=(pad_span * images, 2 * side),
    rowed_r=(pad_span * images, side),
    rowed_i=(pad_span * images, side),
    stack=(2 * pad_span, images * side),
    focal=(2 * side, images * side),
    staged=(2 * side, images * side),
    spec=(images, side, 2 * side),
    otf=(images, side, side),
    part=(32, 16, side),
    core_part=(16, 16, side),
    merged=(16, 16, side),
    inbox=(15, 16, side),
    ratio=(32, 8, side),
    screens=(modes, span * side),
    img=(images, side, side),
    embed=(256, 256),
    first=(256, 256),
    second=(256, 256),
    head=(modes, 256),
    tables=(1680, 256),
)
gradient_shapes = dict(
    grad_embed=(256, 256), grad_first=(256, 256), grad_tail=(128, 256), tail=(128, 256)
)


def ring_distance(step, size):
    return min(step, size - step)


plane_steps = sorted(
    ((dx, dy) for dx in range(4) for dy in range(4) if dx or dy),
    key=lambda d: ring_distance(d[0], 4) + ring_distance(d[1], 4),
)
burst_steps = sorted(
    ((dx, dz) for dx in range(4) for dz in range(4) if dx or dz),
    key=lambda d: ring_distance(d[0], 4) + 2 * ring_distance(d[1], 4),
)
column_steps = sorted(range(1, 8), key=lambda d: ring_distance(d, 8))


class Place:
    def __init__(self):
        self.dp, self.frame = lax.axis_index("dp"), lax.axis_index("frame")
        self.core, self.x = lax.rem(self.frame, 2), lax.rem(self.frame // 2, 4)
        self.y, self.z_lo = self.dp // 2, lax.rem(self.dp, 2)
        self.z_hi = self.frame // 8
        self.z = self.z_hi * 2 + self.z_lo
        self.spot = self.x * 4 + self.y
        self.seat = self.z_hi * 4 + self.x

    def device(self, core, x, y, z):
        return {"dp": y * 2 + lax.rem(z, 2), "frame": (z // 2) * 8 + x * 2 + core}

    def sibling(self):
        return self.device(1 - self.core, self.x, self.y, self.z)

    def plane(self, step, sign=1):
        x = lax.rem(self.x + 4 + sign * step[0], 4)
        y = lax.rem(self.y + 4 + sign * step[1], 4)
        return x * 4 + y, self.device(self.core, x, y, self.z)

    def burst(self, step, sign=1):
        x = lax.rem(self.x + 4 + sign * step[0], 4)
        z_hi = lax.rem(self.z_hi + 4 + sign * step[1], 4)
        return z_hi * 4 + x, self.device(self.core, x, self.y, z_hi * 2 + self.z_lo)

    def column(self, step):
        return self.device(self.core, self.x, self.y, lax.rem(self.z + step, 8))


def greet():
    place = Place()
    targets = [place.sibling()]
    targets += [place.burst(step)[1] for step in burst_steps]
    targets += [place.plane(step)[1] for step in plane_steps if step[1]]
    targets += [place.column(step) for step in column_steps if step % 2]
    for target in targets:
        pl.semaphore_signal(
            pltpu.get_barrier_semaphore(), inc=1, device_id=target, device_id_type=MESH
        )
    return len(targets)


class Mail:
    def __init__(self, sems):
        self.sems, self.used, self.sent = sems, 0, []

    def send(self, src, dst, target):
        slot = self.used
        self.used += 1
        copy = pltpu.make_async_remote_copy(
            src_ref=src,
            dst_ref=dst,
            send_sem=self.sems.at[0, slot],
            recv_sem=self.sems.at[1, slot],
            device_id=target,
            device_id_type=MESH,
        )
        copy.start()
        self.sent.append(copy)
        return copy

    def finish(self):
        for copy in self.sent:
            copy.wait_send()


class SpectralExchange:
    def __init__(self, s, sems):
        self.s, self.place, self.mail = s, Place(), Mail(sems)
        self.core, self.seat = self.place.core, self.place.seat

    def send_core(self):
        theirs = pl.ds((1 - self.core) * 16, 16)
        self.swap = self.mail.send(self.s.part.at[theirs], self.s.core_part, self.place.sibling())

    def send_burst(self):
        s = self.s
        self.swap.wait_recv()
        s.merged[...] = s.part[pl.ds(self.core * 16, 16)] + s.core_part[...]
        self.copies = {}
        for i, step in reversed(list(enumerate(burst_steps))):
            there, device = self.place.burst(step)
            self.copies[i] = self.mail.send(s.merged.at[there], s.inbox.at[i], device)

    def send_back(self, regularizer_strength):
        s = self.s
        total = s.merged[self.seat]
        for i in range(len(burst_steps)):
            self.copies[i].wait_recv()
            total = total + s.inbox[i]
        mine = self.core * 16 + self.seat
        s.ratio[mine] = total[0:8] / (total[8:16] + regularizer_strength)
        self.copies = {}
        for i, step in reversed(list(enumerate(burst_steps))):
            device = self.place.burst(step)[1]
            self.copies[i] = self.mail.send(s.ratio.at[mine], s.ratio.at[mine], device)
        self.passed = [self.mail.send(s.ratio.at[mine], s.ratio.at[mine], self.place.sibling())]

    def pass_on(self):
        ratio = self.s.ratio
        for i, step in enumerate(burst_steps):
            self.copies[i].wait_recv()
            came = self.core * 16 + self.place.burst(step, -1)[0]
            self.passed.append(self.mail.send(ratio.at[came], ratio.at[came], self.place.sibling()))

    def finish(self):
        for copy in self.passed:
            copy.wait_recv()
        self.mail.finish()


class GradientGroup:
    def __init__(self, parts, buffers, sems):
        self.parts = parts
        self.core_in, self.sums, self.inbox, self.column_in, self.full, self.other = buffers
        self.place, self.mail = Place(), Mail(sems)
        core = self.place.core
        self.mine = pl.ds(pl.multiple_of(core * side, side), side)
        self.theirs = pl.ds(pl.multiple_of((1 - core) * side, side), side)
        self.swaps = []

    def send_core(self, part):
        ref, at = self.parts[part]
        rows = ref.shape[0]
        self.swaps.append(
            self.mail.send(
                ref.at[:, self.theirs], self.core_in.at[at : at + rows], self.place.sibling()
            )
        )

    def send_plane(self):
        row = 0
        for swap, (ref, at) in zip(self.swaps, self.parts):
            swap.wait_recv()
            rows = ref.shape[0]
            total = ref[:, self.mine] + self.core_in[at : at + rows]
            each = rows // 16
            self.sums[:, row : row + each, :] = total.reshape(16, each, side)
            row += each
        self.copies = {}
        for i, step in reversed(list(enumerate(plane_steps))):
            there, device = self.place.plane(step)
            self.copies[i] = self.mail.send(self.sums.at[there], self.inbox.at[i], device)

    def send_column(self):
        total = self.sums[self.place.spot]
        for i in range(len(plane_steps)):
            self.copies[i].wait_recv()
            total = total + self.inbox[i]
        z = self.place.z
        self.column_in[z] = total
        self.copies = [
            self.mail.send(self.column_in.at[z], self.column_in.at[z], self.place.column(step))
            for step in reversed(column_steps)
        ]

    def send_back(self):
        for copy in self.copies:
            copy.wait_recv()
        total = self.column_in[0]
        for z in range(1, 8):
            total = total + self.column_in[z]
        spot = self.place.spot
        self.full[spot] = total
        self.copies = {}
        for i, step in reversed(list(enumerate(plane_steps))):
            device = self.place.plane(step)[1]
            self.copies[i] = self.mail.send(self.full.at[spot], self.full.at[spot], device)
        self.passed = [
            self.mail.send(self.full.at[spot], self.other.at[spot], self.place.sibling())
        ]

    def pass_on(self):
        for i, step in enumerate(plane_steps):
            self.copies[i].wait_recv()
            came = self.place.plane(step, -1)[0]
            self.passed.append(
                self.mail.send(self.full.at[came], self.other.at[came], self.place.sibling())
            )

    def finish(self, outs):
        for copy in self.passed:
            copy.wait_recv()
        row = 0
        for (ref, _), out in zip(self.parts, outs):
            each = ref.shape[0] // 16
            for values, lanes in ((self.full, self.mine), (self.other, self.theirs)):
                out[:, lanes] = values[:, row : row + each, :].reshape(16 * each, side)
            row += each
        self.mail.finish()


def group_buffers(rows):
    each = rows // 16
    return [
        (rows, side), (16, each, side), (15, each, side), (8, each, side), (16, each, side),
        (16, each, side),
    ]


operands = ("img", "embed", "first", "second", "head", "tables", "screens")
early_rows = (128, 256)
late_rows = (256,)


def kernel(names, frames_total, *refs):
    sources, (alpha_ref, loss_ref, total_ref), scratch = refs[:7], refs[7:10], refs[10:]
    s = types.SimpleNamespace(**dict(zip(names, scratch)))
    buffers = scratch[len(names) : -4]
    fetch_sems, spectral_sems, early_sems, late_sems = scratch[-4:]
    fetches = {}
    for i, name in enumerate(operands):
        source = sources[i]
        if name == "screens":
            source = source.at[:, pl.ds(half // 2 * side, span * side)]
        fetches[name] = pltpu.make_async_copy(source, getattr(s, name), fetch_sems.at[i])
        fetches[name].start()
    s.wait = lambda name: fetches[name].wait()
    greeted = greet()
    t = split_tables(s.tables)

    for name in ("img", "embed", "first", "second", "head"):
        s.wait(name)
    s.second_head[...] = dot_nt(s.head[...], s.second[...], HIGHEST)
    cut_tiles(s.img, s.tiles)
    alpha = encode(s)
    s.wait("screens")
    s.wait("tables")
    pupil_field(alpha, s.screens, s.spread, s.field)
    pupil_rows(s, t)
    mine = lax.rem(lax.axis_index("frame"), 2)
    burst = SpectralExchange(s, spectral_sems)
    frame_spectra(s, t, 1 - mine)
    spectral_sums(s, t, 1 - mine)
    pl.semaphore_wait(pltpu.get_barrier_semaphore(), greeted)
    burst.send_core()
    frame_spectra(s, t, mine)
    spectral_sums(s, t, mine)
    burst.send_burst()
    prepare_backward(s)
    burst.send_back(regularizer_relative * frames_total)
    burst.pass_on()
    losses = [(mine, focal_adjoint(s, t, mine))]
    burst.finish()
    losses.append((1 - mine, focal_adjoint(s, t, 1 - mine)))
    d_alpha = alpha_adjoint(s, t)

    early = GradientGroup(((s.grad_tail, 0), (s.grad_first, 128)), buffers[:6], early_sems)
    late = GradientGroup(((s.grad_embed, 0),), buffers[6:], late_sems)
    d_pooled, d_inner = gradients_after_mean(s, d_alpha)
    lane = lax.broadcasted_iota(jnp.int32, (1, side), 1)
    row = jnp.zeros((1, side), jnp.float32)
    for p, loss in losses:
        row = jnp.where(lane == lax.axis_index("dp") * len(losses) + p, loss, row)
    s.grad_tail[loss_row : loss_row + 1, 0:side] = row
    early.send_core(0)
    d_inner = gradient_first(s, d_inner)
    early.send_core(1)
    gradient_embed(s, d_pooled, d_inner)
    late.send_core(0)
    early.send_plane()
    late.send_plane()
    alpha_ref[:, 0:modes] = d_alpha.T
    early.send_column()
    late.send_column()
    early.send_back()
    late.send_back()
    early.pass_on()
    late.pass_on()
    early.finish((s.tail, total_ref.at[256:512]))
    total_ref[512:768, :] = gradient_second(s, s.tail)
    total_ref[768 : 768 + modes, :] = s.tail[0:modes, :]
    loss_ref[...] = s.tail[loss_row : loss_row + 1, 0:side] * (1.0 / frames_total)
    late.finish((total_ref.at[0:256],))


def hand_out(
    alpha_ref, loss_ref, total_ref, embed_ref, first_ref, second_ref, head_ref, out_alpha_ref,
    out_loss_ref, head, alpha, loss, sems,
):
    outs = (embed_ref, first_ref, second_ref)
    copies = [
        pltpu.make_async_copy(total_ref.at[256 * i : 256 * (i + 1)], out, sems.at[i])
        for i, out in enumerate(outs)
    ]
    for copy in copies:
        copy.start()
    head[...] = total_ref[768 : 768 + modes, :]
    regions = alpha.shape[0]
    lane = lax.broadcasted_iota(jnp.int32, (1, side), 1)
    at = lax.axis_index("dp") * regions
    for p in range(regions):
        alpha[p] = alpha_ref[p * frames_here : (p + 1) * frames_here, 0:modes]
        one = jnp.where(lane == at + p, loss_ref[...], 0.0)
        loss[:, p : p + 1] = jnp.sum(one, axis=1, keepdims=True)
    small = ((head, head_ref), (alpha, out_alpha_ref), (loss, out_loss_ref))
    for i, (src, dst) in enumerate(small):
        copies.append(pltpu.make_async_copy(src, dst, sems.at[3 + i]))
        copies[-1].start()
    for copy in copies:
        copy.wait()


def local(recorded_exposures, screens, embed, first, second, head):
    regions = recorded_exposures.shape[0]
    frames_total = recorded_exposures.shape[1] * lax.axis_size("frame")
    f32 = jnp.float32
    names = list(state_shapes) + list(gradient_shapes)
    shapes = list(state_shapes.values()) + list(gradient_shapes.values())
    shapes += group_buffers(sum(early_rows)) + group_buffers(sum(late_rows))
    vmem = pl.BlockSpec(memory_space=pltpu.VMEM)
    d_alpha, losses, total = pl.pallas_call(
        functools.partial(kernel, names, frames_total),
        out_shape=[
            jax.ShapeDtypeStruct((images, side), f32),
            jax.ShapeDtypeStruct((1, side), f32),
            jax.ShapeDtypeStruct((816, 2 * side), f32),
        ],
        in_specs=[pl.BlockSpec(memory_space=pltpu.HBM)] * len(operands),
        out_specs=[vmem] * 3,
        scratch_shapes=[pltpu.VMEM(shape, f32) for shape in shapes]
        + [pltpu.SemaphoreType.DMA((len(operands),))]
        + [pltpu.SemaphoreType.DMA((2, 64))] * 3,
        compiler_params=pltpu.CompilerParams(
            collective_id=0, has_side_effects=True, vmem_limit_bytes=40 << 20
        ),
    )(
        *(
            pltpu.with_memory_space_constraint(operand, pltpu.HBM)
            for operand in (
                recorded_exposures.reshape(images, side, side),
                embed, first, second, head.T, jnp.asarray(transform_tables()), screens,
            )
        )
    )
    out = pl.pallas_call(
        hand_out,
        out_shape=[jax.ShapeDtypeStruct((256, 256), f32)] * 3
        + [
            jax.ShapeDtypeStruct((modes, 256), f32),
            jax.ShapeDtypeStruct((regions, frames_here, modes), f32),
            jax.ShapeDtypeStruct((1, regions), f32),
        ],
        in_specs=[vmem] * 3,
        out_specs=[pl.BlockSpec(memory_space=pltpu.HBM)] * 6,
        scratch_shapes=[
            pltpu.VMEM((modes, 256), f32),
            pltpu.VMEM((regions, frames_here, modes), f32),
            pltpu.VMEM((1, regions), f32),
            pltpu.SemaphoreType.DMA((6,)),
        ],
        compiler_params=pltpu.CompilerParams(vmem_limit_bytes=2 << 20),
    )(d_alpha, losses, total)
    return (out[4], out[0], out[1], out[2], out[3].T, out[5].reshape(regions))


def solution(mesh):
    return jax.shard_map(
        local,
        mesh=mesh,
        in_specs=(P("dp", "frame", None, None), P(), P(), P(), P(), P()),
        out_specs=(P("dp", "frame", None), P(), P(), P(), P(), P("dp")),
        check_vma=False,
    )
```
